32 devices in a mesh: seq: 16 (over z, y, x), head: 2 (over core).
Axes of the slice: x: 2, y: 2, z: 4, core: 2. Of those that a mesh axis runs over, the one named last changes fastest.
Arguments:
- activations: bfloat16 [16384, 1024], P('seq'), may hold values from -6 to 6
- log_decay: float32 [16384, 8], P('seq', 'head'), may hold values from -2 to 0, as said below
- doc_starts: int32 [3], replicated, may hold values from 0 to 16383, as said below
- query_weight: bfloat16 [1024, 1024], P('seq', 'head'), may hold values from -0.1875 to 0.1875
- key_weight: bfloat16 [1024, 2048], P('seq', 'head'), may hold values from -0.1875 to 0.1875
- value_weight: bfloat16 [1024, 2048], P('seq', 'head'), may hold values from -0.1875 to 0.1875
- beta_weight: bfloat16 [1024, 16], P('seq', 'head'), may hold values from -0.1875 to 0.1875
- gate_weight: bfloat16 [1024, 1024], P('seq', 'head'), may hold values from -0.1875 to 0.1875
- out_weight: bfloat16 [1024, 1024], P('head', 'seq'), may hold values from -0.375 to 0.375
- query_taps: bfloat16 [4, 1024], P(None, 'head'), may hold values from -3 to 3
- key_taps: bfloat16 [4, 2048], P(None, 'head'), may hold values from -3 to 3
- value_taps: bfloat16 [4, 2048], P(None, 'head'), may hold values from -3 to 3
- mixer_gain: bfloat16 [1024], P('seq'), may hold values from 0.5 to 1.5
- head_gain: bfloat16 [128], replicated, may hold values from 0.5 to 1.5
- feed_gain: bfloat16 [1024], P('seq'), may hold values from 0.5 to 1.5
- feed_gate: bfloat16 [1024, 2816], P('seq', 'head'), may hold values from -0.1875 to 0.1875
- feed_up: bfloat16 [1024, 2816], P('seq', 'head'), may hold values from -0.1875 to 0.1875
- feed_down: bfloat16 [2816, 1024], P('head', 'seq'), may hold values from -0.21875 to 0.21875
- cotangent: bfloat16 [16384, 1024], P('seq'), may hold values from -6 to 6
Outputs:
- output: bfloat16 [16384, 1024], P('seq', 'head')
- grad_input: float32 [16384, 1024], P('seq', 'head')
- grad_query: float32 [1024, 1024], P('seq', 'head')
- grad_key: float32 [1024, 2048], P('seq', 'head')
- grad_value: float32 [1024, 2048], P('seq', 'head')
- grad_beta: float32 [1024, 16], P('seq', 'head')
- grad_gate: float32 [1024, 1024], P('seq', 'head')
- grad_out: float32 [1024, 1024], P('head', 'seq')
- grad_query_taps: float32 [4, 1024], P(None, 'head')
- grad_key_taps: float32 [4, 2048], P(None, 'head')
- grad_value_taps: float32 [4, 2048], P(None, 'head')
- grad_mixer_gain: float32 [1024], P('seq')
- grad_head_gain: float32 [128], replicated
- grad_feed_gain: float32 [1024], P('seq')
- grad_feed_gate: float32 [1024, 2816], P('seq', 'head')
- grad_feed_up: float32 [1024, 2816], P('seq', 'head')
- grad_feed_down: float32 [2816, 1024], P('head', 'seq')
The draws below stay inside these ranges and needn't reach their ends.
Inputs may be any that keep to these rules, and one draw needn't show every extreme that they name: `log_decay`: every entry is at most zero. doc_starts[0] is 0; doc_starts[1] lies in 1 to 1023 and doc_starts[2] in 15361 to 16383, so that the second sequence covers tokens of every index of seq.
All inputs are finite; a program needn't handle non-finite values.
Results may differ from the reference program's by a relative error of at most 0.014.
The reference program's roundings to bfloat16 on the way count: a program that leaves them out, or rounds other values in their place, can miss the bound.
Values may be sent and summed in bfloat16 or wider, within the bound.
No kernel may reach another device: no remote copies, remote signals or barrier semaphores. Data moves between devices by JAX's collectives and lax.ppermute only.
A program may use at most 384 MiB of HBM per device.

```python
import jax
import jax.numpy as jnp
from jax import lax

D = 1024
HEAD_TOTAL = 8
HD = 128
NH = 2
CONV = 4
FF = 2816
BLOCK = 64
TOK_DEV = 1024
QD = 1024
TOKEN_TOTAL = 16384


def draw_log_decay(key, part):
    key = jax.random.fold_in(key, 11)
    key_vectors = jax.random.split(key, 7)
    share = 0.5
    quick = jax.random.uniform(key_vectors[0], (HEAD_TOTAL,)) < share
    quick_rate = jnp.exp(jax.random.uniform(key_vectors[1], (HEAD_TOTAL,), minval=jnp.log(1.0 / 50.0), maxval=jnp.log(1.0 / 30.0)))
    slow_rate = jnp.exp(jax.random.uniform(key_vectors[2], (HEAD_TOTAL,), minval=jnp.log(0.1), maxval=jnp.log(0.6))) / TOKEN_TOTAL
    decay_rates = jnp.where(quick, quick_rate, slow_rate)
    token_multiplier = jnp.exp(jax.random.uniform(key_vectors[3], (TOKEN_TOTAL, HEAD_TOTAL), minval=-0.69, maxval=0.69))
    device_multiplier = jnp.exp(jax.random.uniform(key_vectors[4], (TOKEN_TOTAL // TOK_DEV, HEAD_TOTAL), minval=-0.69, maxval=0.69))
    device_multiplier = jnp.repeat(device_multiplier, TOK_DEV, axis=0)
    segment_place = jax.random.randint(key_vectors[5], (2,), 0, TOKEN_TOTAL)
    segment_length = jax.random.uniform(key_vectors[6], (2, HEAD_TOTAL), minval=0.22, maxval=0.69)
    token_position = jnp.arange(TOKEN_TOTAL)
    segment_runs = (token_position[:, None] == segment_place[0]).astype(jnp.float32) * segment_length[0][None, :]
    segment_runs = segment_runs + (token_position[:, None] == segment_place[1]).astype(jnp.float32) * segment_length[1][None, :]
    return (-(decay_rates[None, :] * token_multiplier * device_multiplier) - segment_runs).astype(jnp.float32)


def draw_doc_starts(key, part):
    key = jax.random.fold_in(key, 5)
    early_key, late_key = jax.random.split(key)
    second = jax.random.randint(early_key, (1,), 1, TOK_DEV)
    third = jax.random.randint(late_key, (1,), TOKEN_TOTAL - TOK_DEV + 1, TOKEN_TOTAL)
    return jnp.concatenate([jnp.zeros((1,), jnp.int32), second.astype(jnp.int32), third.astype(jnp.int32)])


def steps_of(rng, dims, cuts, least, high):
    level, own = 1.0, jax.random.fold_in(rng, 6)
    for axis_at, shards_of in cuts:
        draws = jnp.exp(jax.random.uniform(jax.random.fold_in(own, axis_at), (shards_of,), jnp.float32, least / len(cuts), high / len(cuts)))
        level = level * jnp.repeat(draws, dims[axis_at] // shards_of).reshape([-1 if axis == axis_at else 1 for axis in range(len(dims))])
    return level


def normal_values(rng, dims, scale, reach, cuts=(), held_as=jnp.bfloat16):
    values = jax.random.normal(rng, dims, jnp.float32) * scale
    if len(cuts) > 0:
        values = steps_of(rng, dims, cuts, -0.22, 0.18) * values
    return jnp.clip(values, min=-reach, max=reach).astype(held_as)


def setup_inputs(seed: int = 0) -> dict:
    splits = jax.random.split(jax.random.key(seed), 20)
    activations = normal_values(splits[0], (TOKEN_TOTAL, D), 1.0, 6.0, ((0, 16),))
    log_decay = draw_log_decay(jax.random.fold_in(splits[19], 71), 0)
    doc_starts = draw_doc_starts(jax.random.fold_in(splits[19], 71), 0)
    query_weight = normal_values(splits[3], (D, QD), D ** -0.5, 0.1875, ((0, 16), (1, 2)))
    key_weight = normal_values(splits[4], (D, NH * QD), D ** -0.5, 0.1875, ((0, 16), (1, 2)))
    value_weight = normal_values(splits[5], (D, NH * QD), D ** -0.5, 0.1875, ((0, 16), (1, 2)))
    beta_weight = normal_values(splits[6], (D, NH * HEAD_TOTAL), D ** -0.5, 0.1875, ((0, 16), (1, 2)))
    gate_weight = normal_values(splits[7], (D, QD), D ** -0.5, 0.1875, ((0, 16), (1, 2)))
    out_weight = normal_values(splits[8], (QD, D), (QD // 4) ** -0.5, 0.375, ((0, 2), (1, 16)))
    query_taps = normal_values(splits[9], (CONV, QD), CONV ** -0.5, 3.0, ((1, 2),))
    key_taps = normal_values(splits[10], (CONV, NH * QD), CONV ** -0.5, 3.0, ((1, 2),))
    value_taps = normal_values(splits[11], (CONV, NH * QD), CONV ** -0.5, 3.0, ((1, 2),))
    mixer_gain = jnp.clip(1.0 + 0.1 * jax.random.normal(splits[12], (D,), jnp.float32), 0.5, 1.5).astype(jnp.bfloat16)
    head_gain = jnp.clip(1.0 + 0.1 * jax.random.normal(splits[13], (HD,), jnp.float32), 0.5, 1.5).astype(jnp.bfloat16)
    feed_gain = jnp.clip(1.0 + 0.1 * jax.random.normal(splits[14], (D,), jnp.float32), 0.5, 1.5).astype(jnp.bfloat16)
    feed_gate = normal_values(splits[15], (D, FF), D ** -0.5, 0.1875, ((0, 16), (1, 2)))
    feed_up = normal_values(splits[16], (D, FF), D ** -0.5, 0.1875, ((0, 16), (1, 2)))
    feed_down = normal_values(splits[17], (FF, D), (FF // 4) ** -0.5, 0.21875, ((0, 2), (1, 16)))
    cotangent = normal_values(splits[18], (TOKEN_TOTAL, D), 1.0, 6.0, ((0, 16),))
    return dict(activations=activations, log_decay=log_decay, doc_starts=doc_starts, query_weight=query_weight, key_weight=key_weight, value_weight=value_weight, beta_weight=beta_weight, gate_weight=gate_weight, out_weight=out_weight, query_taps=query_taps, key_taps=key_taps, value_taps=value_taps, mixer_gain=mixer_gain, head_gain=head_gain, feed_gain=feed_gain, feed_gate=feed_gate, feed_up=feed_up, feed_down=feed_down, cotangent=cotangent)


TOP_PRECISION = lax.Precision.HIGHEST
NORM_EPS = 1e-05
UNIT_EPS = 1e-06

@jax.custom_vjp
def low(v):
    return lax.optimization_barrier(v.astype(jnp.bfloat16)).astype(jnp.float32)

@jax.custom_vjp
def low_back(v):
    return v

def low_keep(v):
    return (low(v), None)

def low_pass(kept, grad):
    return (grad,)

def back_keep(v):
    return (v, None)

def back_low(kept, grad):
    return (low(grad),)
low.defvjp(low_keep, low_pass)
low_back.defvjp(back_keep, back_low)

def root_norm(values, gain_vector):
    return values * lax.rsqrt(lax.optimization_barrier(jnp.mean(values * values, axis=-1, keepdims=True)) + NORM_EPS) * gain_vector

def unit_rows(values):
    return values * lax.rsqrt(lax.optimization_barrier(jnp.sum(values * values, axis=-1, keepdims=True)) + UNIT_EPS)

def product(former, latter):
    return jnp.dot(former, latter, precision=TOP_PRECISION)

def short_conv(raw_proj, conv_taps, same_doc):
    outcome = raw_proj * conv_taps[0]
    for offset in range(1, CONV):
        earlier = jnp.concatenate([jnp.zeros((offset, raw_proj.shape[1]), jnp.float32), raw_proj[:-offset]], 0)
        outcome = outcome + earlier * conv_taps[offset] * same_doc[offset][:, None]
    return outcome

def token_step(current_state, token_inputs):
    query_rows, key_rows, value_rows, beta_gate, decays = token_inputs
    current_state = current_state * decays[:, None, None]
    for substep in range(NH):
        current_key = key_rows[:, substep]
        retrieved_values = jnp.einsum('ji,jio->jo', current_key, current_state, precision=TOP_PRECISION)
        update = beta_gate[:, substep][:, None] * (value_rows[:, substep] - retrieved_values)
        current_state = current_state + current_key[:, :, None] * update[:, None, :]
    return (current_state, jnp.einsum('ji,jio->jo', query_rows, current_state, precision=TOP_PRECISION))

@jax.checkpoint
def block_step(current_state, block_inputs):
    return lax.scan(token_step, current_state, block_inputs)

def mixer_scan(query_rows, key_rows, value_rows, beta_gate, decays):
    count = query_rows.shape[0]
    blocks = count // BLOCK
    block_inputs = tuple((tensor.reshape((blocks, BLOCK) + tensor.shape[1:]) for tensor in (query_rows, key_rows, value_rows, beta_gate, decays)))
    initial = jnp.zeros((HEAD_TOTAL, HD, HD), jnp.float32)
    _, outcome = lax.scan(block_step, initial, block_inputs)
    return outcome.reshape(count, HEAD_TOTAL, HD)

def block_forward(activations, query_weight, key_weight, value_weight, beta_weight, gate_weight, out_weight, query_taps, key_taps, value_taps, mixer_gain, head_gain, feed_gain, feed_gate, feed_up, feed_down, decays, same_doc):
    normed = low(root_norm(activations, mixer_gain))
    raw_query = low_back(low(product(normed, query_weight)))
    raw_key = low_back(low(product(normed, key_weight)))
    raw_value = low_back(low(product(normed, value_weight)))
    beta_gate = jax.nn.sigmoid(low_back(product(normed, beta_weight))).reshape(TOKEN_TOTAL, HEAD_TOTAL, NH)
    gate_out = low_back(product(normed, gate_weight)).reshape(TOKEN_TOTAL, HEAD_TOTAL, HD)
    query_rows = low(unit_rows(jax.nn.silu(short_conv(raw_query, query_taps, same_doc)).reshape(TOKEN_TOTAL, HEAD_TOTAL, HD)) * HD ** (-0.5))
    key_rows = low(unit_rows(jax.nn.silu(short_conv(raw_key, key_taps, same_doc)).reshape(TOKEN_TOTAL, HEAD_TOTAL, NH, HD)))
    value_rows = low(jax.nn.silu(short_conv(raw_value, value_taps, same_doc)).reshape(TOKEN_TOTAL, HEAD_TOTAL, NH, HD))
    mixer_out = mixer_scan(query_rows, key_rows, value_rows, beta_gate, decays)
    heads_out = low(root_norm(mixer_out, head_gain) * jax.nn.silu(gate_out)).reshape(TOKEN_TOTAL, QD)
    hidden = activations + low_back(product(heads_out, out_weight))
    normed_ffn = low(root_norm(hidden, feed_gain))
    ffn_gate = low_back(product(normed_ffn, feed_gate))
    ffn_up = low_back(product(normed_ffn, feed_up))
    activation = low(jax.nn.silu(ffn_gate) * ffn_up)
    return hidden + low_back(product(activation, feed_down))

def reference(activations, log_decay, doc_starts, query_weight, key_weight, value_weight, beta_weight, gate_weight, out_weight, query_taps, key_taps, value_taps, mixer_gain, head_gain, feed_gain, feed_gate, feed_up, feed_down, cotangent):
    token_position = jnp.arange(TOKEN_TOTAL, dtype=jnp.int32)
    doc_index = lax.optimization_barrier(jnp.sum((token_position[:, None] >= doc_starts[None, :]).astype(jnp.int32), axis=1))
    is_start = jnp.any(token_position[:, None] == doc_starts[None, :], axis=1).astype(jnp.float32)
    mask_rows = []
    for offset in range(CONV):
        earlier = jnp.maximum(token_position - offset, 0).astype(jnp.int32)
        mask_rows.append(((doc_index[earlier] == doc_index) & (token_position >= offset)).astype(jnp.float32))
    same_doc = jnp.stack(mask_rows)
    decays = jnp.exp(log_decay) * (1.0 - is_start)[:, None]
    floats = tuple((tensor.astype(jnp.float32) for tensor in (activations, query_weight, key_weight, value_weight, beta_weight, gate_weight, out_weight, query_taps, key_taps, value_taps, mixer_gain, head_gain, feed_gain, feed_gate, feed_up, feed_down)))

    def forward_only(*params):
        return block_forward(*params, decays, same_doc)
    result, pullback = jax.vjp(forward_only, *floats)
    grads = pullback(cotangent.astype(jnp.float32))
    return (result.astype(jnp.bfloat16), grads[0], grads[1], grads[2], grads[3], grads[4], grads[5], grads[6], grads[7], grads[8], grads[9], grads[10], grads[11], grads[12], grads[13], grads[14], grads[15])
```

```python
import functools

import jax
import jax.numpy as jnp
from jax import lax
from jax.experimental import pallas as pl
from jax.experimental.pallas import tpu as pltpu
from jax.sharding import PartitionSpec as P

BLOCK = 64
RESET = 256.0
HALO = 16
NORM_EPS = 1e-05
UNIT_EPS = 1e-06
F32 = jnp.float32
BF16 = jnp.bfloat16


def product(former, latter):
    return jnp.dot(former, latter, preferred_element_type=F32)


def inner_rows(former, latter):
    return lax.dot_general(former, latter, (((0,), (0,)), ((), ())), preferred_element_type=F32)


def times_transposed(former, latter):
    return lax.dot_general(former, latter, (((1,), (1,)), ((), ())), preferred_element_type=F32)


def low(values):
    return values.astype(BF16)


def split(values):
    high = values.astype(BF16)
    return high, (values - high.astype(F32)).astype(BF16)


def fine(form, former, latter):
    a_high, a_low = split(former)
    b_high, b_low = split(latter)
    return form(a_high, b_high) + (form(a_low, b_high) + form(a_high, b_low))


def silu_slope(values, sigma):
    return sigma * (1.0 + values * (1.0 - sigma))


def norm_back(values, gain_vector, gradient):
    row_scale = lax.rsqrt(jnp.mean(values * values, axis=-1, keepdims=True) + NORM_EPS)
    unit_value = values * row_scale
    scaled_grad = gradient * gain_vector
    back_value = row_scale * (
        scaled_grad - unit_value * jnp.mean(scaled_grad * unit_value, axis=-1, keepdims=True)
    )
    return (back_value, gradient * unit_value)


def row_maps(rows):
    row = lax.broadcasted_iota(jnp.int32, (rows, rows), 0)
    col = lax.broadcasted_iota(jnp.int32, (rows, rows), 1)
    return row % BLOCK, col % BLOCK, row // BLOCK, col // BLOCK


def lower_inverse(system, row_token, col_token, same_token):
    rows = system.shape[0]
    row = lax.broadcasted_iota(jnp.int32, (rows, rows), 0)
    col = lax.broadcasted_iota(jnp.int32, (rows, rows), 1)
    inverse = jnp.where(row == col, 1.0, 0.0) - jnp.where(same_token, system, 0.0)
    size = 1
    while size < BLOCK:
        joins = (
            (row_token // (2 * size) == col_token // (2 * size))
            & ((row_token // size) % 2 == 1)
            & ((col_token // size) % 2 == 0)
        )
        joint = jnp.where(joins, system, 0.0)
        low_inverse = low(inverse)
        inverse = inverse - product(low(product(low_inverse, low(joint))), low_inverse)
        size *= 2
    residual = jnp.where(row == col, 1.0, 0.0) - inverse - fine(product, system, inverse)
    return inverse + product(low(inverse), low(residual))


def conv_rows(tile, halo, taps, same, columns):
    count = tile.shape[0]
    extended = jnp.concatenate([halo, tile], 0)
    windows = [tile] + [
        pltpu.roll(extended, offset, 0)[8:] for offset in range(1, taps.shape[0])
    ]
    outcome = tile * taps[0:1]
    for offset in range(1, taps.shape[0]):
        outcome = outcome + windows[offset] * taps[offset : offset + 1] * same[:, offset : offset + 1]
    return outcome, windows


def unit_scale(values):
    return lax.rsqrt(jnp.sum(values * values, axis=-1, keepdims=True) + UNIT_EPS)


def pieces_of(head, head_count, substeps, width):
    query = [(head * width, width)]
    keys = [((head_count + head * substeps + n) * width, width) for n in range(substeps)]
    values = [
        ((head_count + (head_count + head) * substeps + n) * width, width) for n in range(substeps)
    ]
    return query + keys + values


def forward_kernel(
    head_count, substeps, width,
    raw, before, edge, taps, same, beta, cum_col, cum_row,
    t_out, p_out, s_out, qtil_out, local_out, map_out, shift_out,
    chain,
):
    chunk = pl.program_id(0)
    rows = BLOCK * substeps
    row_token, col_token, row_step, col_step = row_maps(rows)
    upto = col_token <= row_token
    earlier = (col_token < row_token) | ((col_token == row_token) & (col_step < row_step))
    same_token = (col_token == row_token) & (col_step < row_step)
    eye = jnp.where(
        lax.broadcasted_iota(jnp.int32, (width, width), 0)
        == lax.broadcasted_iota(jnp.int32, (width, width), 1),
        1.0,
        0.0,
    )
    same_rows = same[...]

    @pl.when(chunk == 0)
    def _():
        for head in range(head_count):
            chain[head, :, :width] = eye
            chain[head, :, width:] = jnp.zeros((width, width), F32)

    for head in range(head_count):
        acts = []
        for start, size in pieces_of(head, head_count, substeps, width):
            tile = raw[:, start : start + size].astype(F32)
            halo = jnp.where(
                chunk == 0, edge[:, start : start + size], before[:, start : start + size]
            ).astype(F32)[HALO - 8 :]
            pre, _ = conv_rows(tile, halo, taps[:, start : start + size], same_rows, None)
            acts.append(pre * jax.nn.sigmoid(pre))
        query = low(acts[0] * unit_scale(acts[0]) * width ** (-0.5))
        key = low(jnp.concatenate([a * unit_scale(a) for a in acts[1 : 1 + substeps]], 0))
        value = low(jnp.concatenate(acts[1 + substeps :], 0))
        beta_col = jnp.concatenate(
            [beta[:, head * substeps + n : head * substeps + n + 1] for n in range(substeps)], 0
        )
        cum_token = cum_col[:, head : head + 1]
        cum_rows = jnp.concatenate([cum_token] * substeps, 0)
        cum_cols = cum_row[0, head : head + 1, :]
        last = cum_cols[:, BLOCK - 1 : BLOCK]
        ratio = jnp.exp(jnp.where(upto, cum_rows - cum_cols, -1e4))
        gram = times_transposed(key, key)
        system = jnp.where(earlier, beta_col * ratio * gram, 0.0)
        inverse = low(lower_inverse(system, row_token, col_token, same_token))
        t_out[0, head] = inverse
        carry = jnp.exp(cum_rows)
        key_f = key.astype(F32)
        right = jnp.concatenate(
            [low(beta_col * carry * key_f), low(beta_col * value.astype(F32))], 1
        )
        solved = product(inverse, right)
        solved_low = low(solved)
        end_keys = low(jnp.exp(last - cum_rows) * key_f)
        moved = inner_rows(end_keys, solved_low)
        query_mask = low(ratio[:BLOCK] * times_transposed(query, key))
        seen = product(query_mask, solved_low)
        query_eff = jnp.exp(cum_token) * query.astype(F32) - seen[:, :width]
        chained = chain[head]
        chained_low = low(chained)
        p_out[0, head] = chained_low[:, :width]
        s_out[0, head] = chained_low[:, width:]
        reach = product(low(query_eff), chained_low)
        qtil_out[:, head * width : (head + 1) * width] = low(reach[:, :width])
        local_out[:, head * width : (head + 1) * width] = reach[:, width:] + seen[:, width:]
        step_map = jnp.exp(last) * eye - moved[:, :width]
        new = fine(product, step_map, chained)
        new = jnp.concatenate([new[:, :width], new[:, width:] + moved[:, width:]], 1)
        chain[head] = new
        map_out[head] = new[:, :width]
        shift_out[head] = new[:, width:]


def run_forward(raw, edge, taps, same, beta, cum_col, cum_row, head_count, substeps, width):
    count, columns = raw.shape
    chunks = count // BLOCK
    rows = BLOCK * substeps
    per_halo = BLOCK // HALO
    whole = lambda *shape: pl.BlockSpec(shape, lambda c: (0,) * len(shape))
    tokens = lambda cols: pl.BlockSpec((BLOCK, cols), lambda c: (c, 0))
    square = pl.BlockSpec((1, head_count, width, width), lambda c: (c, 0, 0, 0))
    return pl.pallas_call(
        functools.partial(forward_kernel, head_count, substeps, width),
        grid=(chunks,),
        in_specs=[
            tokens(columns),
            pl.BlockSpec((HALO, columns), lambda c: (jnp.maximum(c * per_halo - 1, 0), 0)),
            whole(HALO, columns),
            whole(*taps.shape),
            tokens(same.shape[1]),
            tokens(beta.shape[1]),
            tokens(head_count),
            pl.BlockSpec((1, head_count, rows), lambda c: (c, 0, 0)),
        ],
        out_specs=[
            pl.BlockSpec((1, head_count, rows, rows), lambda c: (c, 0, 0, 0)),
            square,
            square,
            tokens(head_count * width),
            tokens(head_count * width),
            whole(head_count, width, width),
            whole(head_count, width, width),
        ],
        out_shape=[
            jax.ShapeDtypeStruct((chunks, head_count, rows, rows), BF16),
            jax.ShapeDtypeStruct((chunks, head_count, width, width), BF16),
            jax.ShapeDtypeStruct((chunks, head_count, width, width), BF16),
            jax.ShapeDtypeStruct((count, head_count * width), BF16),
            jax.ShapeDtypeStruct((count, head_count * width), F32),
            jax.ShapeDtypeStruct((head_count, width, width), F32),
            jax.ShapeDtypeStruct((head_count, width, width), F32),
        ],
        scratch_shapes=[pltpu.VMEM((head_count, width, 2 * width), F32)],
        compiler_params=pltpu.CompilerParams(
            dimension_semantics=("arbitrary",), vmem_limit_bytes=48 * 1024 * 1024
        ),
        name="mixer_forward",
    )(raw, raw, edge, taps, same, beta, cum_col, cum_row)


def backward_kernel(
    head_count, substeps, width,
    raw, before, edge, taps, same, same_next, beta, cum_col, cum_row,
    t_in, p_in, s_in, state_in, adjoint_in, d_out,
    d_raw, d_logit, tail_out, first_out, tap_out,
    adjoint, carried,
):
    step = pl.program_id(0)
    chunks = pl.num_programs(0)
    chunk = chunks - 1 - step
    rows = BLOCK * substeps
    tap_count = 4
    row_token, col_token, row_step, col_step = row_maps(rows)
    upto = col_token <= row_token
    earlier = (col_token < row_token) | ((col_token == row_token) & (col_step < row_step))
    same_rows = same[...]
    same_long = jnp.concatenate([same_rows, same_next[...]], 0)

    @pl.when(step == 0)
    def _():
        adjoint[...] = adjoint_in[...]
        carried[...] = jnp.zeros(carried.shape, F32)
        tap_out[...] = jnp.zeros(tap_out.shape, F32)

    logit_cols = []
    for head in range(head_count):
        pieces = pieces_of(head, head_count, substeps, width)
        pres, windows, acts, sigmas = [], [], [], []
        for start, size in pieces:
            tile = raw[:, start : start + size].astype(F32)
            halo = jnp.where(
                chunk == 0, edge[:, start : start + size], before[:, start : start + size]
            ).astype(F32)[HALO - 8 :]
            pre, window = conv_rows(tile, halo, taps[:, start : start + size], same_rows, None)
            sigma = jax.nn.sigmoid(pre)
            pres.append(pre)
            windows.append(window)
            sigmas.append(sigma)
            acts.append(pre * sigma)
        scales = [unit_scale(a) for a in acts[: 1 + substeps]]
        units = [a * s for a, s in zip(acts[: 1 + substeps], scales)]
        query = low(units[0] * width ** (-0.5))
        key = low(jnp.concatenate(units[1:], 0))
        value = low(jnp.concatenate(acts[1 + substeps :], 0)).astype(F32)
        key_f = key.astype(F32)
        beta_col = jnp.concatenate(
            [beta[:, head * substeps + n : head * substeps + n + 1] for n in range(substeps)], 0
        )
        cum_token = cum_col[:, head : head + 1]
        cum_rows = jnp.concatenate([cum_token] * substeps, 0)
        cum_cols = cum_row[0, head : head + 1, :]
        last = cum_cols[:, BLOCK - 1 : BLOCK]
        ratio = jnp.exp(jnp.where(upto, cum_rows - cum_cols, -1e4))
        carry = jnp.exp(cum_rows)
        carry_token = jnp.exp(cum_token)
        end_ratio = jnp.exp(last - cum_rows)
        inverse = t_in[0, head]
        state = low(s_in[0, head].astype(F32) + product(p_in[0, head], state_in[head]))
        gram = times_transposed(key, key)
        fresh = value - carry * product(key, state)
        update = product(inverse, low(beta_col * fresh))
        update_low = low(update)
        d_mix = d_out[:, head * width : (head + 1) * width]
        later = adjoint[head]
        later_low = low(later)
        query_mask = low(ratio[:BLOCK] * times_transposed(query, key))
        d_update = inner_rows(query_mask, d_mix) + product(low(end_ratio * key_f), later_low)
        d_right = inner_rows(inverse, low(d_update))
        d_right_low = low(d_right)
        d_system = jnp.where(earlier, -times_transposed(d_right_low, update_low) * ratio, 0.0)
        d_beta = jnp.sum(d_right * fresh, axis=-1, keepdims=True) + jnp.sum(
            d_system * gram, axis=-1, keepdims=True
        )
        d_gram = low(beta_col * d_system)
        d_value = beta_col * d_right
        d_scores = low(times_transposed(d_mix, update_low) * ratio[:BLOCK])
        d_query = carry_token * times_transposed(d_mix, state) + product(d_scores, key)
        d_key = (
            inner_rows(d_scores, query)
            + end_ratio * times_transposed(update_low, later_low)
            - (beta_col * carry) * times_transposed(d_right_low, state)
            + product(d_gram, key)
            + inner_rows(d_gram, key)
        )
        adjoint[head] = (
            jnp.exp(last) * later
            + inner_rows(low(carry_token * query.astype(F32)), d_mix)
            - inner_rows(low((beta_col * carry) * key_f), d_right_low)
        )
        logits = d_beta * beta_col * (1.0 - beta_col)
        logit_cols += [logits[n * BLOCK : (n + 1) * BLOCK] for n in range(substeps)]
        grads = [width ** (-0.5) * d_query]
        grads += [d_key[n * BLOCK : (n + 1) * BLOCK] for n in range(substeps)]
        grads += [d_value[n * BLOCK : (n + 1) * BLOCK] for n in range(substeps)]
        for at, (start, size) in enumerate(pieces):
            grad = grads[at]
            if at <= substeps:
                grad = scales[at] * (
                    grad - units[at] * jnp.sum(grad * units[at], axis=-1, keepdims=True)
                )
            grad = grad * silu_slope(pres[at], sigmas[at])
            long = jnp.concatenate([grad, carried[:, start : start + size]], 0)
            tap = taps[:, start : start + size]
            spread = grad * tap[0:1]
            sums = [jnp.sum(grad * windows[at][0], axis=0, keepdims=True)]
            for offset in range(1, tap_count):
                masked = long * same_long[:, offset : offset + 1]
                spread = spread + (
                    pltpu.roll(masked, BLOCK + 8 - offset, 0)[:BLOCK] * tap[offset : offset + 1]
                )
                sums.append(
                    jnp.sum(masked[:BLOCK] * windows[at][offset], axis=0, keepdims=True)
                )
            carried[:, start : start + size] = grad[:8]
            tap_out[:, start : start + size] += jnp.concatenate(sums, 0)
            d_raw[:, start : start + size] = low(spread)

            @pl.when(step == 0)
            def _():
                tail_out[:, start : start + size] = spread[BLOCK - 8 :]

            @pl.when(step == chunks - 1)
            def _():
                first_out[:, start : start + size] = grad[:8]

    d_logit[...] = jnp.concatenate(logit_cols, 1)


def run_backward(
    raw, edge, taps, same, beta, cum_col, cum_row, t_part, p_part, s_part, state_in, adjoint_in,
    d_out, head_count, substeps, width,
):
    count, columns = raw.shape
    chunks = count // BLOCK
    rows = BLOCK * substeps
    per_halo = BLOCK // HALO
    per_eight = BLOCK // 8
    whole = lambda *shape: pl.BlockSpec(shape, lambda c: (0,) * len(shape))
    tokens = lambda cols: pl.BlockSpec((BLOCK, cols), lambda c: (chunks - 1 - c, 0))
    square = pl.BlockSpec((1, head_count, width, width), lambda c: (chunks - 1 - c, 0, 0, 0))
    return pl.pallas_call(
        functools.partial(backward_kernel, head_count, substeps, width),
        grid=(chunks,),
        in_specs=[
            tokens(columns),
            pl.BlockSpec(
                (HALO, columns), lambda c: (jnp.maximum((chunks - 1 - c) * per_halo - 1, 0), 0)
            ),
            whole(HALO, columns),
            whole(*taps.shape),
            tokens(same.shape[1]),
            pl.BlockSpec(
                (8, same.shape[1]),
                lambda c: (jnp.minimum((chunks - c) * per_eight, chunks * per_eight - 1), 0),
            ),
            tokens(beta.shape[1]),
            tokens(head_count),
            pl.BlockSpec((1, head_count, rows), lambda c: (chunks - 1 - c, 0, 0)),
            pl.BlockSpec((1, head_count, rows, rows), lambda c: (chunks - 1 - c, 0, 0, 0)),
            square,
            square,
            whole(head_count, width, width),
            whole(head_count, width, width),
            tokens(head_count * width),
        ],
        out_specs=[
            tokens(columns),
            tokens(head_count * substeps),
            whole(8, columns),
            whole(8, columns),
            whole(taps.shape[0], columns),
        ],
        out_shape=[
            jax.ShapeDtypeStruct((count, columns), BF16),
            jax.ShapeDtypeStruct((count, head_count * substeps), F32),
            jax.ShapeDtypeStruct((8, columns), F32),
            jax.ShapeDtypeStruct((8, columns), F32),
            jax.ShapeDtypeStruct((taps.shape[0], columns), F32),
        ],
        scratch_shapes=[
            pltpu.VMEM((head_count, width, width), F32),
            pltpu.VMEM((8, columns), F32),
        ],
        compiler_params=pltpu.CompilerParams(
            dimension_semantics=("arbitrary",), vmem_limit_bytes=48 * 1024 * 1024
        ),
        name="mixer_backward",
    )(
        raw, raw, edge, taps, same, same, beta, cum_col, cum_row, t_part, p_part, s_part,
        state_in, adjoint_in, d_out,
    )


def shift_seq(array, by):
    count = lax.axis_size("seq")
    return lax.ppermute(
        array, "seq", [(i, i + by) for i in range(count) if 0 <= i + by < count]
    )


def swap_seq(array, distance):
    return lax.ppermute(array, "seq", [(i, i ^ distance) for i in range(lax.axis_size("seq"))])


def swap_head(array):
    return lax.ppermute(array, "head", [(0, 1), (1, 0)])


def head_sum(array):
    return array + swap_head(array)


def state_dot(former, latter):
    return jnp.einsum("hij,hjk->hik", former, latter, precision=lax.Precision.HIGH)


def state_dot_t(former, latter):
    return jnp.einsum("hji,hjk->hik", former, latter, precision=lax.Precision.HIGH)


def states_before(state_map, state_shift):
    count, mine = lax.axis_size("seq"), lax.axis_index("seq")
    before = jnp.zeros_like(state_shift)
    before_map = jnp.broadcast_to(jnp.eye(state_map.shape[-1], dtype=F32), state_map.shape)
    maps, shifts = [], []
    distance = 1
    group_map, group_shift = state_map, state_shift
    while distance < count:
        other_map, other_shift = swap_seq(group_map, distance), swap_seq(group_shift, distance)
        upper = (mine & distance) != 0
        maps.append((group_map, other_map, upper))
        before = jnp.where(upper, state_dot(before_map, other_shift) + before, before)
        before_map = jnp.where(upper, state_dot(before_map, other_map), before_map)
        first_map = jnp.where(upper, other_map, group_map)
        first_shift = jnp.where(upper, other_shift, group_shift)
        second_map = jnp.where(upper, group_map, other_map)
        second_shift = jnp.where(upper, group_shift, other_shift)
        group_shift = state_dot(second_map, first_shift) + second_shift
        group_map = state_dot(second_map, first_map)
        distance *= 2
    return before, maps


def adjoints_after(own, maps):
    after = jnp.zeros_like(own)
    after_map = jnp.broadcast_to(jnp.eye(own.shape[-1], dtype=F32), own.shape)
    group = own
    distance = 1
    for group_map, other_map, upper in maps:
        other = swap_seq(group, distance)
        after = jnp.where(upper, after, after + state_dot_t(after_map, other))
        after_map = jnp.where(upper, after_map, state_dot(other_map, after_map))
        first_own = jnp.where(upper, other, group)
        second_own = jnp.where(upper, group, other)
        first_map = jnp.where(upper, other_map, group_map)
        group = first_own + state_dot_t(first_map, second_own)
        distance *= 2
    return after


def per_device(
    activations,
    log_decay,
    doc_starts,
    query_weight,
    key_weight,
    value_weight,
    beta_weight,
    gate_weight,
    out_weight,
    query_taps,
    key_taps,
    value_taps,
    mixer_gain,
    head_gain,
    feed_gain,
    feed_gate,
    feed_up,
    feed_down,
    cotangent,
):
    count, features = activations.shape
    tap_count = query_taps.shape[0]
    width = head_gain.shape[0]
    query_cols = query_weight.shape[1]
    key_cols = key_weight.shape[1]
    conv_cols = query_cols + 2 * key_cols
    hidden_cols = feed_gate.shape[1]
    head_count = query_cols // width
    beta_cols = beta_weight.shape[1]
    substeps = beta_cols // head_count
    device_rank = lax.axis_index("seq")
    head_rank = lax.axis_index("head")
    extra = 128
    shard_rows = query_weight.shape[0]
    pad = jnp.zeros((shard_rows, extra - beta_cols - 2), BF16)
    first_pack = jnp.concatenate(
        [
            query_weight,
            key_weight,
            value_weight,
            gate_weight,
            beta_weight,
            mixer_gain[:, None],
            feed_gain[:, None],
            pad,
        ],
        1,
    )
    second_pack = jnp.concatenate([out_weight.T, feed_gate, feed_up, feed_down.T], 1)
    first_full = lax.all_gather(first_pack, "seq", axis=0, tiled=True)
    first_full, second_pack = lax.optimization_barrier((first_full, second_pack))
    second_full = lax.all_gather(second_pack, "seq", axis=0, tiled=True)
    weight_conv = first_full[:, :conv_cols]
    weight_gate = first_full[:, conv_cols : conv_cols + query_cols]
    tail_cols = first_full[:, conv_cols + query_cols :]
    weight_beta = tail_cols[:, :beta_cols]
    gain_one = tail_cols[:, beta_cols].astype(F32)
    gain_two = tail_cols[:, beta_cols + 1].astype(F32)
    weight_out = second_full[:, :query_cols]
    weight_feed = second_full[:, query_cols : query_cols + 2 * hidden_cols]
    weight_down = second_full[:, query_cols + 2 * hidden_cols :]

    token_position = device_rank * count + jnp.arange(count, dtype=jnp.int32)
    is_start = jnp.any(token_position[:, None] == doc_starts[None, :], axis=1)

    def same_docs(position):
        doc = lambda p: jnp.sum((p[:, None] >= doc_starts[None, :]).astype(jnp.int32), axis=1)
        own = doc(position)
        return jnp.stack(
            [
                ((doc(position - offset) == own) & (position >= offset)).astype(F32)
                for offset in range(tap_count)
            ],
            1,
        )

    same = same_docs(token_position)
    log_gate = log_decay - RESET * is_start.astype(F32)[:, None]
    chunks = count // BLOCK
    cumulative = jnp.cumsum(log_gate.reshape(chunks, BLOCK, head_count), axis=1)
    cum_col = cumulative.reshape(count, head_count)
    cum_row = jnp.concatenate([jnp.swapaxes(cumulative, 1, 2)] * substeps, 2)
    taps_all = jnp.concatenate([query_taps, key_taps, value_taps], 1).astype(F32)

    inputs = activations.astype(F32)
    in_scale = lax.rsqrt(jnp.mean(inputs * inputs, axis=-1, keepdims=True) + NORM_EPS)
    normed = low(inputs * in_scale * gain_one)
    raw_all = low(product(normed, weight_conv))
    beta_gate = jax.nn.sigmoid(product(normed, weight_beta))
    gate_view = product(normed, weight_gate)
    edge = shift_seq(raw_all[count - HALO :], 1)
    t_part, p_part, s_part, q_reach, local_out, state_map, state_shift = run_forward(
        raw_all, edge, taps_all, same, beta_gate, cum_col, cum_row, head_count, substeps, width
    )
    state_in, maps = states_before(state_map, state_shift)
    state_low = low(state_in)

    by_head = lambda array: array.reshape(count, head_count, width)
    mixer_out = by_head(local_out) + jnp.einsum(
        "thk,hkv->thv", by_head(q_reach), state_low, preferred_element_type=F32
    )
    head_gain_f = head_gain.astype(F32)
    head_scale = lax.rsqrt(jnp.mean(mixer_out * mixer_out, axis=-1, keepdims=True) + NORM_EPS)
    head_unit = mixer_out * head_scale
    gate_view = by_head(gate_view)
    gate_sigma = jax.nn.sigmoid(gate_view)
    gate_act = gate_view * gate_sigma
    heads_out = low(head_unit * head_gain_f * gate_act).reshape(count, query_cols)
    hidden = inputs + head_sum(times_transposed(heads_out, weight_out))
    feed_scale = lax.rsqrt(jnp.mean(hidden * hidden, axis=-1, keepdims=True) + NORM_EPS)
    normed_ffn = low(hidden * feed_scale * gain_two)
    ffn = product(normed_ffn, weight_feed)
    ffn_gate, ffn_up = ffn[:, :hidden_cols], ffn[:, hidden_cols:]
    ffn_sigma = jax.nn.sigmoid(ffn_gate)
    activation = low(ffn_gate * ffn_sigma * ffn_up)
    branch_two = low(times_transposed(activation, weight_down))
    half = features // lax.axis_size("head")
    own_half = lambda array: lax.dynamic_slice_in_dim(array, head_rank * half, half, 1)
    other_half = lambda array: lax.dynamic_slice_in_dim(array, (1 - head_rank) * half, half, 1)
    output = low(
        own_half(hidden)
        + own_half(branch_two).astype(F32)
        + swap_head(other_half(branch_two)).astype(F32)
    )

    grad_result = cotangent.astype(F32)
    d_activation = product(cotangent, weight_down)
    d_up = low(d_activation * (ffn_gate * ffn_sigma))
    d_gate = low(d_activation * ffn_up * silu_slope(ffn_gate, ffn_sigma))
    d_ffn = jnp.concatenate([d_gate, d_up], 1)
    d_normed_ffn = head_sum(times_transposed(d_ffn, weight_feed))
    d_hidden_norm, feed_terms = norm_back(hidden, gain_two, d_normed_ffn)
    grad_feed_gain = jnp.sum(feed_terms, axis=0)
    d_hidden = grad_result + d_hidden_norm
    grad_mixer = low(d_hidden)
    d_heads = by_head(product(grad_mixer, weight_out))
    d_gate_logit = low(
        d_heads * head_unit * head_gain_f * silu_slope(gate_view, gate_sigma)
    ).reshape(count, query_cols)
    d_mixer_out, head_terms = norm_back(mixer_out, head_gain_f, d_heads * gate_act)
    head_gain_part = jnp.sum(head_terms, axis=(0, 1))
    d_mixer_low = low(d_mixer_out)
    own_part = jnp.einsum("thk,thv->hkv", by_head(q_reach), d_mixer_low, preferred_element_type=F32)
    adjoint = adjoints_after(own_part, maps)

    second_grads = jnp.concatenate(
        [
            low(inner_rows(grad_mixer, heads_out)),
            low(inner_rows(normed_ffn, d_ffn)),
            low(inner_rows(cotangent, activation)),
        ],
        1,
    )
    second_sum = lax.psum_scatter(second_grads, "seq", scatter_dimension=0, tiled=True).astype(F32)

    d_raw, d_beta_logit, tail, first_rows, tap_grads = run_backward(
        raw_all, edge, taps_all, same, beta_gate, cum_col, cum_row, t_part, p_part, s_part,
        state_low, adjoint, d_mixer_low.reshape(count, query_cols), head_count, substeps, width,
    )
    returned = shift_seq(first_rows, -1)
    same_after = same_docs(token_position[-1] + 1 + jnp.arange(8, dtype=jnp.int32))
    spread = jnp.zeros_like(tail)
    for offset in range(1, tap_count):
        masked = returned * same_after[:, offset : offset + 1] * taps_all[offset]
        spread = spread + jnp.pad(masked[:offset], ((8 - offset, 0), (0, 0)))
    d_raw = lax.dynamic_update_slice(d_raw, low(tail + spread), (count - 8, 0))
    d_beta_low = low(d_beta_logit)
    grad_conv = inner_rows(normed, d_raw)
    grad_gate = inner_rows(normed, d_gate_logit)
    grad_beta = inner_rows(normed, d_beta_low)
    d_normed_part = times_transposed(d_raw, weight_conv) + (
        times_transposed(d_beta_low, weight_beta) + times_transposed(d_gate_logit, weight_gate)
    )
    d_normed = head_sum(low(d_normed_part).astype(F32))
    d_input_norm, mixer_terms = norm_back(inputs, gain_one, d_normed)
    grad_mixer_gain = jnp.sum(mixer_terms, axis=0)
    grad_input = own_half(d_hidden + d_input_norm)
    first_grads = jnp.concatenate(
        [
            low(grad_conv),
            low(grad_gate),
            low(grad_beta),
            low(grad_mixer_gain)[:, None],
            low(grad_feed_gain)[:, None],
            jnp.zeros((features, extra - beta_cols - 2), BF16),
        ],
        1,
    )
    first_sum = lax.psum_scatter(first_grads, "seq", scatter_dimension=0, tiled=True).astype(F32)
    head_gain_sum = head_sum(head_gain_part)
    tap_total, grad_head_gain = lax.psum((tap_grads, head_gain_sum), "seq")
    cut = lambda array, start, size: array[:, start : start + size]
    base = conv_cols + query_cols
    return (
        output,
        grad_input,
        cut(first_sum, 0, query_cols),
        cut(first_sum, query_cols, key_cols),
        cut(first_sum, query_cols + key_cols, key_cols),
        cut(first_sum, base, beta_cols),
        cut(first_sum, conv_cols, query_cols),
        cut(second_sum, 0, query_cols).T,
        cut(tap_total, 0, query_cols),
        cut(tap_total, query_cols, key_cols),
        cut(tap_total, query_cols + key_cols, key_cols),
        first_sum[:, base + beta_cols],
        grad_head_gain,
        first_sum[:, base + beta_cols + 1],
        cut(second_sum, query_cols, hidden_cols),
        cut(second_sum, query_cols + hidden_cols, hidden_cols),
        cut(second_sum, query_cols + 2 * hidden_cols, hidden_cols).T,
    )


def solution(mesh):
    in_specs = (
        P("seq", None),
        P("seq", "head"),
        P(),
        P("seq", "head"),
        P("seq", "head"),
        P("seq", "head"),
        P("seq", "head"),
        P("seq", "head"),
        P("head", "seq"),
        P(None, "head"),
        P(None, "head"),
        P(None, "head"),
        P("seq"),
        P(),
        P("seq"),
        P("seq", "head"),
        P("seq", "head"),
        P("head", "seq"),
        P("seq", None),
    )
    out_specs = (
        P("seq", "head"),
        P("seq", "head"),
        P("seq", "head"),
        P("seq", "head"),
        P("seq", "head"),
        P("seq", "head"),
        P("seq", "head"),
        P("head", "seq"),
        P(None, "head"),
        P(None, "head"),
        P(None, "head"),
        P("seq"),
        P(),
        P("seq"),
        P("seq", "head"),
        P("seq", "head"),
        P("head", "seq"),
    )
    return jax.shard_map(
        per_device, mesh=mesh, in_specs=in_specs, out_specs=out_specs, check_vma=False
    )
```

```python
import functools

import jax
import jax.numpy as jnp
from jax import lax
from jax.experimental import pallas as pl
from jax.experimental.pallas import tpu as pltpu
from jax.sharding import PartitionSpec as P

BLOCK = 64
RESET = 256.0
HALO = 16
BACK_CALLS = 3
NORM_EPS = 1e-05
UNIT_EPS = 1e-06
F32 = jnp.float32
BF16 = jnp.bfloat16


def product(former, latter):
    return jnp.dot(former, latter, preferred_element_type=F32)


def inner_rows(former, latter):
    return lax.dot_general(former, latter, (((0,), (0,)), ((), ())), preferred_element_type=F32)


def times_transposed(former, latter):
    return lax.dot_general(former, latter, (((1,), (1,)), ((), ())), preferred_element_type=F32)


def low(values):
    return values.astype(BF16)


def split(values):
    high = values.astype(BF16)
    return high, (values - high.astype(F32)).astype(BF16)


def fine(form, former, latter):
    a_high, a_low = split(former)
    b_high, b_low = split(latter)
    return form(a_high, b_high) + (form(a_low, b_high) + form(a_high, b_low))


def silu_slope(values, sigma):
    return sigma * (1.0 + values * (1.0 - sigma))


def norm_back(values, gain_vector, gradient):
    row_scale = lax.rsqrt(jnp.mean(values * values, axis=-1, keepdims=True) + NORM_EPS)
    unit_value = values * row_scale
    scaled_grad = gradient * gain_vector
    back_value = row_scale * (
        scaled_grad - unit_value * jnp.mean(scaled_grad * unit_value, axis=-1, keepdims=True)
    )
    return (back_value, gradient * unit_value)


def row_maps(rows):
    row = lax.broadcasted_iota(jnp.int32, (rows, rows), 0)
    col = lax.broadcasted_iota(jnp.int32, (rows, rows), 1)
    return row % BLOCK, col % BLOCK, row // BLOCK, col // BLOCK


def lower_inverses(systems, apart):
    rows = systems[0].shape[0]
    row = lax.broadcasted_iota(jnp.int32, (rows, rows), 0)
    col = lax.broadcasted_iota(jnp.int32, (rows, rows), 1)
    eye = jnp.where(row == col, 1.0, 0.0)
    inverses = [eye - jnp.where(apart == 0, system, 0.0) for system in systems]
    level = 0
    while (1 << level) < BLOCK:
        joins = (apart >> level) == 1
        joints = [low(jnp.where(joins, system, 0.0)) for system in systems]
        lows = [low(inverse) for inverse in inverses]
        halves = [low(product(a, b)) for a, b in zip(lows, joints)]
        inverses = [c - product(a, b) for a, b, c in zip(halves, lows, inverses)]
        level += 1
    return inverses


def conv_rows(tile, halo, taps, same, columns):
    count = tile.shape[0]
    extended = jnp.concatenate([halo, tile], 0)
    windows = [tile] + [
        pltpu.roll(extended, offset, 0)[8:] for offset in range(1, taps.shape[0])
    ]
    outcome = tile * taps[0:1]
    for offset in range(1, taps.shape[0]):
        outcome = outcome + windows[offset] * taps[offset : offset + 1] * same[:, offset : offset + 1]
    return outcome, windows


def unit_scale(values):
    return lax.rsqrt(jnp.sum(values * values, axis=-1, keepdims=True) + UNIT_EPS)


def pieces_of(head, head_count, substeps, width):
    query = [(head * width, width)]
    keys = [((head_count + head * substeps + n) * width, width) for n in range(substeps)]
    values = [
        ((head_count + (head_count + head) * substeps + n) * width, width) for n in range(substeps)
    ]
    return query + keys + values


def forward_kernel(
    head_count, substeps, width,
    raw, before, edge, taps, same, beta, cum_col, cum_row,
    t_out, p_out, s_out, qtil_out, local_out, group_out,
    chain,
):
    chunk = pl.program_id(0)
    rows = BLOCK * substeps
    row_token, col_token, row_step, col_step = row_maps(rows)
    upto = col_token <= row_token
    earlier = (col_token < row_token) | ((col_token == row_token) & (col_step < row_step))
    apart = row_token ^ col_token
    eye = jnp.where(
        lax.broadcasted_iota(jnp.int32, (width, width), 0)
        == lax.broadcasted_iota(jnp.int32, (width, width), 1),
        1.0,
        0.0,
    )
    same_rows = same[...]

    @pl.when(chunk == 0)
    def _():
        for head in range(head_count):
            chain[head, :, :width] = eye
            chain[head, :, width:] = jnp.zeros((width, width), F32)

    heads = range(head_count)
    queries, keys, values, betas, ratios, systems = [], [], [], [], [], []
    for head in heads:
        acts = []
        for start, size in pieces_of(head, head_count, substeps, width):
            tile = raw[:, start : start + size].astype(F32)
            halo = jnp.where(
                chunk == 0, edge[:, start : start + size], before[:, start : start + size]
            ).astype(F32)[HALO - 8 :]
            pre, _ = conv_rows(tile, halo, taps[:, start : start + size], same_rows, None)
            acts.append(pre * jax.nn.sigmoid(pre))
        queries.append(low(acts[0] * unit_scale(acts[0]) * width ** (-0.5)))
        keys.append(low(jnp.concatenate([a * unit_scale(a) for a in acts[1 : 1 + substeps]], 0)))
        values.append(low(jnp.concatenate(acts[1 + substeps :], 0)))
        betas.append(
            jnp.concatenate(
                [beta[:, head * substeps + n : head * substeps + n + 1] for n in range(substeps)], 0
            )
        )
    cum_rows = [jnp.concatenate([cum_col[:, h : h + 1]] * substeps, 0) for h in heads]
    cum_cols = [cum_row[0, h : h + 1, :] for h in heads]
    lasts = [c[:, BLOCK - 1 : BLOCK] for c in cum_cols]
    ratios = [jnp.exp(jnp.where(upto, a - b, -1e4)) for a, b in zip(cum_rows, cum_cols)]
    grams = [times_transposed(key, key) for key in keys]
    scores = [times_transposed(query, key) for query, key in zip(queries, keys)]
    systems = [
        jnp.where(earlier, beta_col * ratio * gram, 0.0)
        for beta_col, ratio, gram in zip(betas, ratios, grams)
    ]
    inverses = [low(inverse) for inverse in lower_inverses(systems, apart)]
    rights = [
        jnp.concatenate(
            [
                low(beta_col * jnp.exp(cum) * key.astype(F32)),
                low(beta_col * value.astype(F32)),
            ],
            1,
        )
        for beta_col, cum, key, value in zip(betas, cum_rows, keys, values)
    ]
    solved = [low(product(inverse, right)) for inverse, right in zip(inverses, rights)]
    ends = [
        low(jnp.exp(last - cum) * key.astype(F32))
        for last, cum, key in zip(lasts, cum_rows, keys)
    ]
    moved = [inner_rows(end, both) for end, both in zip(ends, solved)]
    seen = [
        product(low(ratio[:BLOCK] * score), both)
        for ratio, score, both in zip(ratios, scores, solved)
    ]
    chains = [chain[head] for head in heads]
    chains_low = [low(chained) for chained in chains]
    reached = [
        product(
            low(jnp.exp(cum[:BLOCK]) * query.astype(F32) - see[:, :width]), chained
        )
        for cum, query, see, chained in zip(cum_rows, queries, seen, chains_low)
    ]
    grown = [
        fine(product, jnp.exp(last) * eye - move[:, :width], chained)
        for last, move, chained in zip(lasts, moved, chains)
    ]
    for head in heads:
        at = slice(head * width, (head + 1) * width)
        t_out[0, head] = inverses[head]
        p_out[0, head] = chains_low[head][:, :width]
        s_out[0, head] = chains_low[head][:, width:]
        qtil_out[:, at] = low(reached[head][:, :width])
        local_out[:, at] = reached[head][:, width:] + seen[head][:, width:]
        new_map = grown[head][:, :width]
        new_shift = grown[head][:, width:] + moved[head][:, width:]
        chain[head, :, :width] = new_map
        chain[head, :, width:] = new_shift
        group_out[head, :, :width] = new_map
        group_out[head, :, width:] = new_shift


def run_forward(raw, edge, taps, same, beta, cum_col, cum_row, head_count, substeps, width):
    count, columns = raw.shape
    chunks = count // BLOCK
    rows = BLOCK * substeps
    per_halo = BLOCK // HALO
    whole = lambda *shape: pl.BlockSpec(shape, lambda c: (0,) * len(shape))
    tokens = lambda cols: pl.BlockSpec((BLOCK, cols), lambda c: (c, 0))
    square = pl.BlockSpec((1, head_count, width, width), lambda c: (c, 0, 0, 0))
    return pl.pallas_call(
        functools.partial(forward_kernel, head_count, substeps, width),
        grid=(chunks,),
        in_specs=[
            tokens(columns),
            pl.BlockSpec((HALO, columns), lambda c: (jnp.maximum(c * per_halo - 1, 0), 0)),
            whole(HALO, columns),
            whole(*taps.shape),
            tokens(same.shape[1]),
            tokens(beta.shape[1]),
            tokens(head_count),
            pl.BlockSpec((1, head_count, rows), lambda c: (c, 0, 0)),
        ],
        out_specs=[
            pl.BlockSpec((1, head_count, rows, rows), lambda c: (c, 0, 0, 0)),
            square,
            square,
            tokens(head_count * width),
            tokens(head_count * width),
            whole(head_count, width, 2 * width),
        ],
        out_shape=[
            jax.ShapeDtypeStruct((chunks, head_count, rows, rows), BF16),
            jax.ShapeDtypeStruct((chunks, head_count, width, width), BF16),
            jax.ShapeDtypeStruct((chunks, head_count, width, width), BF16),
            jax.ShapeDtypeStruct((count, head_count * width), BF16),
            jax.ShapeDtypeStruct((count, head_count * width), F32),
            jax.ShapeDtypeStruct((head_count, width, 2 * width), F32),
        ],
        scratch_shapes=[pltpu.VMEM((head_count, width, 2 * width), F32)],
        compiler_params=pltpu.CompilerParams(
            dimension_semantics=("arbitrary",), vmem_limit_bytes=48 * 1024 * 1024
        ),
        name="mixer_forward",
    )(raw, raw, edge, taps, same, beta, cum_col, cum_row)


def backward_kernel(
    head_count, substeps, width, end,
    raw, before, edge, taps, same, same_next, beta, cum_col, cum_row,
    t_in, p_in, s_in, state_in, d_out, adjoint_in, carried_in, tap_in, raw_in, logit_in,
    d_raw, d_logit, tail_out, adjoint, carried, tap_out,
    tail_next,
):
    step = pl.program_id(0)
    chunk = end - 1 - step
    rows = BLOCK * substeps
    tap_count = taps.shape[0]
    row_token, col_token, row_step, col_step = row_maps(rows)
    upto = col_token <= row_token
    earlier = (col_token < row_token) | ((col_token == row_token) & (col_step < row_step))
    same_rows = same[...]
    same_long = jnp.concatenate([same_rows, same_next[...]], 0)

    @pl.when(step == 0)
    def _():
        adjoint[...] = adjoint_in[...]
        carried[...] = carried_in[...]
        tap_out[...] = tap_in[...]

    heads = range(head_count)
    pieces = [pieces_of(head, head_count, substeps, width) for head in heads]
    pres, sigmas, scales, units = [], [], [], []
    queries, keys, values, betas = [], [], [], []

    def windows_of(start, size):
        tile = raw[:, start : start + size].astype(F32)
        halo = jnp.where(
            chunk == 0, edge[:, start : start + size], before[:, start : start + size]
        ).astype(F32)[HALO - 8 :]
        return conv_rows(tile, halo, taps[:, start : start + size], same_rows, None)

    for head in heads:
        pre = [windows_of(start, size)[0] for start, size in pieces[head]]
        sigma = [jax.nn.sigmoid(p) for p in pre]
        acts = [p * s for p, s in zip(pre, sigma)]
        pres.append(pre)
        sigmas.append(sigma)
        scales.append([unit_scale(a) for a in acts[: 1 + substeps]])
        units.append([a * s for a, s in zip(acts[: 1 + substeps], scales[head])])
        queries.append(low(units[head][0] * width ** (-0.5)))
        keys.append(low(jnp.concatenate(units[head][1:], 0)))
        values.append(low(jnp.concatenate(acts[1 + substeps :], 0)))
        betas.append(
            jnp.concatenate(
                [beta[:, head * substeps + n : head * substeps + n + 1] for n in range(substeps)], 0
            )
        )
    cum_rows = [jnp.concatenate([cum_col[:, h : h + 1]] * substeps, 0) for h in heads]
    cum_cols = [cum_row[0, h : h + 1, :] for h in heads]
    lasts = [c[:, BLOCK - 1 : BLOCK] for c in cum_cols]
    ratios = [jnp.exp(jnp.where(upto, a - b, -1e4)) for a, b in zip(cum_rows, cum_cols)]
    carries = [jnp.exp(c) for c in cum_rows]
    end_ratios = [jnp.exp(last - c) for last, c in zip(lasts, cum_rows)]
    inverses = [t_in[0, h] for h in heads]
    laters = [adjoint[h] for h in heads]
    laters_low = [low(later) for later in laters]
    d_mixes = [d_out[:, h * width : (h + 1) * width] for h in heads]
    states = [low(s_in[0, h].astype(F32) + product(p_in[0, h], state_in[h])) for h in heads]
    scores = [times_transposed(query, key) for query, key in zip(queries, keys)]
    masks = [low(ratio[:BLOCK] * score) for ratio, score in zip(ratios, scores)]
    d_updates = [
        low(inner_rows(mask, d_mix) + product(low(end * key.astype(F32)), later))
        for mask, d_mix, end, key, later in zip(masks, d_mixes, end_ratios, keys, laters_low)
    ]
    d_rights = [inner_rows(inverse, d_update) for inverse, d_update in zip(inverses, d_updates)]
    d_rights_low = [low(d_right) for d_right in d_rights]
    d_states = [
        inner_rows(low(carry[:BLOCK] * query.astype(F32)), d_mix)
        - inner_rows(low((beta_col * carry) * key.astype(F32)), d_right)
        for carry, query, d_mix, beta_col, key, d_right in zip(
            carries, queries, d_mixes, betas, keys, d_rights_low
        )
    ]
    for h in heads:
        adjoint[h] = jnp.exp(lasts[h]) * laters[h] + d_states[h]
    grams = [times_transposed(key, key) for key in keys]
    freshes = [
        value.astype(F32) - carry * product(key, state)
        for value, carry, key, state in zip(values, carries, keys, states)
    ]
    updates = [
        low(product(inverse, low(beta_col * fresh)))
        for inverse, beta_col, fresh in zip(inverses, betas, freshes)
    ]
    d_systems = [
        jnp.where(earlier, -times_transposed(d_right, update) * ratio, 0.0)
        for d_right, update, ratio in zip(d_rights_low, updates, ratios)
    ]
    d_scores = [
        low(times_transposed(d_mix, update) * ratio[:BLOCK])
        for d_mix, update, ratio in zip(d_mixes, updates, ratios)
    ]
    d_grams = [low(beta_col * d_system) for beta_col, d_system in zip(betas, d_systems)]
    d_betas = [
        jnp.sum(d_right * fresh, axis=-1, keepdims=True)
        + jnp.sum(d_system * gram, axis=-1, keepdims=True)
        for d_right, fresh, d_system, gram in zip(d_rights, freshes, d_systems, grams)
    ]
    d_queries = [
        carry[:BLOCK] * times_transposed(d_mix, state) + product(d_score, key)
        for carry, d_mix, state, d_score, key in zip(carries, d_mixes, states, d_scores, keys)
    ]
    d_keys = [
        inner_rows(d_scores[h], queries[h])
        + end_ratios[h] * times_transposed(updates[h], laters_low[h])
        - (betas[h] * carries[h]) * times_transposed(d_rights_low[h], states[h])
        + product(d_grams[h], keys[h])
        + inner_rows(d_grams[h], keys[h])
        for h in heads
    ]
    logit_cols = []
    for h in heads:
        logits = d_betas[h] * betas[h] * (1.0 - betas[h])
        logit_cols += [logits[n * BLOCK : (n + 1) * BLOCK] for n in range(substeps)]
    d_logit[...] = jnp.concatenate(logit_cols, 1)

    for head in heads:
        d_value = betas[head] * d_rights[head]
        grads = [width ** (-0.5) * d_queries[head]]
        grads += [d_keys[head][n * BLOCK : (n + 1) * BLOCK] for n in range(substeps)]
        grads += [d_value[n * BLOCK : (n + 1) * BLOCK] for n in range(substeps)]
        for at, (start, size) in enumerate(pieces[head]):
            grad = grads[at]
            if at <= substeps:
                unit = units[head][at]
                grad = scales[head][at] * (
                    grad - unit * jnp.sum(grad * unit, axis=-1, keepdims=True)
                )
            grad = grad * silu_slope(pres[head][at], sigmas[head][at])
            windows = windows_of(start, size)[1]
            long = jnp.concatenate([grad, carried[:, start : start + size]], 0)
            tap = taps[:, start : start + size]
            spread = grad * tap[0:1]
            sums = [jnp.sum(grad * windows[0], axis=0, keepdims=True)]
            for offset in range(1, tap_count):
                masked = long * same_long[:, offset : offset + 1]
                spread = spread + (
                    pltpu.roll(masked, BLOCK + 8 - offset, 0)[:BLOCK] * tap[offset : offset + 1]
                )
                sums.append(jnp.sum(masked[:BLOCK] * windows[offset], axis=0, keepdims=True))
            carried[:, start : start + size] = grad[:8]
            tap_out[:, start : start + size] += jnp.concatenate(sums, 0)
            d_raw[:, start : start + size] = low(spread)
            tail_next[:, start : start + size] = spread[BLOCK - 8 :]

    @pl.when(step == 0)
    def _():
        tail_out[...] = tail_next[...]


def run_backward(
    begin, end, raw, edge, taps, same, beta, cum_col, cum_row, t_part, p_part, s_part, state_in,
    d_out, passed, head_count, substeps, width,
):
    count, columns = raw.shape
    chunks = count // BLOCK
    rows = BLOCK * substeps
    per_halo = BLOCK // HALO
    per_eight = BLOCK // 8
    whole = lambda *shape: pl.BlockSpec(shape, lambda c: (0,) * len(shape))
    tokens = lambda cols: pl.BlockSpec((BLOCK, cols), lambda c: (end - 1 - c, 0))
    square = pl.BlockSpec((1, head_count, width, width), lambda c: (end - 1 - c, 0, 0, 0))
    anywhere = pl.BlockSpec(memory_space=pl.ANY)
    state = (head_count, width, width)
    return pl.pallas_call(
        functools.partial(backward_kernel, head_count, substeps, width, end),
        grid=(end - begin,),
        in_specs=[
            tokens(columns),
            pl.BlockSpec(
                (HALO, columns), lambda c: (jnp.maximum((end - 1 - c) * per_halo - 1, 0), 0)
            ),
            whole(HALO, columns),
            whole(*taps.shape),
            tokens(same.shape[1]),
            pl.BlockSpec(
                (8, same.shape[1]),
                lambda c: (jnp.minimum((end - c) * per_eight, chunks * per_eight - 1), 0),
            ),
            tokens(beta.shape[1]),
            tokens(head_count),
            pl.BlockSpec((1, head_count, rows), lambda c: (end - 1 - c, 0, 0)),
            pl.BlockSpec((1, head_count, rows, rows), lambda c: (end - 1 - c, 0, 0, 0)),
            square,
            square,
            whole(*state),
            tokens(head_count * width),
            whole(*state),
            whole(8, columns),
            whole(*taps.shape),
            anywhere,
            anywhere,
        ],
        out_specs=[
            tokens(columns),
            tokens(head_count * substeps),
            whole(8, columns),
            whole(*state),
            whole(8, columns),
            whole(*taps.shape),
        ],
        out_shape=[
            jax.ShapeDtypeStruct((count, columns), BF16),
            jax.ShapeDtypeStruct((count, head_count * substeps), F32),
            jax.ShapeDtypeStruct((8, columns), F32),
            jax.ShapeDtypeStruct(state, F32),
            jax.ShapeDtypeStruct((8, columns), F32),
            jax.ShapeDtypeStruct(taps.shape, F32),
        ],
        scratch_shapes=[pltpu.VMEM((8, columns), F32)],
        input_output_aliases={17: 0, 18: 1},
        compiler_params=pltpu.CompilerParams(
            dimension_semantics=("arbitrary",), vmem_limit_bytes=48 * 1024 * 1024
        ),
        name="mixer_backward",
    )(
        raw, raw, edge, taps, same, same, beta, cum_col, cum_row, t_part, p_part, s_part,
        state_in, d_out, *passed,
    )


def shift_seq(array, by):
    count = lax.axis_size("seq")
    return lax.ppermute(
        array, "seq", [(i, i + by) for i in range(count) if 0 <= i + by < count]
    )


def swap_seq(array, distance):
    return lax.ppermute(array, "seq", [(i, i ^ distance) for i in range(lax.axis_size("seq"))])


def swap_head(array):
    return lax.ppermute(array, "head", [(0, 1), (1, 0)])


def head_sum(array):
    return array + swap_head(array)


def fine_low(form, former, latter):
    high, rest = split(former)
    return form(high, latter) + form(rest, latter)


def fine_first(form, former, latter):
    high, rest = split(latter)
    return form(former, high) + form(former, rest)


def join_kernel(final, upper, group, other, before, group_out, low_out, before_out):
    heads, width, _ = group.shape

    @pl.when(upper[0] == 1)
    def _():
        for head in range(heads):
            theirs = other[head]
            reach = fine_low(product, before[head, :, :width], theirs)
            before_out[head, :, :width] = reach[:, :width]
            before_out[head, :, width:] = reach[:, width:] + before[head, :, width:]
            if not final:
                mine = fine_low(product, group[head, :, :width], theirs)
                group_out[head, :, :width] = mine[:, :width]
                group_out[head, :, width:] = mine[:, width:] + group[head, :, width:]

    @pl.when(upper[0] == 0)
    def _():
        before_out[...] = before[...]
        if not final:
            for head in range(heads):
                theirs = other[head]
                mine = fine_first(product, theirs[:, :width], group[head])
                group_out[head, :, :width] = mine[:, :width]
                group_out[head, :, width:] = mine[:, width:] + theirs[:, width:].astype(F32)

    low_out[...] = low(group_out[...]) if not final else low(before_out[...])


def join_groups(final, upper, group, other, before):
    whole = pl.BlockSpec(memory_space=pltpu.VMEM)
    full = jax.ShapeDtypeStruct(group.shape, F32)
    return pl.pallas_call(
        functools.partial(join_kernel, final),
        in_specs=[pl.BlockSpec(memory_space=pltpu.SMEM), whole, whole, whole],
        out_specs=[whole, whole, whole],
        out_shape=[full, jax.ShapeDtypeStruct(group.shape, BF16), full],
        name="join_groups",
    )(upper, group, other, before)


def back_kernel(final, upper, group, other, after, group_map, other_map, after_map, *outs):
    group_out, low_out, after_out, after_map_out = outs
    heads, width, _ = group.shape
    after_out[...] = after[...]
    after_map_out[...] = after_map[...]
    if final:
        group_out[...] = group[...]

    @pl.when(upper[0] == 1)
    def _():
        if not final:
            for head in range(heads):
                theirs = other_map[head, :, :width]
                group_out[head] = other[head].astype(F32) + fine_first(
                    inner_rows, theirs, group[head]
                )

    @pl.when(upper[0] == 0)
    def _():
        for head in range(heads):
            theirs = other[head]
            after_out[head] += fine_low(inner_rows, after_map[head], theirs)
            if not final:
                group_out[head] = group[head] + fine_low(
                    inner_rows, group_map[head, :, :width], theirs
                )
                after_map_out[head] = fine_first(
                    product, other_map[head, :, :width], after_map[head]
                )

    low_out[...] = low(group_out[...])


def join_back(final, upper, group, other, after, group_map, other_map, after_map):
    whole = pl.BlockSpec(memory_space=pltpu.VMEM)
    full = jax.ShapeDtypeStruct(group.shape, F32)
    return pl.pallas_call(
        functools.partial(back_kernel, final),
        in_specs=[pl.BlockSpec(memory_space=pltpu.SMEM)] + [whole] * 6,
        out_specs=[whole] * 4,
        out_shape=[full, jax.ShapeDtypeStruct(group.shape, BF16), full, full],
        name="join_back",
    )(upper, group, other, after, group_map, other_map, after_map)


def states_before(group, eye):
    count, mine = lax.axis_size("seq"), lax.axis_index("seq")
    before = jnp.concatenate([eye, jnp.zeros_like(eye)], 2)
    group_low = low(group)
    kept = []
    distance = 1
    while distance < count:
        other = swap_seq(group_low, distance)
        upper = ((mine // distance) % 2).astype(jnp.int32).reshape(1)
        kept.append((group, other, upper))
        final = 2 * distance >= count
        group, group_low, before = join_groups(final, upper, group, other, before)
        distance *= 2
    return group_low[:, :, group.shape[1] :], kept


def adjoints_after(own, kept, eye):
    group, group_low = own, low(own)
    after, after_map = jnp.zeros_like(own), eye
    distance = 1
    for group_map, other_map, upper in kept:
        other = swap_seq(group_low, distance)
        final = 2 * distance >= lax.axis_size("seq")
        group, group_low, after, after_map = join_back(
            final, upper, group, other, after, group_map, other_map, after_map
        )
        distance *= 2
    return after


def bit_orders(count):
    distances = [1 << k for k in range(count.bit_length() - 1)]
    near, far = distances[:3], distances[3:]
    return [near[k:] + near[:k] for k in range(len(near))], far


def scatter_view(array):
    count = lax.axis_size("seq")
    bits = count.bit_length() - 1
    return array.reshape((2,) * bits + (array.shape[0] // count, array.shape[1]))


def scatter_halves(view, distance):
    axis = view.ndim - 2 - distance.bit_length()
    own = (lax.axis_index("seq") // distance) % 2
    keep = lax.dynamic_slice_in_dim(view, own, 1, axis)
    send = lax.dynamic_slice_in_dim(view, 1 - own, 1, axis)
    return keep, low(send)


def swap_all(arrays, distances):
    return [swap_seq(array, distance) for array, distance in zip(arrays, distances)]


def halve_all(views, distances):
    halves = [scatter_halves(view, distance) for view, distance in zip(views, distances)]
    return [half[0] for half in halves], [half[1] for half in halves]


def join_all(keeps, others):
    return [keep.astype(F32) + other.astype(F32) for keep, other in zip(keeps, others)]


def far_steps(views, distances):
    for distance in distances:
        keeps, sends = halve_all(views, [distance] * len(views))
        widths = [send.shape[-1] for send in sends]
        merged = swap_seq(jnp.concatenate(sends, -1), distance)
        others, start = [], 0
        for wide in widths:
            others.append(lax.slice_in_dim(merged, start, start + wide, axis=merged.ndim - 1))
            start += wide
        views = join_all(keeps, others)
    return [view.reshape(view.shape[-2:]) for view in views]


def per_device(
    activations,
    log_decay,
    doc_starts,
    query_weight,
    key_weight,
    value_weight,
    beta_weight,
    gate_weight,
    out_weight,
    query_taps,
    key_taps,
    value_taps,
    mixer_gain,
    head_gain,
    feed_gain,
    feed_gate,
    feed_up,
    feed_down,
    cotangent,
):
    count, features = activations.shape
    tap_count = query_taps.shape[0]
    width = head_gain.shape[0]
    query_cols = query_weight.shape[1]
    key_cols = key_weight.shape[1]
    conv_cols = query_cols + 2 * key_cols
    hidden_cols = feed_gate.shape[1]
    head_count = query_cols // width
    beta_cols = beta_weight.shape[1]
    substeps = beta_cols // head_count
    device_rank = lax.axis_index("seq")
    head_rank = lax.axis_index("head")
    extra = 128
    shard_rows = query_weight.shape[0]
    pad = jnp.zeros((shard_rows, extra - beta_cols - 2), BF16)
    first_pack = jnp.concatenate(
        [
            query_weight,
            key_weight,
            value_weight,
            gate_weight,
            beta_weight,
            mixer_gain[:, None],
            feed_gain[:, None],
            pad,
        ],
        1,
    )
    second_pack = jnp.concatenate([out_weight.T, feed_gate, feed_up, feed_down.T], 1)
    first_full = lax.all_gather(first_pack, "seq", axis=0, tiled=True)
    first_full, second_pack = lax.optimization_barrier((first_full, second_pack))
    second_full = lax.all_gather(second_pack, "seq", axis=0, tiled=True)
    weight_conv = first_full[:, :conv_cols]
    weight_gate = first_full[:, conv_cols : conv_cols + query_cols]
    tail_cols = first_full[:, conv_cols + query_cols :]
    weight_beta = tail_cols[:, :beta_cols]
    gain_one = tail_cols[:, beta_cols].astype(F32)
    gain_two = tail_cols[:, beta_cols + 1].astype(F32)
    weight_out = second_full[:, :query_cols]
    weight_feed = second_full[:, query_cols : query_cols + 2 * hidden_cols]
    weight_down = second_full[:, query_cols + 2 * hidden_cols :]

    token_position = device_rank * count + jnp.arange(count, dtype=jnp.int32)
    is_start = jnp.any(token_position[:, None] == doc_starts[None, :], axis=1)

    def same_docs(position):
        doc = lambda p: jnp.sum((p[:, None] >= doc_starts[None, :]).astype(jnp.int32), axis=1)
        own = doc(position)
        return jnp.stack(
            [
                ((doc(position - offset) == own) & (position >= offset)).astype(F32)
                for offset in range(tap_count)
            ],
            1,
        )

    same = same_docs(token_position)
    log_gate = log_decay - RESET * is_start.astype(F32)[:, None]
    chunks = count // BLOCK
    cumulative = jnp.cumsum(log_gate.reshape(chunks, BLOCK, head_count), axis=1)
    cum_col = cumulative.reshape(count, head_count)
    cum_row = jnp.concatenate([jnp.swapaxes(cumulative, 1, 2)] * substeps, 2)
    taps_all = jnp.concatenate([query_taps, key_taps, value_taps], 1).astype(F32)

    inputs = activations.astype(F32)
    in_scale = lax.rsqrt(jnp.mean(inputs * inputs, axis=-1, keepdims=True) + NORM_EPS)
    normed = low(inputs * in_scale * gain_one)
    raw_all = low(product(normed, weight_conv))
    beta_gate = jax.nn.sigmoid(product(normed, weight_beta))
    gate_view = product(normed, weight_gate)
    edge = shift_seq(raw_all[count - HALO :], 1)
    t_part, p_part, s_part, q_reach, local_out, group = run_forward(
        raw_all, edge, taps_all, same, beta_gate, cum_col, cum_row, head_count, substeps, width
    )
    eye = jnp.broadcast_to(jnp.eye(width, dtype=F32), (head_count, width, width))
    state_low, kept = states_before(group, eye)

    by_head = lambda array: array.reshape(count, head_count, width)
    mixer_out = by_head(local_out) + jnp.einsum(
        "thk,hkv->thv", by_head(q_reach), state_low, preferred_element_type=F32
    )
    head_gain_f = head_gain.astype(F32)
    head_scale = lax.rsqrt(jnp.mean(mixer_out * mixer_out, axis=-1, keepdims=True) + NORM_EPS)
    head_unit = mixer_out * head_scale
    gate_view = by_head(gate_view)
    gate_sigma = jax.nn.sigmoid(gate_view)
    gate_act = gate_view * gate_sigma
    heads_out = low(head_unit * head_gain_f * gate_act).reshape(count, query_cols)
    hidden = inputs + head_sum(times_transposed(heads_out, weight_out))
    feed_scale = lax.rsqrt(jnp.mean(hidden * hidden, axis=-1, keepdims=True) + NORM_EPS)
    normed_ffn = low(hidden * feed_scale * gain_two)
    ffn = product(normed_ffn, weight_feed)
    ffn_gate, ffn_up = ffn[:, :hidden_cols], ffn[:, hidden_cols:]
    ffn_sigma = jax.nn.sigmoid(ffn_gate)
    activation = low(ffn_gate * ffn_sigma * ffn_up)
    branch_two = low(times_transposed(activation, weight_down))
    half = features // lax.axis_size("head")
    own_half = lambda array: lax.dynamic_slice_in_dim(array, head_rank * half, half, 1)
    other_half = lambda array: lax.dynamic_slice_in_dim(array, (1 - head_rank) * half, half, 1)
    output = low(
        own_half(hidden)
        + own_half(branch_two).astype(F32)
        + swap_head(other_half(branch_two)).astype(F32)
    )

    grad_result = cotangent.astype(F32)
    d_activation = product(cotangent, weight_down)
    d_up = low(d_activation * (ffn_gate * ffn_sigma))
    d_gate = low(d_activation * ffn_up * silu_slope(ffn_gate, ffn_sigma))
    orders, far = bit_orders(lax.axis_size("seq"))
    at_step = lambda k: [order[k] for order in orders]
    feed_keeps, feed_sends = halve_all(
        [
            scatter_view(inner_rows(normed_ffn, d_gate)),
            scatter_view(inner_rows(normed_ffn, d_up)),
            scatter_view(inner_rows(cotangent, activation)),
        ],
        at_step(0),
    )
    d_gate, d_up, feed_sends = lax.optimization_barrier((d_gate, d_up, feed_sends))
    feed_others = swap_all(feed_sends, at_step(0))
    d_ffn = jnp.concatenate([d_gate, d_up], 1)
    d_normed_ffn = head_sum(times_transposed(d_ffn, weight_feed))
    d_hidden_norm, feed_terms = norm_back(hidden, gain_two, d_normed_ffn)
    grad_feed_gain = jnp.sum(feed_terms, axis=0)
    d_hidden = grad_result + d_hidden_norm
    grad_mixer = low(d_hidden)
    d_heads = by_head(product(grad_mixer, weight_out))
    d_gate_logit = low(
        d_heads * head_unit * head_gain_f * silu_slope(gate_view, gate_sigma)
    ).reshape(count, query_cols)
    d_mixer_out, head_terms = norm_back(mixer_out, head_gain_f, d_heads * gate_act)
    head_gain_part = jnp.sum(head_terms, axis=(0, 1))
    d_mixer_low = low(d_mixer_out)
    own_part = jnp.einsum("thk,thv->hkv", by_head(q_reach), d_mixer_low, preferred_element_type=F32)
    adjoint = adjoints_after(own_part, kept, eye)

    side_views = [
        scatter_view(inner_rows(grad_mixer, heads_out)),
        scatter_view(inner_rows(normed, d_gate_logit)),
    ]
    chunks_at = [chunks - (chunks * k) // BACK_CALLS for k in range(BACK_CALLS + 1)]
    adjoint, feed_others = lax.optimization_barrier((adjoint, feed_others))
    feed_views = join_all(feed_keeps, feed_others)
    passed = (
        adjoint,
        jnp.zeros((8, conv_cols), F32),
        jnp.zeros((tap_count, conv_cols), F32),
        jnp.zeros((count, conv_cols), BF16),
        jnp.zeros((count, beta_cols), F32),
    )
    for call in range(BACK_CALLS):
        distances = (at_step(call + 1) if call < 2 else []) + at_step(call)[:2]
        last = call == BACK_CALLS - 1
        views = side_views if last else feed_views + side_views
        keeps, sends = halve_all(views, distances)
        first_passed, sends = lax.optimization_barrier((passed[0], sends))
        others = swap_all(sends, distances)
        if last:
            feed_sums = far_steps(feed_views, far)
        d_raw, d_beta_logit, new_tail, *carried = run_backward(
            chunks_at[call + 1], chunks_at[call],
            raw_all, edge, taps_all, same, beta_gate, cum_col, cum_row, t_part, p_part, s_part,
            state_low, d_mixer_low.reshape(count, query_cols), (first_passed,) + passed[1:],
            head_count, substeps, width,
        )
        if call == 0:
            tail = new_tail
        carried[0], others = lax.optimization_barrier((carried[0], others))
        passed = (*carried, d_raw, d_beta_logit)
        joined = join_all(keeps, others)
        if not last:
            feed_views = joined[:3]
        side_views = joined[-2:]
    first_rows, tap_grads = carried[1], carried[2]
    returned = shift_seq(first_rows, -1)
    same_after = same_docs(token_position[-1] + 1 + jnp.arange(8, dtype=jnp.int32))
    spread = jnp.zeros_like(tail)
    for offset in range(1, tap_count):
        masked = returned * same_after[:, offset : offset + 1] * taps_all[offset]
        spread = spread + jnp.pad(masked[:offset], ((8 - offset, 0), (0, 0)))
    d_raw = lax.dynamic_update_slice(d_raw, low(tail + spread), (count - 8, 0))
    d_beta_low = low(d_beta_logit)
    each = -(-conv_cols // (len(orders) * width)) * width
    keeps, sends = halve_all(
        [
            scatter_view(inner_rows(normed, d_raw[:, k * each : (k + 1) * each]))
            for k in range(len(orders))
        ],
        at_step(0),
    )
    d_raw, d_beta_low, sends = lax.optimization_barrier((d_raw, d_beta_low, sends))
    others = swap_all(sends, at_step(0))
    grad_beta = inner_rows(normed, d_beta_low)
    d_normed_part = times_transposed(d_raw, weight_conv) + (
        times_transposed(d_beta_low, weight_beta) + times_transposed(d_gate_logit, weight_gate)
    )
    d_normed = head_sum(low(d_normed_part).astype(F32))
    d_input_norm, mixer_terms = norm_back(inputs, gain_one, d_normed)
    grad_mixer_gain = jnp.sum(mixer_terms, axis=0)
    small = jnp.concatenate(
        [
            grad_beta.T.reshape(-1),
            grad_mixer_gain,
            grad_feed_gain,
            tap_grads.reshape(-1),
            head_gain_part + swap_head(head_gain_part),
        ]
    )
    small = jnp.pad(small, (0, -small.shape[0] % 1024)).reshape(-1, 128)
    small, d_input_norm, others = lax.optimization_barrier((small, d_input_norm, others))
    grad_input = own_half(d_hidden + d_input_norm)
    near = orders[0]
    for at in (1, 2):
        keeps, sends = halve_all(join_all(keeps, others), at_step(at))
        small, sends = lax.optimization_barrier((small, sends))
        others = swap_all(sends, at_step(at))
        small = small + swap_seq(small, near[at - 1])
        small, others = lax.optimization_barrier((small, others))
    conv_views = join_all(keeps, others)
    *conv_sums, side_out, side_gate = far_steps(conv_views + side_views, far)
    conv_sum = jnp.concatenate(conv_sums, 1)
    for distance in near[2:] + far:
        small = small + swap_seq(small, distance)
    small = small.reshape(-1)
    ends, at = [], 0
    for size in (beta_cols * features, features, features, tap_count * conv_cols, width):
        ends.append(small[at : at + size])
        at += size
    own_rows = lambda vector: lax.dynamic_slice_in_dim(
        vector, device_rank * shard_rows, shard_rows, vector.ndim - 1
    )
    tap_total = ends[3].reshape(tap_count, conv_cols)
    cut = lambda array, start, size: array[:, start : start + size]
    return (
        output,
        grad_input,
        cut(conv_sum, 0, query_cols),
        cut(conv_sum, query_cols, key_cols),
        cut(conv_sum, query_cols + key_cols, key_cols),
        own_rows(ends[0].reshape(beta_cols, features)).T,
        side_gate,
        side_out.T,
        cut(tap_total, 0, query_cols),
        cut(tap_total, query_cols, key_cols),
        cut(tap_total, query_cols + key_cols, key_cols),
        own_rows(ends[1]),
        ends[4],
        own_rows(ends[2]),
        feed_sums[0],
        feed_sums[1],
        feed_sums[2].T,
    )


def solution(mesh):
    in_specs = (
        P("seq", None),
        P("seq", "head"),
        P(),
        P("seq", "head"),
        P("seq", "head"),
        P("seq", "head"),
        P("seq", "head"),
        P("seq", "head"),
        P("head", "seq"),
        P(None, "head"),
        P(None, "head"),
        P(None, "head"),
        P("seq"),
        P(),
        P("seq"),
        P("seq", "head"),
        P("seq", "head"),
        P("head", "seq"),
        P("seq", None),
    )
    out_specs = (
        P("seq", "head"),
        P("seq", "head"),
        P("seq", "head"),
        P("seq", "head"),
        P("seq", "head"),
        P("seq", "head"),
        P("seq", "head"),
        P("head", "seq"),
        P(None, "head"),
        P(None, "head"),
        P(None, "head"),
        P("seq"),
        P(),
        P("seq"),
        P("seq", "head"),
        P("seq", "head"),
        P("head", "seq"),
    )
    return jax.shard_map(
        per_device, mesh=mesh, in_specs=in_specs, out_specs=out_specs, check_vma=False
    )
```

```python
import functools

import jax
import jax.numpy as jnp
from jax import lax
from jax.experimental import pallas as pl
from jax.experimental.pallas import tpu as pltpu
from jax.sharding import PartitionSpec as P

BLOCK = 64
RESET = 256.0
HALO = 16
VMEM_BYTES = 63 * 1024 * 1024
PAIR = 2
QUERY_CHUNKS = 2
TILE = 256
AHEAD_CALLS = 3
NORM_EPS = 1e-05
UNIT_EPS = 1e-06
F32 = jnp.float32
BF16 = jnp.bfloat16


def product(former, latter):
    return jnp.dot(former, latter, preferred_element_type=F32)


def inner_rows(former, latter):
    return lax.dot_general(former, latter, (((0,), (0,)), ((), ())), preferred_element_type=F32)


def times_transposed(former, latter):
    return lax.dot_general(former, latter, (((1,), (1,)), ((), ())), preferred_element_type=F32)


def low(values):
    return values.astype(BF16)


def split(values):
    high = values.astype(BF16)
    return high, (values - high.astype(F32)).astype(BF16)


def fine(form, former, latter):
    a_high, a_low = split(former)
    b_high, b_low = split(latter)
    return form(a_high, b_high) + (form(a_low, b_high) + form(a_high, b_low))


def silu_slope(values, sigma):
    return sigma * (1.0 + values * (1.0 - sigma))


def norm_back(values, gain_vector, gradient):
    row_scale = lax.rsqrt(jnp.mean(values * values, axis=-1, keepdims=True) + NORM_EPS)
    unit_value = values * row_scale
    scaled_grad = gradient * gain_vector
    back_value = row_scale * (
        scaled_grad - unit_value * jnp.mean(scaled_grad * unit_value, axis=-1, keepdims=True)
    )
    return (back_value, gradient * unit_value)


def row_maps(rows):
    row = lax.broadcasted_iota(jnp.int32, (rows, rows), 0)
    col = lax.broadcasted_iota(jnp.int32, (rows, rows), 1)
    return row % BLOCK, col % BLOCK, row // BLOCK, col // BLOCK


def lower_inverses(systems, apart):
    rows = systems[0].shape[0]
    row = lax.broadcasted_iota(jnp.int32, (rows, rows), 0)
    col = lax.broadcasted_iota(jnp.int32, (rows, rows), 1)
    eye = jnp.where(row == col, 1.0, 0.0)
    inverses = [eye - jnp.where(apart == 0, system, 0.0) for system in systems]
    level = 0
    while (1 << level) < BLOCK:
        joins = (apart >> level) == 1
        joints = [low(jnp.where(joins, system, 0.0)) for system in systems]
        lows = [low(inverse) for inverse in inverses]
        halves = [low(product(a, b)) for a, b in zip(lows, joints)]
        inverses = [c - product(a, b) for a, b, c in zip(halves, lows, inverses)]
        level += 1
    return inverses


def conv_rows(tile, halo, taps, same):
    count = tile.shape[0]
    extended = jnp.concatenate([halo, tile], 0)
    windows = [tile] + [
        pltpu.roll(extended, offset, 0)[8:] for offset in range(1, taps.shape[0])
    ]
    outcome = tile * taps[0:1]
    for offset in range(1, taps.shape[0]):
        outcome = outcome + windows[offset] * taps[offset : offset + 1] * same[:, offset : offset + 1]
    return outcome, windows


def unit_scale(values):
    return lax.rsqrt(jnp.sum(values * values, axis=-1, keepdims=True) + UNIT_EPS)


def pieces_of(head, head_count, substeps, width):
    query = [(head * width, width)]
    keys = [((head_count + head * substeps + n) * width, width) for n in range(substeps)]
    values = [
        ((head_count + (head_count + head) * substeps + n) * width, width) for n in range(substeps)
    ]
    return query + keys + values


def conv_of(source, first, start, size, taps, same_rows):
    tile_ref, before, edge, offset = source
    columns = slice(start - offset, start - offset + size)
    halo = jnp.where(first, edge[:, columns], before[:, columns]).astype(F32)[HALO - 8 :]
    return conv_rows(
        tile_ref[:, columns].astype(F32), halo, taps[:, start : start + size], same_rows
    )


def beta_rows(beta, head, substeps):
    columns = [beta[:, head * substeps + n : head * substeps + n + 1] for n in range(substeps)]
    return jnp.concatenate(columns, 0)


def forward_kernel(
    head_count, substeps, width, begin,
    raw, before, edge, taps, same, beta, cum_col, cum_row, chain_in, *refs,
):
    t_out, p_out, s_out, key_out, solved_out, chain = refs[-6:]
    step = pl.program_id(0)
    first = step + begin == 0
    rows = BLOCK * substeps
    row_token, col_token, row_step, col_step = row_maps(rows)
    upto = col_token <= row_token
    earlier = (col_token < row_token) | ((col_token == row_token) & (col_step < row_step))
    apart = row_token ^ col_token
    eye = jnp.where(
        lax.broadcasted_iota(jnp.int32, (width, width), 0)
        == lax.broadcasted_iota(jnp.int32, (width, width), 1),
        1.0,
        0.0,
    )
    same_rows = same[...]

    @pl.when(step == 0)
    def _():
        chain[...] = chain_in[...]

    heads = range(head_count)
    offset = head_count * width
    source = (raw, before, edge, offset)
    units = [(j, h) for j in range(PAIR) for h in heads]
    rows_at = [slice(j * BLOCK, (j + 1) * BLOCK) for j in range(PAIR)]
    keys, values, betas = {}, {}, {}
    for head in heads:
        acts = []
        for start, size in pieces_of(head, head_count, substeps, width)[1:]:
            pre, _ = conv_of(source, first, start, size, taps, same_rows)
            acts.append(pre * jax.nn.sigmoid(pre))
        acts = [a * unit_scale(a) for a in acts[:substeps]] + acts[substeps:]
        acts = [low(a) for a in acts]
        for j, at in enumerate(rows_at):
            keys[j, head] = jnp.concatenate([a[at] for a in acts[:substeps]], 0)
            values[j, head] = jnp.concatenate([a[at] for a in acts[substeps:]], 0)
            betas[j, head] = beta_rows(beta[at], head, substeps)
    keys, values, betas = ([held[u] for u in units] for held in (keys, values, betas))
    cum_rows = [jnp.concatenate([cum_col[rows_at[j], h : h + 1]] * substeps, 0) for j, h in units]
    cum_cols = [cum_row[j, h : h + 1, :] for j, h in units]
    lasts = [c[:, BLOCK - 1 : BLOCK] for c in cum_cols]
    ratios = [jnp.exp(jnp.where(upto, a - b, -1e4)) for a, b in zip(cum_rows, cum_cols)]
    grams = [times_transposed(key, key) for key in keys]
    systems = [
        jnp.where(earlier, beta_col * ratio * gram, 0.0)
        for beta_col, ratio, gram in zip(betas, ratios, grams)
    ]
    inverses = [low(inverse) for inverse in lower_inverses(systems, apart)]
    rights = [
        jnp.concatenate(
            [
                low(beta_col * jnp.exp(cum) * key.astype(F32)),
                low(beta_col * value.astype(F32)),
            ],
            1,
        )
        for beta_col, cum, key, value in zip(betas, cum_rows, keys, values)
    ]
    solved = [low(product(inverse, right)) for inverse, right in zip(inverses, rights)]
    ends = [
        low(jnp.exp(last - cum) * key.astype(F32))
        for last, cum, key in zip(lasts, cum_rows, keys)
    ]
    moved = [inner_rows(end, both) for end, both in zip(ends, solved)]
    step_maps = [split(jnp.exp(last) * eye - move[:, :width]) for last, move in zip(lasts, moved)]
    chains = [chain[head] for head in heads]
    for at, (j, head) in enumerate(units):
        t_out[j, head] = inverses[at]
        key_out[j, head] = keys[at]
        solved_out[j, head] = solved[at]
    for j in range(PAIR):
        at = j * head_count
        splits = [split(chained) for chained in chains]
        for head in heads:
            p_out[j, head] = splits[head][0][:, :width]
            s_out[j, head] = splits[head][0][:, width:]
        chains = [
            product(step_maps[at + h][0], splits[h][0])
            + (product(step_maps[at + h][1], splits[h][0]) + product(step_maps[at + h][0], splits[h][1]))
            for h in heads
        ]
        chains = [
            jnp.concatenate([c[:, :width], c[:, width:] + moved[at + h][:, width:]], 1)
            for h, c in enumerate(chains)
        ]
    for head in heads:
        chain[head] = chains[head]


def whole_spec(*shape):
    return pl.BlockSpec(shape, lambda *c: (0,) * len(shape))


def run_forward(
    begin, end, raw, edge, taps, same, beta, cum_col, cum_row, chain, passed,
    head_count, substeps, width,
):
    count, columns = raw.shape
    chunks = count // BLOCK
    rows = BLOCK * substeps
    begin, end = begin // PAIR, end // PAIR
    per_halo = PAIR * BLOCK // HALO
    tokens = lambda cols: pl.BlockSpec((PAIR * BLOCK, cols), lambda c: (c + begin, 0))
    tiles = lambda *shape: pl.BlockSpec((PAIR, head_count) + shape, lambda c: (c + begin, 0, 0, 0))
    shapes = [(rows, rows), (width, width), (width, width), (rows, width), (rows, 2 * width)]
    anywhere = pl.BlockSpec(memory_space=pl.ANY)
    return pl.pallas_call(
        functools.partial(forward_kernel, head_count, substeps, width, begin),
        grid=(end - begin,),
        in_specs=[
            tokens(columns),
            pl.BlockSpec(
                (HALO, columns), lambda c: (jnp.maximum((c + begin) * per_halo - 1, 0), 0)
            ),
            whole_spec(HALO, columns),
            whole_spec(*taps.shape),
            tokens(same.shape[1]),
            tokens(beta.shape[1]),
            tokens(head_count),
            pl.BlockSpec((PAIR, head_count, rows), lambda c: (c + begin, 0, 0)),
            whole_spec(*chain.shape),
        ]
        + [anywhere] * len(passed),
        out_specs=[tiles(*shape) for shape in shapes] + [whole_spec(*chain.shape)],
        out_shape=[
            jax.ShapeDtypeStruct((chunks, head_count) + shape, BF16) for shape in shapes
        ]
        + [jax.ShapeDtypeStruct(chain.shape, F32)],
        input_output_aliases={9 + k: k for k in range(len(passed))},
        compiler_params=pltpu.CompilerParams(
            dimension_semantics=("arbitrary",), vmem_limit_bytes=VMEM_BYTES
        ),
        name="mixer_forward",
    )(raw, raw, edge, taps, same, beta, cum_col, cum_row, chain, *passed)


def query_kernel(
    head_count, substeps, width,
    raw, before, edge, taps, same, cum_col, cum_row, key_in, solved_in, p_in, s_in,
    qtil_out, local_out,
):
    first = pl.program_id(0) == 0
    rows = BLOCK * substeps
    row_token, col_token, _, _ = row_maps(rows)
    upto = (col_token <= row_token)[:BLOCK]
    same_rows = same[...]
    heads = range(head_count)
    units = [(j, h) for j in range(QUERY_CHUNKS) for h in heads]
    rows_at = [slice(j * BLOCK, (j + 1) * BLOCK) for j in range(QUERY_CHUNKS)]
    queries = []
    for head in heads:
        start, size = pieces_of(head, head_count, substeps, width)[0]
        pre, _ = conv_of((raw, before, edge, 0), first, start, size, taps, same_rows)
        act = pre * jax.nn.sigmoid(pre)
        queries.append(low(act * unit_scale(act) * width ** (-0.5)))
    queries = [queries[h][rows_at[j]] for j, h in units]
    cum_rows = [cum_col[rows_at[j], h : h + 1] for j, h in units]
    ratios = [
        jnp.exp(jnp.where(upto, cum - cum_row[j, h : h + 1, :], -1e4))
        for cum, (j, h) in zip(cum_rows, units)
    ]
    scores = [times_transposed(query, key_in[j, h]) for query, (j, h) in zip(queries, units)]
    seen = [
        product(low(ratio * score), solved_in[j, h])
        for ratio, score, (j, h) in zip(ratios, scores, units)
    ]
    effective = [
        low(jnp.exp(cum) * query.astype(F32) - see[:, :width])
        for cum, query, see in zip(cum_rows, queries, seen)
    ]
    reached = [
        (product(eff, p_in[j, h]), product(eff, s_in[j, h]))
        for eff, (j, h) in zip(effective, units)
    ]
    for k, (j, h) in enumerate(units):
        at = slice(h * width, (h + 1) * width)
        qtil_out[rows_at[j], at] = low(reached[k][0])
        local_out[rows_at[j], at] = reached[k][1] + seen[k][:, width:]


def run_query(
    raw, edge, taps, same, cum_col, cum_row, key_rows, solved, p_part, s_part,
    head_count, substeps, width,
):
    count, columns = raw.shape
    chunks = count // BLOCK
    rows = BLOCK * substeps
    per_halo = QUERY_CHUNKS * BLOCK // HALO
    tokens = lambda cols: pl.BlockSpec((QUERY_CHUNKS * BLOCK, cols), lambda c: (c, 0))
    tiles = lambda *shape: pl.BlockSpec((QUERY_CHUNKS, head_count) + shape, lambda c: (c, 0, 0, 0))
    return pl.pallas_call(
        functools.partial(query_kernel, head_count, substeps, width),
        grid=(chunks // QUERY_CHUNKS,),
        in_specs=[
            tokens(columns),
            pl.BlockSpec((HALO, columns), lambda c: (jnp.maximum(c * per_halo - 1, 0), 0)),
            whole_spec(HALO, columns),
            whole_spec(*taps.shape),
            tokens(same.shape[1]),
            tokens(head_count),
            pl.BlockSpec((QUERY_CHUNKS, head_count, rows), lambda c: (c, 0, 0)),
            tiles(rows, width),
            tiles(rows, 2 * width),
            tiles(width, width),
            tiles(width, width),
        ],
        out_specs=[tokens(columns), tokens(columns)],
        out_shape=[
            jax.ShapeDtypeStruct((count, columns), BF16),
            jax.ShapeDtypeStruct((count, columns), F32),
        ],
        compiler_params=pltpu.CompilerParams(
            dimension_semantics=("arbitrary",), vmem_limit_bytes=VMEM_BYTES
        ),
        name="mixer_query",
    )(raw, raw, edge, taps, same, cum_col, cum_row, key_rows, solved, p_part, s_part)


def backward_kernel(
    head_count, substeps, width, end,
    raw_q, before_q, edge_q, raw, before, edge, taps, same, same_next, beta, cum_col, cum_row,
    t_in, p_in, s_in, state_in, d_out, adjoint_in, carried_in, tap_in, *refs,
):
    d_raw, d_logit, tail_out, adjoint, carried, tap_out, tail_next = refs[-7:]
    step = pl.program_id(0)
    pair = end - 1 - step
    rows = BLOCK * substeps
    tap_count = taps.shape[0]
    count = PAIR * BLOCK
    row_token, col_token, row_step, col_step = row_maps(rows)
    upto = col_token <= row_token
    earlier = (col_token < row_token) | ((col_token == row_token) & (col_step < row_step))
    same_rows = same[...]
    same_long = jnp.concatenate([same_rows, same_next[...]], 0)

    @pl.when(step == 0)
    def _():
        adjoint[...] = adjoint_in[...]
        carried[...] = carried_in[...]
        tap_out[...] = tap_in[...]

    heads = range(head_count)
    units_at = [(j, h) for j in range(PAIR) for h in heads]
    rows_at = [slice(j * BLOCK, (j + 1) * BLOCK) for j in range(PAIR)]
    pieces = [pieces_of(head, head_count, substeps, width) for head in heads]
    pres, sigmas, scales, units = [], [], [], []
    queries, keys, values, betas = {}, {}, {}, {}
    key_start = head_count * width
    sources = [(raw_q, before_q, edge_q, 0), (raw, before, edge, key_start)]

    def windows_of(start, size):
        return conv_of(sources[int(start >= key_start)], pair == 0, start, size, taps, same_rows)

    for head in heads:
        pre = [windows_of(start, size)[0] for start, size in pieces[head]]
        sigma = [jax.nn.sigmoid(p) for p in pre]
        acts = [p * s for p, s in zip(pre, sigma)]
        pres.append(pre)
        sigmas.append(sigma)
        scales.append([unit_scale(a) for a in acts[: 1 + substeps]])
        units.append([a * s for a, s in zip(acts[: 1 + substeps], scales[head])])
        query = low(units[head][0] * width ** (-0.5))
        key = [low(unit) for unit in units[head][1:]]
        value = [low(act) for act in acts[1 + substeps :]]
        for j, at in enumerate(rows_at):
            queries[j, head] = query[at]
            keys[j, head] = jnp.concatenate([k[at] for k in key], 0)
            values[j, head] = jnp.concatenate([v[at] for v in value], 0)
            betas[j, head] = beta_rows(beta[at], head, substeps)
    queries, keys, values, betas = (
        [held[u] for u in units_at] for held in (queries, keys, values, betas)
    )
    cum_rows = [
        jnp.concatenate([cum_col[rows_at[j], h : h + 1]] * substeps, 0) for j, h in units_at
    ]
    cum_cols = [cum_row[j, h : h + 1, :] for j, h in units_at]
    lasts = [c[:, BLOCK - 1 : BLOCK] for c in cum_cols]
    ratios = [jnp.exp(jnp.where(upto, a - b, -1e4)) for a, b in zip(cum_rows, cum_cols)]
    carries = [jnp.exp(c) for c in cum_rows]
    end_ratios = [jnp.exp(last - c) for last, c in zip(lasts, cum_rows)]
    inverses = [t_in[j, h] for j, h in units_at]
    d_mixes = [d_out[rows_at[j], h * width : (h + 1) * width] for j, h in units_at]
    states = [
        low(s_in[j, h].astype(F32) + product(p_in[j, h], state_in[h])) for j, h in units_at
    ]
    stacks = [jnp.concatenate([query, key], 0) for query, key in zip(queries, keys)]
    both_grams = [times_transposed(stack, key) for stack, key in zip(stacks, keys)]
    grams = [both[BLOCK:] for both in both_grams]
    masks = [low(ratio[:BLOCK] * both[:BLOCK]) for ratio, both in zip(ratios, both_grams)]
    d_both = [
        inner_rows(
            jnp.concatenate([mask, low(carry[:BLOCK] * query.astype(F32))], 1), d_mix
        )
        for mask, carry, query, d_mix in zip(masks, carries, queries, d_mixes)
    ]
    d_seen = [both[:rows] for both in d_both]
    d_reach = [both[rows:] for both in d_both]
    end_keys = [low(end * key.astype(F32)) for end, key in zip(end_ratios, keys)]
    start_keys = [
        low((beta_col * carry) * key.astype(F32))
        for beta_col, carry, key in zip(betas, carries, keys)
    ]
    freshes = [
        value.astype(F32) - carry * product(key, state)
        for value, carry, key, state in zip(values, carries, keys, states)
    ]
    updates = [
        low(product(inverse, low(beta_col * fresh)))
        for inverse, beta_col, fresh in zip(inverses, betas, freshes)
    ]
    laters_low, d_rights, d_rights_low = {}, {}, {}
    for j in range(PAIR - 1, -1, -1):
        ids = [j * head_count + h for h in heads]
        laters = [adjoint[h] for h in heads]
        for h, at in enumerate(ids):
            laters_low[at] = low(laters[h])
        d_updates = [low(d_seen[at] + product(end_keys[at], laters_low[at])) for at in ids]
        for h, at in enumerate(ids):
            d_rights[at] = inner_rows(inverses[at], d_updates[h])
            d_rights_low[at] = low(d_rights[at])
        for h, at in enumerate(ids):
            adjoint[h] = (
                jnp.exp(lasts[at]) * laters[h]
                + d_reach[at]
                - inner_rows(start_keys[at], d_rights_low[at])
            )
    ids = range(len(units_at))
    outer = [jnp.concatenate([d_mixes[at], d_rights_low[at]], 0) for at in ids]
    by_update = [times_transposed(outer[at], updates[at]) for at in ids]
    by_state = [times_transposed(outer[at], states[at]) for at in ids]
    d_systems = [
        jnp.where(earlier, -by_update[at][BLOCK:] * ratios[at], 0.0) for at in ids
    ]
    d_scores = [by_update[at][:BLOCK] * ratios[at][:BLOCK] for at in ids]
    d_grams = [betas[at] * d_systems[at] for at in ids]
    d_scores = [low(d_score) for d_score in d_scores]
    d_grams = [low(d_gram + jnp.transpose(d_gram)) for d_gram in d_grams]
    d_betas = [
        jnp.sum(d_rights[at] * freshes[at], axis=-1, keepdims=True)
        + jnp.sum(d_systems[at] * grams[at], axis=-1, keepdims=True)
        for at in ids
    ]
    d_queries = [
        carries[at][:BLOCK] * by_state[at][:BLOCK] + product(d_scores[at], keys[at])
        for at in ids
    ]
    d_keys = [
        inner_rows(jnp.concatenate([d_scores[at], d_grams[at]], 0), stacks[at])
        + end_ratios[at] * times_transposed(updates[at], laters_low[at])
        - (betas[at] * carries[at]) * by_state[at][BLOCK:]
        for at in ids
    ]
    for j in range(PAIR):
        logit_cols = []
        for h in heads:
            at = j * head_count + h
            logits = d_betas[at] * betas[at] * (1.0 - betas[at])
            logit_cols += [logits[n * BLOCK : (n + 1) * BLOCK] for n in range(substeps)]
        d_logit[rows_at[j], :] = jnp.concatenate(logit_cols, 1)

    for head in heads:
        mine = [j * head_count + head for j in range(PAIR)]
        step_rows = lambda arrays, n: jnp.concatenate(
            [array[n * BLOCK : (n + 1) * BLOCK] for array in arrays], 0
        )
        d_value = [betas[at] * d_rights[at] for at in mine]
        grads = [width ** (-0.5) * jnp.concatenate([d_queries[at] for at in mine], 0)]
        grads += [step_rows([d_keys[at] for at in mine], n) for n in range(substeps)]
        grads += [step_rows(d_value, n) for n in range(substeps)]
        for at, (start, size) in enumerate(pieces[head]):
            grad = grads[at]
            if at <= substeps:
                unit = units[head][at]
                grad = scales[head][at] * (
                    grad - unit * jnp.sum(grad * unit, axis=-1, keepdims=True)
                )
            grad = grad * silu_slope(pres[head][at], sigmas[head][at])
            windows = windows_of(start, size)[1]
            long = jnp.concatenate([grad, carried[:, start : start + size]], 0)
            tap = taps[:, start : start + size]
            spread = grad * tap[0:1]
            sums = [jnp.sum(grad * windows[0], axis=0, keepdims=True)]
            for offset in range(1, tap_count):
                masked = long * same_long[:, offset : offset + 1]
                spread = spread + (
                    pltpu.roll(masked, count + 8 - offset, 0)[:count] * tap[offset : offset + 1]
                )
                sums.append(jnp.sum(masked[:count] * windows[offset], axis=0, keepdims=True))
            carried[:, start : start + size] = grad[:8]
            tap_out[:, start : start + size] += jnp.concatenate(sums, 0)
            d_raw[:, start : start + size] = low(spread)
            tail_next[:, start : start + size] = spread[count - 8 :]

    @pl.when(step == 0)
    def _():
        tail_out[...] = tail_next[...]


def run_backward(
    begin, end, raw_q, edge_q, raw, edge, taps, same, beta, cum_col, cum_row, t_part, p_part,
    s_part, state_in, d_out, adjoint, carried, tap_grads, passed, head_count, substeps, width,
):
    count = raw.shape[0]
    columns = taps.shape[1]
    chunks = count // BLOCK
    rows = BLOCK * substeps
    begin, end, chunks = begin // PAIR, end // PAIR, chunks // PAIR
    per_halo = PAIR * BLOCK // HALO
    per_eight = PAIR * BLOCK // 8
    tokens = lambda cols: pl.BlockSpec((PAIR * BLOCK, cols), lambda c: (end - 1 - c, 0))
    halo = lambda cols: pl.BlockSpec(
        (HALO, cols), lambda c: (jnp.maximum((end - 1 - c) * per_halo - 1, 0), 0)
    )
    tiles = lambda *shape: pl.BlockSpec((PAIR, head_count) + shape, lambda c: (end - 1 - c, 0, 0, 0))
    anywhere = pl.BlockSpec(memory_space=pl.ANY)
    state = (head_count, width, width)
    sources = []
    for array in (raw_q, raw):
        cols = array.shape[1]
        sources += [tokens(cols), halo(cols), whole_spec(HALO, cols)]
    return pl.pallas_call(
        functools.partial(backward_kernel, head_count, substeps, width, end),
        grid=(end - begin,),
        in_specs=sources
        + [
            whole_spec(*taps.shape),
            tokens(same.shape[1]),
            pl.BlockSpec(
                (8, same.shape[1]),
                lambda c: (jnp.minimum((end - c) * per_eight, chunks * per_eight - 1), 0),
            ),
            tokens(beta.shape[1]),
            tokens(head_count),
            pl.BlockSpec((PAIR, head_count, rows), lambda c: (end - 1 - c, 0, 0)),
            tiles(rows, rows),
            tiles(width, width),
            tiles(width, width),
            whole_spec(*state),
            tokens(head_count * width),
            whole_spec(*state),
            whole_spec(8, columns),
            whole_spec(*taps.shape),
        ]
        + [anywhere] * len(passed),
        out_specs=[
            tokens(columns),
            tokens(head_count * substeps),
            whole_spec(8, columns),
            whole_spec(*state),
            whole_spec(8, columns),
            whole_spec(*taps.shape),
        ],
        out_shape=[
            jax.ShapeDtypeStruct((count, columns), BF16),
            jax.ShapeDtypeStruct((count, head_count * substeps), F32),
            jax.ShapeDtypeStruct((8, columns), F32),
            jax.ShapeDtypeStruct(state, F32),
            jax.ShapeDtypeStruct((8, columns), F32),
            jax.ShapeDtypeStruct(taps.shape, F32),
        ],
        scratch_shapes=[pltpu.VMEM((8, columns), F32)],
        input_output_aliases={20 + k: k for k in range(len(passed))},
        compiler_params=pltpu.CompilerParams(
            dimension_semantics=("arbitrary",), vmem_limit_bytes=VMEM_BYTES
        ),
        name="mixer_backward",
    )(
        raw_q, raw_q, edge_q, raw, raw, edge, taps, same, same, beta, cum_col, cum_row,
        t_part, p_part, s_part, state_in, d_out, adjoint, carried, tap_grads, *passed,
    )


def row_scale_of(values):
    return lax.rsqrt(jnp.mean(values * values, axis=-1, keepdims=True) + NORM_EPS)


def project_kernel(parts, raw_cols, inputs, edge, gain, *refs):
    weights, outs = refs[:parts], refs[parts:]
    normed_out, edge_normed, raw_out, edge_out, extra_out = outs
    gain_row = gain[...]

    def rows_of(values):
        values = values.astype(F32)
        return low(values * row_scale_of(values) * gain_row)

    def fill(normed, raw_ref, extra_ref):
        at = 0
        for weight in weights:
            cols = weight.shape[1]
            both = product(normed, weight[...])
            raw_part = min(cols, raw_cols - at)
            raw_ref[:, at : at + raw_part] = low(both[:, :raw_part])
            if extra_ref is not None and raw_part < cols:
                extra_ref[...] = jax.nn.sigmoid(both[:, raw_part:])
            at += cols

    normed = rows_of(inputs[...])
    normed_out[...] = normed
    fill(normed, raw_out, extra_out)

    @pl.when(pl.program_id(0) == 0)
    def _():
        normed_edge = rows_of(edge[...])
        edge_normed[...] = normed_edge
        fill(normed_edge, edge_out, None)


def once(shape):
    return pl.BlockSpec(shape, lambda *c: (0,) * len(shape), pipeline_mode=pl.Buffered(1))


def run_project(inputs, edge, gain, weights, raw_cols, extra):
    count, features = inputs.shape
    tile = min(TILE, count)
    tokens = lambda cols: pl.BlockSpec((tile, cols), lambda c: (c, 0))
    return pl.pallas_call(
        functools.partial(project_kernel, len(weights), raw_cols),
        grid=(count // tile,),
        in_specs=[tokens(features), whole_spec(HALO, features), whole_spec(1, features)]
        + [once(weight.shape) for weight in weights],
        out_specs=[
            tokens(features), whole_spec(HALO, features), tokens(raw_cols),
            whole_spec(HALO, raw_cols), tokens(extra),
        ],
        out_shape=[
            jax.ShapeDtypeStruct((count, features), BF16),
            jax.ShapeDtypeStruct((HALO, features), BF16),
            jax.ShapeDtypeStruct((count, raw_cols), BF16),
            jax.ShapeDtypeStruct((HALO, raw_cols), BF16),
            jax.ShapeDtypeStruct((count, extra), F32),
        ],
        compiler_params=pltpu.CompilerParams(
            dimension_semantics=("arbitrary",), vmem_limit_bytes=VMEM_BYTES
        ),
        name="project",
    )(inputs, edge, gain, *weights)


def project_side_kernel(normed, edge, query_w, gate_w, raw_out, edge_out, gate_out):
    raw_out[...] = low(product(normed[...], query_w[...]))
    gate_out[...] = product(normed[...], gate_w[...])

    @pl.when(pl.program_id(0) == 0)
    def _():
        edge_out[...] = low(product(edge[...], query_w[...]))


def run_project_side(normed, edge, query_w, gate_w):
    count, features = normed.shape
    cols = query_w.shape[1]
    tile = min(TILE, count)
    tokens = lambda cols: pl.BlockSpec((tile, cols), lambda c: (c, 0))
    return pl.pallas_call(
        project_side_kernel,
        grid=(count // tile,),
        in_specs=[
            tokens(features), whole_spec(HALO, features), once(query_w.shape), once(gate_w.shape)
        ],
        out_specs=[tokens(cols), whole_spec(HALO, cols), tokens(cols)],
        out_shape=[
            jax.ShapeDtypeStruct((count, cols), BF16),
            jax.ShapeDtypeStruct((HALO, cols), BF16),
            jax.ShapeDtypeStruct((count, cols), F32),
        ],
        compiler_params=pltpu.CompilerParams(
            dimension_semantics=("arbitrary",), vmem_limit_bytes=VMEM_BYTES
        ),
        name="project_side",
    )(normed, edge, query_w, gate_w)


def heads_kernel(
    head_count, width,
    local, reach, state, gate, gain, weight,
    mixer_out, heads_out, own_out, low_out,
):
    gain_row = gain[...]
    for h in range(head_count):
        at = slice(h * width, (h + 1) * width)
        mixer = local[:, at] + product(reach[:, at], state[h])
        logit = gate[:, at]
        mixer_out[:, at] = mixer
        heads_out[:, at] = low(
            mixer * row_scale_of(mixer) * gain_row * (logit * jax.nn.sigmoid(logit))
        )
    branch = times_transposed(heads_out[...], weight[...])
    own_out[...] = branch
    low_out[...] = low(branch)


def run_heads(local, reach, state, gate, gain, weight, head_count, width):
    count, cols = local.shape
    features = weight.shape[0]
    tile = min(TILE, count)
    tokens = lambda cols: pl.BlockSpec((tile, cols), lambda c: (c, 0))
    return pl.pallas_call(
        functools.partial(heads_kernel, head_count, width),
        grid=(count // tile,),
        in_specs=[
            tokens(cols), tokens(cols), whole_spec(*state.shape), tokens(cols),
            whole_spec(*gain.shape), once(weight.shape),
        ],
        out_specs=[tokens(cols), tokens(cols), tokens(features), tokens(features)],
        out_shape=[
            jax.ShapeDtypeStruct((count, cols), F32),
            jax.ShapeDtypeStruct((count, cols), BF16),
            jax.ShapeDtypeStruct((count, features), F32),
            jax.ShapeDtypeStruct((count, features), BF16),
        ],
        compiler_params=pltpu.CompilerParams(
            dimension_semantics=("arbitrary",), vmem_limit_bytes=VMEM_BYTES
        ),
        name="heads",
    )(local, reach, state, gate, gain, weight)


def feed_kernel(
    inputs, own, other, gain, cotangent, gate_w, up_w, down_w,
    hidden_out, normed_out, act_out, d_gate_out, d_up_out, branch_out, own_out, low_out,
):
    hidden = inputs[...].astype(F32) + own[...] + other[...].astype(F32)
    hidden_out[...] = hidden
    normed = low(hidden * row_scale_of(hidden) * gain[...])
    normed_out[...] = normed
    gate = product(normed, gate_w[...])
    up = product(normed, up_w[...])
    d_act = product(cotangent[...], down_w[...])
    sigma = jax.nn.sigmoid(gate)
    act = gate * sigma
    activation = low(act * up)
    d_up = low(d_act * act)
    d_gate = low(d_act * up * silu_slope(gate, sigma))
    act_out[...] = activation
    d_gate_out[...] = d_gate
    d_up_out[...] = d_up
    branch_out[...] = low(times_transposed(activation, down_w[...]))
    d_normed = times_transposed(d_gate, gate_w[...]) + times_transposed(d_up, up_w[...])
    own_out[...] = d_normed
    low_out[...] = low(d_normed)


def run_feed(inputs, own, other, gain, cotangent, gate_w, up_w, down_w):
    count, features = inputs.shape
    cols = gate_w.shape[1]
    tile = min(TILE, count)
    tokens = lambda cols: pl.BlockSpec((tile, cols), lambda c: (c, 0))
    shape = lambda cols, kind: jax.ShapeDtypeStruct((count, cols), kind)
    return pl.pallas_call(
        feed_kernel,
        grid=(count // tile,),
        in_specs=[tokens(features)] * 3
        + [whole_spec(1, features), tokens(features)]
        + [once(weight.shape) for weight in (gate_w, up_w, down_w)],
        out_specs=[tokens(features)] * 2 + [tokens(cols)] * 3 + [tokens(features)] * 3,
        out_shape=[shape(features, F32), shape(features, BF16)]
        + [shape(cols, BF16)] * 3
        + [shape(features, BF16), shape(features, F32), shape(features, BF16)],
        compiler_params=pltpu.CompilerParams(
            dimension_semantics=("arbitrary",), vmem_limit_bytes=VMEM_BYTES
        ),
        name="feed",
    )(inputs, own, other, gain, cotangent, gate_w, up_w, down_w)


def turn_kernel(
    head_count, width,
    hidden, own, other, gain, cotangent, weight, mixer_in, gate, head_gain, reach,
    d_hidden_out, d_low_out, d_gate_out, d_mixer_out, state_out, feed_gain_out, head_gain_out,
):
    @pl.when(pl.program_id(0) == 0)
    def _():
        state_out[...] = jnp.zeros(state_out.shape, F32)
        feed_gain_out[...] = jnp.zeros(feed_gain_out.shape, F32)
        head_gain_out[...] = jnp.zeros(head_gain_out.shape, F32)

    d_normed = own[...] + other[...].astype(F32)
    back, terms = norm_back(hidden[...], gain[...], d_normed)
    feed_gain_out[...] += jnp.sum(terms, axis=0, keepdims=True)
    d_hidden = cotangent[...].astype(F32) + back
    d_hidden_out[...] = d_hidden
    d_low = low(d_hidden)
    d_low_out[...] = d_low
    d_heads = product(d_low, weight[...])
    gain_row = head_gain[...]
    for h in range(head_count):
        at = slice(h * width, (h + 1) * width)
        mixer = mixer_in[:, at]
        unit = mixer * row_scale_of(mixer)
        logit = gate[:, at]
        sigma = jax.nn.sigmoid(logit)
        d_head = d_heads[:, at]
        d_gate_out[:, at] = low(d_head * (unit * gain_row) * silu_slope(logit, sigma))
        d_mixer, head_terms = norm_back(mixer, gain_row, d_head * (logit * sigma))
        head_gain_out[...] += jnp.sum(head_terms, axis=0, keepdims=True)
        d_mixer_low = low(d_mixer)
        d_mixer_out[:, at] = d_mixer_low
        state_out[h] += inner_rows(reach[:, at], d_mixer_low)


def run_turn(
    hidden, own, other, gain, cotangent, weight, mixer, gate, head_gain, reach, head_count, width
):
    count, features = hidden.shape
    cols = mixer.shape[1]
    tile = min(TILE, count)
    tokens = lambda cols: pl.BlockSpec((tile, cols), lambda c: (c, 0))
    shape = lambda cols, kind: jax.ShapeDtypeStruct((count, cols), kind)
    state = (head_count, width, width)
    return pl.pallas_call(
        functools.partial(turn_kernel, head_count, width),
        grid=(count // tile,),
        in_specs=[tokens(features)] * 3
        + [whole_spec(1, features), tokens(features), once(weight.shape)]
        + [tokens(cols), tokens(cols), whole_spec(1, width), tokens(cols)],
        out_specs=[tokens(features)] * 2
        + [tokens(cols)] * 2
        + [whole_spec(*state), whole_spec(1, features), whole_spec(1, width)],
        out_shape=[shape(features, F32), shape(features, BF16)]
        + [shape(cols, BF16)] * 2
        + [
            jax.ShapeDtypeStruct(state, F32),
            jax.ShapeDtypeStruct((1, features), F32),
            jax.ShapeDtypeStruct((1, width), F32),
        ],
        compiler_params=pltpu.CompilerParams(
            dimension_semantics=("arbitrary",), vmem_limit_bytes=VMEM_BYTES
        ),
        name="turn",
    )(hidden, own, other, gain, cotangent, weight, mixer, gate, head_gain, reach)


def back_project_kernel(extra, inputs, d_raw, d_extra, d_gate, query_w, gate_w, *refs):
    weights, (out, gain_out) = refs[:-2], refs[-2:]
    at = query_w.shape[1]
    total = times_transposed(d_raw[:, :at], query_w[...])
    for k, weight in enumerate(weights):
        size = weight.shape[1] - (extra if k == len(weights) - 1 else 0)
        total += times_transposed(d_raw[:, at : at + size], weight[:, :size])
        at += size
    total += times_transposed(d_extra[...], weights[-1][:, -extra:])
    total += times_transposed(d_gate[...], gate_w[...])
    total = low(total)
    out[...] = total

    @pl.when(pl.program_id(0) == 0)
    def _():
        gain_out[...] = jnp.zeros(gain_out.shape, F32)

    values = inputs[...].astype(F32)
    gain_out[...] += jnp.sum(
        total.astype(F32) * (values * row_scale_of(values)), axis=0, keepdims=True
    )


def run_back_project(inputs, d_raw, d_extra, d_gate, weights):
    count, features = inputs.shape
    tile = min(TILE, count)
    tokens = lambda cols: pl.BlockSpec((tile, cols), lambda c: (c, 0))
    return pl.pallas_call(
        functools.partial(back_project_kernel, d_extra.shape[1]),
        grid=(count // tile,),
        in_specs=[tokens(array.shape[1]) for array in (inputs, d_raw, d_extra, d_gate)]
        + [once(weight.shape) for weight in weights],
        out_specs=[tokens(features), whole_spec(1, features)],
        out_shape=[
            jax.ShapeDtypeStruct((count, features), BF16),
            jax.ShapeDtypeStruct((1, features), F32),
        ],
        compiler_params=pltpu.CompilerParams(
            dimension_semantics=("arbitrary",), vmem_limit_bytes=VMEM_BYTES
        ),
        name="back_project",
    )(inputs, d_raw, d_extra, d_gate, *weights)


def shift_seq(array, by):
    count = lax.axis_size("seq")
    return lax.ppermute(
        array, "seq", [(i, i + by) for i in range(count) if 0 <= i + by < count]
    )


def swap_seq(array, distance):
    return lax.ppermute(array, "seq", [(i, i ^ distance) for i in range(lax.axis_size("seq"))])


def swap_head(array):
    return lax.ppermute(array, "head", [(0, 1), (1, 0)])


def head_sum(array):
    return array + swap_head(array)


def fine_low(form, former, latter):
    high, rest = split(former)
    return form(high, latter) + form(rest, latter)


def fine_first(form, former, latter):
    high, rest = split(latter)
    return form(former, high) + form(former, rest)


def join_kernel(final, upper, group, other, before, group_out, low_out, before_out):
    heads, width, _ = group.shape

    @pl.when(upper[0] == 1)
    def _():
        for head in range(heads):
            theirs = other[head]
            reach = fine_low(product, before[head, :, :width], theirs)
            before_out[head, :, :width] = reach[:, :width]
            before_out[head, :, width:] = reach[:, width:] + before[head, :, width:]
            if not final:
                mine = fine_low(product, group[head, :, :width], theirs)
                group_out[head, :, :width] = mine[:, :width]
                group_out[head, :, width:] = mine[:, width:] + group[head, :, width:]

    @pl.when(upper[0] == 0)
    def _():
        before_out[...] = before[...]
        if not final:
            for head in range(heads):
                theirs = other[head]
                mine = fine_first(product, theirs[:, :width], group[head])
                group_out[head, :, :width] = mine[:, :width]
                group_out[head, :, width:] = mine[:, width:] + theirs[:, width:].astype(F32)

    low_out[...] = low(group_out[...]) if not final else low(before_out[...])


def join_groups(final, upper, group, other, before):
    whole = pl.BlockSpec(memory_space=pltpu.VMEM)
    full = jax.ShapeDtypeStruct(group.shape, F32)
    return pl.pallas_call(
        functools.partial(join_kernel, final),
        in_specs=[pl.BlockSpec(memory_space=pltpu.SMEM), whole, whole, whole],
        out_specs=[whole, whole, whole],
        out_shape=[full, jax.ShapeDtypeStruct(group.shape, BF16), full],
        compiler_params=pltpu.CompilerParams(vmem_limit_bytes=VMEM_BYTES),
        name="join_groups",
    )(upper, group, other, before)


def back_kernel(final, upper, group, other, after, group_map, other_map, after_map, *outs):
    group_out, low_out, after_out, after_map_out = outs
    heads, width, _ = group.shape
    after_out[...] = after[...]
    after_map_out[...] = after_map[...]
    if final:
        group_out[...] = group[...]

    @pl.when(upper[0] == 1)
    def _():
        if not final:
            for head in range(heads):
                theirs = other_map[head, :, :width]
                group_out[head] = other[head].astype(F32) + fine_first(
                    inner_rows, theirs, group[head]
                )

    @pl.when(upper[0] == 0)
    def _():
        for head in range(heads):
            theirs = other[head]
            after_out[head] += fine_low(inner_rows, after_map[head], theirs)
            if not final:
                group_out[head] = group[head] + fine_low(
                    inner_rows, group_map[head, :, :width], theirs
                )
                after_map_out[head] = fine_first(
                    product, other_map[head, :, :width], after_map[head]
                )

    low_out[...] = low(group_out[...])


def join_back(final, upper, group, other, after, group_map, other_map, after_map):
    whole = pl.BlockSpec(memory_space=pltpu.VMEM)
    full = jax.ShapeDtypeStruct(group.shape, F32)
    return pl.pallas_call(
        functools.partial(back_kernel, final),
        in_specs=[pl.BlockSpec(memory_space=pltpu.SMEM)] + [whole] * 6,
        out_specs=[whole] * 4,
        out_shape=[full, jax.ShapeDtypeStruct(group.shape, BF16), full, full],
        compiler_params=pltpu.CompilerParams(vmem_limit_bytes=VMEM_BYTES),
        name="join_back",
    )(upper, group, other, after, group_map, other_map, after_map)


def states_before(group, eye):
    count, mine = lax.axis_size("seq"), lax.axis_index("seq")
    before = jnp.concatenate([eye, jnp.zeros_like(eye)], 2)
    group_low = low(group)
    kept = []
    distance = 1
    while distance < count:
        other = swap_seq(group_low, distance)
        upper = ((mine // distance) % 2).astype(jnp.int32).reshape(1)
        kept.append((group, other, upper))
        final = 2 * distance >= count
        group, group_low, before = join_groups(final, upper, group, other, before)
        distance *= 2
    return group_low[:, :, group.shape[1] :], kept


def adjoints_after(own, kept, eye):
    group, group_low = own, low(own)
    after, after_map = jnp.zeros_like(own), eye
    distance = 1
    for group_map, other_map, upper in kept:
        other = swap_seq(group_low, distance)
        final = 2 * distance >= lax.axis_size("seq")
        group, group_low, after, after_map = join_back(
            final, upper, group, other, after, group_map, other_map, after_map
        )
        distance *= 2
    return after


def bit_orders(count):
    distances = [1 << k for k in range(count.bit_length() - 1)]
    near, far = distances[:3], distances[3:]
    return [near[k:] + near[:k] for k in range(len(near))], far


def scatter_view(array):
    count = lax.axis_size("seq")
    bits = count.bit_length() - 1
    return array.reshape((2,) * bits + (array.shape[0] // count, array.shape[1]))


def swap_all(arrays, distances):
    return [swap_seq(array, distance) for array, distance in zip(arrays, distances)]


def halve_all(terms, distances):
    keeps, sends = [], []
    for arrays, distance in zip(terms, distances):
        axis = arrays[0].ndim - 2 - distance.bit_length()
        own = (lax.axis_index("seq") // distance) % 2
        cut = lambda array, at: lax.dynamic_slice_in_dim(array, at, 1, axis).astype(F32)
        keeps.append(low(functools.reduce(jnp.add, [cut(array, own) for array in arrays])))
        sends.append(low(functools.reduce(jnp.add, [cut(array, 1 - own) for array in arrays])))
    return keeps, sends


def block_at(me, q, have, free, flipped):
    index, left = 0, len(free)
    for distance in have:
        if distance in free:
            left -= 1
            digit = (q // (1 << left)) % 2
        else:
            digit = (me // distance) % 2
            digit = 1 - digit if distance == flipped else digit
        index = index * 2 + digit
    return index


def halve_kernel(counts, me, *refs):
    ins, outs = refs[: 2 * sum(counts)], refs[2 * sum(counts) :]
    for part, count in enumerate(counts):
        for side in range(2):
            total = ins[0][...].astype(F32)
            for ref in ins[1:count]:
                total = total + ref[...].astype(F32)
            outs[2 * part + side][...] = low(total)
            ins = ins[count:]


def halve_parts(terms, haves, distances):
    rows = terms[0][0].shape[-2]
    arrays, specs, out_specs, shapes = [], [], [], []
    blocks = 1 << (min(len(have) for have in haves[0]) - 1)
    for part, part_haves, distance in zip(terms, haves, distances):
        free = [d for d in min(part_haves, key=len) if d != distance]
        columns = part[0].shape[-1]
        for flipped in (None, distance):
            for array, have in zip(part, part_haves):
                arrays.append(array.reshape(-1, columns))
                specs.append(
                    pl.BlockSpec(
                        (rows, columns),
                        lambda q, me, have=have, free=free, flipped=flipped: (
                            block_at(me[0], q, have, free, flipped), 0
                        ),
                    )
                )
            out_specs.append(pl.BlockSpec((rows, columns), lambda q, me: (q, 0)))
            shapes.append(jax.ShapeDtypeStruct((blocks * rows, columns), BF16))
    outs = pl.pallas_call(
        functools.partial(halve_kernel, [len(part) for part in terms]),
        grid_spec=pltpu.PrefetchScalarGridSpec(
            num_scalar_prefetch=1, grid=(blocks,), in_specs=specs, out_specs=out_specs
        ),
        out_shape=shapes,
        compiler_params=pltpu.CompilerParams(
            dimension_semantics=("arbitrary",), vmem_limit_bytes=VMEM_BYTES
        ),
        name="halve",
    )(lax.axis_index("seq").astype(jnp.int32).reshape(1), *arrays)
    return outs[0::2], outs[1::2]


def far_steps(terms, distances):
    for distance in distances:
        keeps, sends = halve_all(terms, [distance] * len(terms))
        merged = swap_seq(jnp.concatenate(sends, -1), distance)
        others, start = [], 0
        for send in sends:
            wide = send.shape[-1]
            others.append(lax.slice_in_dim(merged, start, start + wide, axis=merged.ndim - 1))
            start += wide
        terms = list(zip(keeps, others))
    return [
        functools.reduce(jnp.add, [a.astype(F32) for a in arrays]).reshape(arrays[0].shape[-2:])
        for arrays in terms
    ]


def gather_join(view, other, distance):
    axis = view.ndim - 2 - distance.bit_length()
    upper = (lax.axis_index("seq") // distance) % 2 == 1
    return jnp.concatenate(
        [jnp.where(upper, other, view), jnp.where(upper, view, other)], axis
    )


def gather_far(pack, distances):
    bits = lax.axis_size("seq").bit_length() - 1
    view = pack.reshape((1,) * bits + pack.shape)
    for distance in distances[::-1]:
        view = gather_join(view, swap_seq(view, distance), distance)
    return view


def gather_cut(view, widths):
    parts, at = [], 0
    for wide in widths:
        parts.append(lax.slice_in_dim(view, at, at + wide, axis=view.ndim - 1))
        at += wide
    return parts


def gather_end(views):
    return [view.reshape(-1, view.shape[-1]) for view in views]


def tied(*values):
    return lax.optimization_barrier(values)


def per_device(
    activations,
    log_decay,
    doc_starts,
    query_weight,
    key_weight,
    value_weight,
    beta_weight,
    gate_weight,
    out_weight,
    query_taps,
    key_taps,
    value_taps,
    mixer_gain,
    head_gain,
    feed_gain,
    feed_gate,
    feed_up,
    feed_down,
    cotangent,
):
    count, features = activations.shape
    tap_count = query_taps.shape[0]
    width = head_gain.shape[0]
    query_cols = query_weight.shape[1]
    key_cols = key_weight.shape[1]
    conv_cols = query_cols + 2 * key_cols
    hidden_cols = feed_gate.shape[1]
    head_count = query_cols // width
    beta_cols = beta_weight.shape[1]
    substeps = beta_cols // head_count
    device_rank = lax.axis_index("seq")
    head_rank = lax.axis_index("head")
    extra = 128
    shard_rows = query_weight.shape[0]
    orders, far = bit_orders(lax.axis_size("seq"))
    at_step = lambda k: [order[k] for order in orders]
    gather_at = lambda k: [order[2 - k] for order in orders]
    pad = jnp.zeros((shard_rows, extra - beta_cols - 2), BF16)
    kv_pack = jnp.concatenate(
        [key_weight, value_weight, beta_weight, mixer_gain[:, None], feed_gain[:, None], pad], 1
    )
    side_pack = jnp.concatenate([query_weight, gate_weight, out_weight.T], 1)
    feed_pack = jnp.concatenate([feed_gate, feed_up, feed_down.T], 1)
    third = -(-kv_pack.shape[1] // (3 * width)) * width
    input_edge = shift_seq(activations[count - HALO :], 1)
    kv_view = gather_far(kv_pack, far)
    kv_view, side_pack = tied(kv_view, side_pack)
    kv_parts = gather_cut(kv_view, [third, third, kv_pack.shape[1] - 2 * third])
    side_view = gather_far(side_pack, far)
    for k in range(3):
        others = swap_all(kv_parts, gather_at(k))
        kv_parts = [gather_join(v, o, d) for v, o, d in zip(kv_parts, others, gather_at(k))]
    side_parts = gather_cut(side_view, [query_cols] * 3)
    weights_kv = gather_end(kv_parts)
    weights_kv, side_parts, feed_pack, input_edge = tied(
        weights_kv, side_parts, feed_pack, input_edge
    )
    gains = weights_kv[2][:, -extra + beta_cols : -extra + beta_cols + 2].T.astype(F32)
    gain_one, gain_two = gains[0:1], gains[1:2]

    token_position = device_rank * count + jnp.arange(count, dtype=jnp.int32)
    is_start = jnp.any(token_position[:, None] == doc_starts[None, :], axis=1)

    def same_docs(position):
        doc = lambda p: jnp.sum((p[:, None] >= doc_starts[None, :]).astype(jnp.int32), axis=1)
        own = doc(position)
        return jnp.stack(
            [
                ((doc(position - offset) == own) & (position >= offset)).astype(F32)
                for offset in range(tap_count)
            ],
            1,
        )

    same = same_docs(token_position)
    log_gate = log_decay - RESET * is_start.astype(F32)[:, None]
    chunks = count // BLOCK
    cumulative = jnp.cumsum(log_gate.reshape(chunks, BLOCK, head_count), axis=1)
    cum_col = cumulative.reshape(count, head_count)
    cum_row = jnp.concatenate([jnp.swapaxes(cumulative, 1, 2)] * substeps, 2)
    taps_all = jnp.concatenate([query_taps, key_taps, value_taps], 1).astype(F32)

    side_others = swap_all(side_parts, gather_at(0))
    feed_view = gather_far(feed_pack, far)
    normed, edge_normed, raw_kv, edge_kv, sigmas = run_project(
        activations, input_edge, gain_one, weights_kv, 2 * key_cols, extra
    )
    beta_gate = sigmas[:, :beta_cols]
    eye = jnp.broadcast_to(jnp.eye(width, dtype=F32), (head_count, width, width))
    chain = jnp.concatenate([eye, jnp.zeros_like(eye)], 2)
    passed = ()
    feed_parts = None
    side_at, feed_at = 1, 0
    sides = [gather_join(v, o, d) for v, o, d in zip(side_parts, side_others, gather_at(0))]
    marks = [(chunks * k) // (AHEAD_CALLS * PAIR) * PAIR for k in range(AHEAD_CALLS + 1)]
    sends, distances = sides, gather_at(1)
    for call in range(AHEAD_CALLS):
        chain, sends = tied(chain, sends)
        others = swap_all(sends, distances)
        *passed, chain = run_forward(
            marks[call], marks[call + 1], raw_kv, edge_kv, taps_all, same, beta_gate, cum_col,
            cum_row, chain, tuple(passed), head_count, substeps, width,
        )
        if call == 0:
            chain, others, feed_view = tied(chain, others, feed_view)
        else:
            chain, others = tied(chain, others)
        joined = [gather_join(v, o, d) for v, o, d in zip(sends, others, distances)]
        if call == 0:
            feed_parts = gather_cut(feed_view, [hidden_cols] * 3)
            sends, distances = joined + feed_parts, gather_at(2) + gather_at(0)
        elif call == 1:
            sides, sends, distances = joined[:3], joined[3:], gather_at(1)
        else:
            feed_parts = joined
    t_part, p_part, s_part, key_rows, solved = passed
    weight_query, weight_gate, weight_out = gather_end(sides)

    state_low, kept = states_before(chain, eye)
    state_low, feed_parts = tied(state_low, feed_parts)
    others = swap_all(feed_parts, gather_at(2))
    feed_gate_w, feed_up_w, feed_down_w = gather_end(
        [gather_join(v, o, d) for v, o, d in zip(feed_parts, others, gather_at(2))]
    )
    raw_query, edge_query, gate_view = run_project_side(
        normed, edge_normed, weight_query, weight_gate
    )
    q_reach, local_out = run_query(
        raw_query, edge_query, taps_all[:, :query_cols], same, cum_col, cum_row, key_rows, solved,
        p_part, s_part, head_count, substeps, width,
    )
    head_gain_row = head_gain.astype(F32)[None]
    mixer_out, heads_out, branch_own, branch_low = run_heads(
        local_out, q_reach, state_low, gate_view, head_gain_row, weight_out, head_count, width
    )
    (
        hidden, normed_ffn, activation, d_gate, d_up, branch_two, d_normed_own, d_normed_low,
    ) = run_feed(
        activations, branch_own, swap_head(branch_low), gain_two, cotangent,
        feed_gate_w, feed_up_w, feed_down_w,
    )
    half = features // lax.axis_size("head")
    own_half = lambda array: lax.dynamic_slice_in_dim(array, head_rank * half, half, 1)
    other_half = lambda array: lax.dynamic_slice_in_dim(array, (1 - head_rank) * half, half, 1)
    output = low(
        own_half(hidden)
        + own_half(branch_two).astype(F32)
        + swap_head(other_half(branch_two)).astype(F32)
    )

    near = orders[0]
    grad_orders = [
        [near[2], near[1], near[0]],
        [near[0], near[2], near[1]],
        [near[1], near[0], near[2]],
        [near[1], near[0], near[2]],
        [near[1], near[2], near[0]],
    ]
    down_grad = scatter_view(low(inner_rows(cotangent, activation)))
    _, down_send = halve_all([(down_grad,)], [grad_orders[2][0]])
    d_normed_other, down_send = tied(swap_head(d_normed_low), down_send)
    down_other = swap_all(down_send, [grad_orders[2][0]])[0]
    (
        d_hidden, grad_mixer, d_gate_logit, d_mixer_low, own_part, grad_feed_gain, head_gain_part,
    ) = run_turn(
        hidden, d_normed_own, d_normed_other, gain_two, cotangent, weight_out,
        mixer_out, gate_view, head_gain_row, q_reach, head_count, width,
    )
    grad_feed_gain, head_gain_part = grad_feed_gain[0], head_gain_part[0]
    adjoint = adjoints_after(own_part, kept, eye)
    terms = [
        (scatter_view(low(inner_rows(normed_ffn, d_gate))),),
        (scatter_view(low(inner_rows(normed_ffn, d_up))),),
        (scatter_view(low(inner_rows(grad_mixer, heads_out))),),
        (scatter_view(low(inner_rows(normed, d_gate_logit))),),
    ]
    down_other, adjoint = tied(down_other, adjoint)
    marks = [chunks, (3 * chunks // 8) // PAIR * PAIR, (chunks // 8) // PAIR * PAIR, 0]
    carried = jnp.zeros((8, conv_cols), F32)
    tap_grads = jnp.zeros((tap_count, conv_cols), F32)
    passed = ()
    every = [1 << k for k in range(lax.axis_size("seq").bit_length() - 1)][::-1]
    left = [every] * 5
    haves = [[every]] * 5
    down_terms = (down_grad, down_other)
    bits = len(every)
    for call in range(3):
        distances = [order[call] for order in grad_orders]
        if call == 0:
            kinds = [0, 1, 3, 4]
            sends = halve_all(terms, [distances[k] for k in kinds])[1]
            keeps = [part[0] for part in terms]
            distances = [distances[k] for k in kinds]
        elif shard_rows < HALO:
            views = [
                (
                    [array.reshape((2,) * len(have) + array.shape[-2:]) for array, have in zip(*p)],
                    p[1],
                )
                for p in zip(terms, haves)
            ]
            sums = []
            for part, part_haves in views:
                small_have = min(part_haves, key=len)
                total = None
                for array, have in zip(part, part_haves):
                    for axis, d in reversed(list(enumerate(have))):
                        if d not in small_have:
                            array = lax.dynamic_index_in_dim(
                                array, (lax.axis_index("seq") // d) % 2, axis, keepdims=False
                            )
                    array = array.astype(F32)
                    total = array if total is None else total + array
                sums.append((total, small_have))
            keeps, sends = [], []
            for (total, have), d in zip(sums, distances):
                own = (lax.axis_index("seq") // d) % 2
                columns = total.shape[-1]
                pick = lambda at: low(
                    lax.dynamic_index_in_dim(total, at, have.index(d), keepdims=False)
                ).reshape(-1, columns)
                keeps.append(pick(own))
                sends.append(pick(1 - own))
        else:
            keeps, sends = halve_parts(terms, haves, distances)
        adjoint, sends, keeps = tied(adjoint, sends, keeps)
        others = swap_all(sends, distances)
        d_raw, d_beta_logit, new_tail, adjoint, carried, tap_grads = run_backward(
            marks[call + 1], marks[call],
            raw_query, edge_query, raw_kv, edge_kv, taps_all, same, beta_gate, cum_col, cum_row,
            t_part, p_part, s_part, state_low, d_mixer_low, adjoint, carried, tap_grads, passed,
            head_count, substeps, width,
        )
        if call == 0:
            tail = new_tail
        adjoint, carried, others = tied(adjoint, carried, others)
        passed = (d_raw, d_beta_logit)
        terms = [
            (k.reshape(-1, k.shape[-1]), o.reshape(-1, o.shape[-1])) for k, o in zip(keeps, others)
        ]
        if call == 0:
            down = tuple(array.reshape(-1, array.shape[-1]) for array in down_terms)
            terms = terms[:2] + [down] + terms[2:]
        left = [[d for d in l if d != order[call]] for l, order in zip(left, grad_orders)]
        haves = [[every if call == 0 else l, l] for l in left]
        cube = lambda a: a.reshape(-1, shard_rows, a.shape[-1])
        terms = [tuple(cube(a) for a in part) for part in terms]
    ones = (1,) * (bits - len(far))
    terms = [
        tuple(a.reshape((2,) * len(far) + ones + (shard_rows, a.shape[-1])) for a in part)
        for part in terms
    ]
    first_rows = carried
    returned = shift_seq(first_rows, -1)
    same_after = same_docs(token_position[-1] + 1 + jnp.arange(8, dtype=jnp.int32))
    spread = jnp.zeros_like(tail)
    for offset in range(1, tap_count):
        masked = returned * same_after[:, offset : offset + 1] * taps_all[offset]
        spread = spread + jnp.pad(masked[:offset], ((8 - offset, 0), (0, 0)))
    d_raw = lax.dynamic_update_slice(d_raw, low(tail + spread), (count - 8, 0))
    d_beta_low = low(d_beta_logit)
    fifth = -(-conv_cols // (5 * width)) * width
    conv_marks = [0, 2 * fifth, 4 * fifth, conv_cols]
    keeps, sends = halve_all(
        [
            (scatter_view(low(inner_rows(normed, d_raw[:, a:b]))),)
            for a, b in zip(conv_marks[:-1], conv_marks[1:])
        ],
        at_step(0),
    )
    d_raw, d_beta_low, sends, keeps = tied(d_raw, d_beta_low, sends, keeps)
    others = swap_all(sends, at_step(0))
    feed_sums = far_steps(terms, far)
    d_extra = jnp.pad(d_beta_low, ((0, 0), (0, extra - beta_cols)))
    d_low, gain_part = run_back_project(
        activations, d_raw, d_extra, d_gate_logit, [weight_query, weight_gate, *weights_kv]
    )
    d_low, gain_part, others = tied(d_low, gain_part, others)
    both_heads = jnp.concatenate([gain_part[0], head_gain_part])
    both_heads = both_heads + swap_head(both_heads)
    d_other = swap_head(d_low)
    small = jnp.concatenate(
        [
            inner_rows(d_beta_low, normed).reshape(-1),
            both_heads[:features],
            grad_feed_gain,
            tap_grads.reshape(-1),
            both_heads[features:],
        ]
    )
    small = jnp.pad(small, (0, -small.shape[0] % 1024)).reshape(-1, 128)
    for at in (1, 2):
        keeps, sends = halve_all(list(zip(keeps, others)), at_step(at))
        small, sends, keeps = tied(small, sends, keeps)
        others = swap_all(sends, at_step(at))
        small = small + swap_seq(small, near[at - 1])
        if at == 1:
            d_normed = d_low.astype(F32) + d_other.astype(F32)
            d_input_norm, _ = norm_back(activations.astype(F32), gain_one, d_normed)
            grad_input = own_half(d_hidden + d_input_norm)
            grad_input, small, others = tied(grad_input, small, others)
        else:
            small, others = tied(small, others)
    conv_sum = jnp.concatenate(far_steps(list(zip(keeps, others)), far), 1)
    for distance in near[2:] + far:
        small = small + swap_seq(small, distance)
    small = small.reshape(-1)
    ends, at = [], 0
    for size in (beta_cols * features, features, features, tap_count * conv_cols, width):
        ends.append(small[at : at + size])
        at += size
    own_rows = lambda vector: lax.dynamic_slice_in_dim(
        vector, device_rank * shard_rows, shard_rows, vector.ndim - 1
    )
    tap_total = ends[3].reshape(tap_count, conv_cols)
    cut = lambda array, start, size: array[:, start : start + size]
    return (
        output,
        grad_input,
        cut(conv_sum, 0, query_cols),
        cut(conv_sum, query_cols, key_cols),
        cut(conv_sum, query_cols + key_cols, key_cols),
        own_rows(ends[0].reshape(beta_cols, features)).T,
        feed_sums[4],
        feed_sums[3].T,
        cut(tap_total, 0, query_cols),
        cut(tap_total, query_cols, key_cols),
        cut(tap_total, query_cols + key_cols, key_cols),
        own_rows(ends[1]),
        ends[4],
        own_rows(ends[2]),
        feed_sums[0],
        feed_sums[1],
        feed_sums[2].T,
    )


def solution(mesh):
    in_specs = (
        P("seq", None),
        P("seq", "head"),
        P(),
        P("seq", "head"),
        P("seq", "head"),
        P("seq", "head"),
        P("seq", "head"),
        P("seq", "head"),
        P("head", "seq"),
        P(None, "head"),
        P(None, "head"),
        P(None, "head"),
        P("seq"),
        P(),
        P("seq"),
        P("seq", "head"),
        P("seq", "head"),
        P("head", "seq"),
        P("seq", None),
    )
    out_specs = (
        P("seq", "head"),
        P("seq", "head"),
        P("seq", "head"),
        P("seq", "head"),
        P("seq", "head"),
        P("seq", "head"),
        P("seq", "head"),
        P("head", "seq"),
        P(None, "head"),
        P(None, "head"),
        P(None, "head"),
        P("seq"),
        P(),
        P("seq"),
        P("seq", "head"),
        P("seq", "head"),
        P("head", "seq"),
    )
    return jax.shard_map(
        per_device, mesh=mesh, in_specs=in_specs, out_specs=out_specs, check_vma=False
    )
```

```python
import functools

import jax
import jax.numpy as jnp
from jax import lax
from jax.experimental import pallas as pl
from jax.experimental.pallas import tpu as pltpu
from jax.sharding import PartitionSpec as P

BLOCK = 64
RESET = 256.0
HALO = 16
VMEM_BYTES = 63 * 1024 * 1024
PAIR = 2
QUERY_CHUNKS = 2
TILE = 256
AHEAD_CALLS = 3
NORM_EPS = 1e-05
UNIT_EPS = 1e-06
F32 = jnp.float32
BF16 = jnp.bfloat16


def product(former, latter):
    return jnp.dot(former, latter, preferred_element_type=F32)


def inner_rows(former, latter):
    return lax.dot_general(former, latter, (((0,), (0,)), ((), ())), preferred_element_type=F32)


def times_transposed(former, latter):
    return lax.dot_general(former, latter, (((1,), (1,)), ((), ())), preferred_element_type=F32)


def low(values):
    return values.astype(BF16)


def split(values):
    high = values.astype(BF16)
    return high, (values - high.astype(F32)).astype(BF16)


def fine(form, former, latter):
    a_high, a_low = split(former)
    b_high, b_low = split(latter)
    return form(a_high, b_high) + (form(a_low, b_high) + form(a_high, b_low))


def silu_slope(values, sigma):
    return sigma * (1.0 + values * (1.0 - sigma))


def norm_back(values, gain_vector, gradient):
    row_scale = lax.rsqrt(jnp.mean(values * values, axis=-1, keepdims=True) + NORM_EPS)
    unit_value = values * row_scale
    scaled_grad = gradient * gain_vector
    back_value = row_scale * (
        scaled_grad - unit_value * jnp.mean(scaled_grad * unit_value, axis=-1, keepdims=True)
    )
    return (back_value, gradient * unit_value)


def row_maps(rows):
    row = lax.broadcasted_iota(jnp.int32, (rows, rows), 0)
    col = lax.broadcasted_iota(jnp.int32, (rows, rows), 1)
    return row % BLOCK, col % BLOCK, row // BLOCK, col // BLOCK


def lower_inverses(systems, apart):
    rows = systems[0].shape[0]
    row = lax.broadcasted_iota(jnp.int32, (rows, rows), 0)
    col = lax.broadcasted_iota(jnp.int32, (rows, rows), 1)
    eye = jnp.where(row == col, 1.0, 0.0)
    inverses = [eye - jnp.where(apart == 0, system, 0.0) for system in systems]
    level = 0
    while (1 << level) < BLOCK:
        joins = (apart >> level) == 1
        joints = [low(jnp.where(joins, system, 0.0)) for system in systems]
        lows = [low(inverse) for inverse in inverses]
        halves = [low(product(a, b)) for a, b in zip(lows, joints)]
        inverses = [c - product(a, b) for a, b, c in zip(halves, lows, inverses)]
        level += 1
    return inverses


def conv_rows(tile, halo, taps, same):
    count = tile.shape[0]
    extended = jnp.concatenate([halo, tile], 0)
    windows = [tile] + [
        pltpu.roll(extended, offset, 0)[8:] for offset in range(1, taps.shape[0])
    ]
    outcome = tile * taps[0:1]
    for offset in range(1, taps.shape[0]):
        outcome = outcome + windows[offset] * taps[offset : offset + 1] * same[:, offset : offset + 1]
    return outcome, windows


def unit_scale(values):
    return lax.rsqrt(jnp.sum(values * values, axis=-1, keepdims=True) + UNIT_EPS)


def pieces_of(head, head_count, substeps, width):
    query = [(head * width, width)]
    keys = [((head_count + head * substeps + n) * width, width) for n in range(substeps)]
    values = [
        ((head_count + (head_count + head) * substeps + n) * width, width) for n in range(substeps)
    ]
    return query + keys + values


def conv_of(source, first, start, size, taps, same_rows):
    tile_ref, before, edge, offset = source
    columns = slice(start - offset, start - offset + size)
    halo = jnp.where(first, edge[:, columns], before[:, columns]).astype(F32)[HALO - 8 :]
    return conv_rows(
        tile_ref[:, columns].astype(F32), halo, taps[:, start : start + size], same_rows
    )


def beta_rows(beta, head, substeps):
    columns = [beta[:, head * substeps + n : head * substeps + n + 1] for n in range(substeps)]
    return jnp.concatenate(columns, 0)


def forward_kernel(
    head_count, substeps, width, begin,
    raw, before, edge, taps, same, beta, cum_col, cum_row, chain_in, *refs,
):
    t_out, p_out, s_out, key_out, solved_out, chain = refs[-6:]
    step = pl.program_id(0)
    first = step + begin == 0
    rows = BLOCK * substeps
    row_token, col_token, row_step, col_step = row_maps(rows)
    upto = col_token <= row_token
    earlier = (col_token < row_token) | ((col_token == row_token) & (col_step < row_step))
    apart = row_token ^ col_token
    eye = jnp.where(
        lax.broadcasted_iota(jnp.int32, (width, width), 0)
        == lax.broadcasted_iota(jnp.int32, (width, width), 1),
        1.0,
        0.0,
    )
    same_rows = same[...]

    @pl.when(step == 0)
    def _():
        chain[...] = chain_in[...]

    heads = range(head_count)
    offset = head_count * width
    source = (raw, before, edge, offset)
    units = [(j, h) for j in range(PAIR) for h in heads]
    rows_at = [slice(j * BLOCK, (j + 1) * BLOCK) for j in range(PAIR)]
    keys, values, betas = {}, {}, {}
    for head in heads:
        acts = []
        for start, size in pieces_of(head, head_count, substeps, width)[1:]:
            pre, _ = conv_of(source, first, start, size, taps, same_rows)
            acts.append(pre * jax.nn.sigmoid(pre))
        acts = [a * unit_scale(a) for a in acts[:substeps]] + acts[substeps:]
        acts = [low(a) for a in acts]
        for j, at in enumerate(rows_at):
            keys[j, head] = jnp.concatenate([a[at] for a in acts[:substeps]], 0)
            values[j, head] = jnp.concatenate([a[at] for a in acts[substeps:]], 0)
            betas[j, head] = beta_rows(beta[at], head, substeps)
    keys, values, betas = ([held[u] for u in units] for held in (keys, values, betas))
    cum_rows = [jnp.concatenate([cum_col[rows_at[j], h : h + 1]] * substeps, 0) for j, h in units]
    cum_cols = [cum_row[j, h : h + 1, :] for j, h in units]
    lasts = [c[:, BLOCK - 1 : BLOCK] for c in cum_cols]
    ratios = [jnp.exp(jnp.where(upto, a - b, -1e4)) for a, b in zip(cum_rows, cum_cols)]
    grams = [times_transposed(key, key) for key in keys]
    systems = [
        jnp.where(earlier, beta_col * ratio * gram, 0.0)
        for beta_col, ratio, gram in zip(betas, ratios, grams)
    ]
    inverses = [low(inverse) for inverse in lower_inverses(systems, apart)]
    rights = [
        jnp.concatenate(
            [
                low(beta_col * jnp.exp(cum) * key.astype(F32)),
                low(beta_col * value.astype(F32)),
            ],
            1,
        )
        for beta_col, cum, key, value in zip(betas, cum_rows, keys, values)
    ]
    solved = [low(product(inverse, right)) for inverse, right in zip(inverses, rights)]
    ends = [
        low(jnp.exp(last - cum) * key.astype(F32))
        for last, cum, key in zip(lasts, cum_rows, keys)
    ]
    moved = [inner_rows(end, both) for end, both in zip(ends, solved)]
    step_maps = [split(jnp.exp(last) * eye - move[:, :width]) for last, move in zip(lasts, moved)]
    chains = [chain[head] for head in heads]
    for at, (j, head) in enumerate(units):
        t_out[j, head] = inverses[at]
        key_out[j, head] = keys[at]
        solved_out[j, head] = solved[at]
    for j in range(PAIR):
        at = j * head_count
        splits = [split(chained) for chained in chains]
        for head in heads:
            p_out[j, head] = splits[head][0][:, :width]
            s_out[j, head] = splits[head][0][:, width:]
        chains = [
            product(step_maps[at + h][0], splits[h][0])
            + (product(step_maps[at + h][1], splits[h][0]) + product(step_maps[at + h][0], splits[h][1]))
            for h in heads
        ]
        chains = [
            jnp.concatenate([c[:, :width], c[:, width:] + moved[at + h][:, width:]], 1)
            for h, c in enumerate(chains)
        ]
    for head in heads:
        chain[head] = chains[head]


def whole_spec(*shape):
    return pl.BlockSpec(shape, lambda *c: (0,) * len(shape))


def run_forward(
    begin, end, raw, edge, taps, same, beta, cum_col, cum_row, chain, passed,
    head_count, substeps, width,
):
    count, columns = raw.shape
    chunks = count // BLOCK
    rows = BLOCK * substeps
    begin, end = begin // PAIR, end // PAIR
    per_halo = PAIR * BLOCK // HALO
    tokens = lambda cols: pl.BlockSpec((PAIR * BLOCK, cols), lambda c: (c + begin, 0))
    tiles = lambda *shape: pl.BlockSpec((PAIR, head_count) + shape, lambda c: (c + begin, 0, 0, 0))
    shapes = [(rows, rows), (width, width), (width, width), (rows, width), (rows, 2 * width)]
    anywhere = pl.BlockSpec(memory_space=pl.ANY)
    return pl.pallas_call(
        functools.partial(forward_kernel, head_count, substeps, width, begin),
        grid=(end - begin,),
        in_specs=[
            tokens(columns),
            pl.BlockSpec(
                (HALO, columns), lambda c: (jnp.maximum((c + begin) * per_halo - 1, 0), 0)
            ),
            whole_spec(HALO, columns),
            whole_spec(*taps.shape),
            tokens(same.shape[1]),
            tokens(beta.shape[1]),
            tokens(head_count),
            pl.BlockSpec((PAIR, head_count, rows), lambda c: (c + begin, 0, 0)),
            whole_spec(*chain.shape),
        ]
        + [anywhere] * len(passed),
        out_specs=[tiles(*shape) for shape in shapes] + [whole_spec(*chain.shape)],
        out_shape=[
            jax.ShapeDtypeStruct((chunks, head_count) + shape, BF16) for shape in shapes
        ]
        + [jax.ShapeDtypeStruct(chain.shape, F32)],
        input_output_aliases={9 + k: k for k in range(len(passed))},
        compiler_params=pltpu.CompilerParams(
            dimension_semantics=("arbitrary",), vmem_limit_bytes=VMEM_BYTES
        ),
        name="mixer_forward",
    )(raw, raw, edge, taps, same, beta, cum_col, cum_row, chain, *passed)


def query_kernel(
    head_count, substeps, width,
    raw, before, edge, taps, same, cum_col, cum_row, key_in, solved_in, p_in, s_in,
    qtil_out, local_out,
):
    first = pl.program_id(0) == 0
    rows = BLOCK * substeps
    row_token, col_token, _, _ = row_maps(rows)
    upto = (col_token <= row_token)[:BLOCK]
    same_rows = same[...]
    heads = range(head_count)
    units = [(j, h) for j in range(QUERY_CHUNKS) for h in heads]
    rows_at = [slice(j * BLOCK, (j + 1) * BLOCK) for j in range(QUERY_CHUNKS)]
    queries = []
    for head in heads:
        start, size = pieces_of(head, head_count, substeps, width)[0]
        pre, _ = conv_of((raw, before, edge, 0), first, start, size, taps, same_rows)
        act = pre * jax.nn.sigmoid(pre)
        queries.append(low(act * unit_scale(act) * width ** (-0.5)))
    queries = [queries[h][rows_at[j]] for j, h in units]
    cum_rows = [cum_col[rows_at[j], h : h + 1] for j, h in units]
    ratios = [
        jnp.exp(jnp.where(upto, cum - cum_row[j, h : h + 1, :], -1e4))
        for cum, (j, h) in zip(cum_rows, units)
    ]
    scores = [times_transposed(query, key_in[j, h]) for query, (j, h) in zip(queries, units)]
    seen = [
        product(low(ratio * score), solved_in[j, h])
        for ratio, score, (j, h) in zip(ratios, scores, units)
    ]
    effective = [
        low(jnp.exp(cum) * query.astype(F32) - see[:, :width])
        for cum, query, see in zip(cum_rows, queries, seen)
    ]
    reached = [
        (product(eff, p_in[j, h]), product(eff, s_in[j, h]))
        for eff, (j, h) in zip(effective, units)
    ]
    for k, (j, h) in enumerate(units):
        at = slice(h * width, (h + 1) * width)
        qtil_out[rows_at[j], at] = low(reached[k][0])
        local_out[rows_at[j], at] = reached[k][1] + seen[k][:, width:]


def run_query(
    raw, edge, taps, same, cum_col, cum_row, key_rows, solved, p_part, s_part,
    head_count, substeps, width,
):
    count, columns = raw.shape
    chunks = count // BLOCK
    rows = BLOCK * substeps
    per_halo = QUERY_CHUNKS * BLOCK // HALO
    tokens = lambda cols: pl.BlockSpec((QUERY_CHUNKS * BLOCK, cols), lambda c: (c, 0))
    tiles = lambda *shape: pl.BlockSpec((QUERY_CHUNKS, head_count) + shape, lambda c: (c, 0, 0, 0))
    return pl.pallas_call(
        functools.partial(query_kernel, head_count, substeps, width),
        grid=(chunks // QUERY_CHUNKS,),
        in_specs=[
            tokens(columns),
            pl.BlockSpec((HALO, columns), lambda c: (jnp.maximum(c * per_halo - 1, 0), 0)),
            whole_spec(HALO, columns),
            whole_spec(*taps.shape),
            tokens(same.shape[1]),
            tokens(head_count),
            pl.BlockSpec((QUERY_CHUNKS, head_count, rows), lambda c: (c, 0, 0)),
            tiles(rows, width),
            tiles(rows, 2 * width),
            tiles(width, width),
            tiles(width, width),
        ],
        out_specs=[tokens(columns), tokens(columns)],
        out_shape=[
            jax.ShapeDtypeStruct((count, columns), BF16),
            jax.ShapeDtypeStruct((count, columns), F32),
        ],
        compiler_params=pltpu.CompilerParams(
            dimension_semantics=("arbitrary",), vmem_limit_bytes=VMEM_BYTES
        ),
        name="mixer_query",
    )(raw, raw, edge, taps, same, cum_col, cum_row, key_rows, solved, p_part, s_part)


def backward_kernel(
    head_count, substeps, width, end,
    raw_q, before_q, edge_q, raw, before, edge, taps, same, same_next, beta, cum_col, cum_row,
    t_in, p_in, s_in, state_in, d_out, adjoint_in, carried_in, tap_in, *refs,
):
    d_raw, d_logit, tail_out, adjoint, carried, tap_out, tail_next = refs[-7:]
    step = pl.program_id(0)
    pair = end - 1 - step
    rows = BLOCK * substeps
    tap_count = taps.shape[0]
    count = PAIR * BLOCK
    row_token, col_token, row_step, col_step = row_maps(rows)
    upto = col_token <= row_token
    earlier = (col_token < row_token) | ((col_token == row_token) & (col_step < row_step))
    same_rows = same[...]
    same_long = jnp.concatenate([same_rows, same_next[...]], 0)

    @pl.when(step == 0)
    def _():
        adjoint[...] = adjoint_in[...]
        carried[...] = carried_in[...]
        tap_out[...] = tap_in[...]

    heads = range(head_count)
    units_at = [(j, h) for j in range(PAIR) for h in heads]
    rows_at = [slice(j * BLOCK, (j + 1) * BLOCK) for j in range(PAIR)]
    pieces = [pieces_of(head, head_count, substeps, width) for head in heads]
    pres, sigmas, scales, units = [], [], [], []
    queries, keys, values, betas = {}, {}, {}, {}
    key_start = head_count * width
    sources = [(raw_q, before_q, edge_q, 0), (raw, before, edge, key_start)]

    def windows_of(start, size):
        return conv_of(sources[int(start >= key_start)], pair == 0, start, size, taps, same_rows)

    for head in heads:
        pre = [windows_of(start, size)[0] for start, size in pieces[head]]
        sigma = [jax.nn.sigmoid(p) for p in pre]
        acts = [p * s for p, s in zip(pre, sigma)]
        pres.append(pre)
        sigmas.append(sigma)
        scales.append([unit_scale(a) for a in acts[: 1 + substeps]])
        units.append([a * s for a, s in zip(acts[: 1 + substeps], scales[head])])
        query = low(units[head][0] * width ** (-0.5))
        key = [low(unit) for unit in units[head][1:]]
        value = [low(act) for act in acts[1 + substeps :]]
        for j, at in enumerate(rows_at):
            queries[j, head] = query[at]
            keys[j, head] = jnp.concatenate([k[at] for k in key], 0)
            values[j, head] = jnp.concatenate([v[at] for v in value], 0)
            betas[j, head] = beta_rows(beta[at], head, substeps)
    queries, keys, values, betas = (
        [held[u] for u in units_at] for held in (queries, keys, values, betas)
    )
    cum_rows = [
        jnp.concatenate([cum_col[rows_at[j], h : h + 1]] * substeps, 0) for j, h in units_at
    ]
    cum_cols = [cum_row[j, h : h + 1, :] for j, h in units_at]
    lasts = [c[:, BLOCK - 1 : BLOCK] for c in cum_cols]
    ratios = [jnp.exp(jnp.where(upto, a - b, -1e4)) for a, b in zip(cum_rows, cum_cols)]
    carries = [jnp.exp(c) for c in cum_rows]
    end_ratios = [jnp.exp(last - c) for last, c in zip(lasts, cum_rows)]
    inverses = [t_in[j, h] for j, h in units_at]
    d_mixes = [d_out[rows_at[j], h * width : (h + 1) * width] for j, h in units_at]
    states = [
        low(s_in[j, h].astype(F32) + product(p_in[j, h], state_in[h])) for j, h in units_at
    ]
    stacks = [jnp.concatenate([query, key], 0) for query, key in zip(queries, keys)]
    both_grams = [times_transposed(stack, key) for stack, key in zip(stacks, keys)]
    grams = [both[BLOCK:] for both in both_grams]
    masks = [low(ratio[:BLOCK] * both[:BLOCK]) for ratio, both in zip(ratios, both_grams)]
    d_both = [
        inner_rows(
            jnp.concatenate([mask, low(carry[:BLOCK] * query.astype(F32))], 1), d_mix
        )
        for mask, carry, query, d_mix in zip(masks, carries, queries, d_mixes)
    ]
    d_seen = [both[:rows] for both in d_both]
    d_reach = [both[rows:] for both in d_both]
    end_keys = [low(end * key.astype(F32)) for end, key in zip(end_ratios, keys)]
    start_keys = [
        low((beta_col * carry) * key.astype(F32))
        for beta_col, carry, key in zip(betas, carries, keys)
    ]
    freshes = [
        value.astype(F32) - carry * product(key, state)
        for value, carry, key, state in zip(values, carries, keys, states)
    ]
    updates = [
        low(product(inverse, low(beta_col * fresh)))
        for inverse, beta_col, fresh in zip(inverses, betas, freshes)
    ]
    laters_low, d_rights, d_rights_low = {}, {}, {}
    for j in range(PAIR - 1, -1, -1):
        ids = [j * head_count + h for h in heads]
        laters = [adjoint[h] for h in heads]
        for h, at in enumerate(ids):
            laters_low[at] = low(laters[h])
        d_updates = [low(d_seen[at] + product(end_keys[at], laters_low[at])) for at in ids]
        for h, at in enumerate(ids):
            d_rights[at] = inner_rows(inverses[at], d_updates[h])
            d_rights_low[at] = low(d_rights[at])
        for h, at in enumerate(ids):
            adjoint[h] = (
                jnp.exp(lasts[at]) * laters[h]
                + d_reach[at]
                - inner_rows(start_keys[at], d_rights_low[at])
            )
    ids = range(len(units_at))
    outer = [jnp.concatenate([d_mixes[at], d_rights_low[at]], 0) for at in ids]
    by_update = [times_transposed(outer[at], updates[at]) for at in ids]
    by_state = [times_transposed(outer[at], states[at]) for at in ids]
    d_systems = [
        jnp.where(earlier, -by_update[at][BLOCK:] * ratios[at], 0.0) for at in ids
    ]
    d_scores = [by_update[at][:BLOCK] * ratios[at][:BLOCK] for at in ids]
    d_grams = [betas[at] * d_systems[at] for at in ids]
    d_scores = [low(d_score) for d_score in d_scores]
    d_grams = [low(d_gram + jnp.transpose(d_gram)) for d_gram in d_grams]
    d_betas = [
        jnp.sum(d_rights[at] * freshes[at], axis=-1, keepdims=True)
        + jnp.sum(d_systems[at] * grams[at], axis=-1, keepdims=True)
        for at in ids
    ]
    d_queries = [
        carries[at][:BLOCK] * by_state[at][:BLOCK] + product(d_scores[at], keys[at])
        for at in ids
    ]
    d_keys = [
        inner_rows(jnp.concatenate([d_scores[at], d_grams[at]], 0), stacks[at])
        + end_ratios[at] * times_transposed(updates[at], laters_low[at])
        - (betas[at] * carries[at]) * by_state[at][BLOCK:]
        for at in ids
    ]
    for j in range(PAIR):
        logit_cols = []
        for h in heads:
            at = j * head_count + h
            logits = d_betas[at] * betas[at] * (1.0 - betas[at])
            logit_cols += [logits[n * BLOCK : (n + 1) * BLOCK] for n in range(substeps)]
        d_logit[rows_at[j], :] = jnp.concatenate(logit_cols, 1)

    for head in heads:
        mine = [j * head_count + head for j in range(PAIR)]
        step_rows = lambda arrays, n: jnp.concatenate(
            [array[n * BLOCK : (n + 1) * BLOCK] for array in arrays], 0
        )
        d_value = [betas[at] * d_rights[at] for at in mine]
        grads = [width ** (-0.5) * jnp.concatenate([d_queries[at] for at in mine], 0)]
        grads += [step_rows([d_keys[at] for at in mine], n) for n in range(substeps)]
        grads += [step_rows(d_value, n) for n in range(substeps)]
        for at, (start, size) in enumerate(pieces[head]):
            grad = grads[at]
            if at <= substeps:
                unit = units[head][at]
                grad = scales[head][at] * (
                    grad - unit * jnp.sum(grad * unit, axis=-1, keepdims=True)
                )
            grad = grad * silu_slope(pres[head][at], sigmas[head][at])
            windows = windows_of(start, size)[1]
            long = jnp.concatenate([grad, carried[:, start : start + size]], 0)
            tap = taps[:, start : start + size]
            spread = grad * tap[0:1]
            sums = [jnp.sum(grad * windows[0], axis=0, keepdims=True)]
            for offset in range(1, tap_count):
                masked = long * same_long[:, offset : offset + 1]
                spread = spread + (
                    pltpu.roll(masked, count + 8 - offset, 0)[:count] * tap[offset : offset + 1]
                )
                sums.append(jnp.sum(masked[:count] * windows[offset], axis=0, keepdims=True))
            carried[:, start : start + size] = grad[:8]
            tap_out[:, start : start + size] += jnp.concatenate(sums, 0)
            d_raw[:, start : start + size] = low(spread)
            tail_next[:, start : start + size] = spread[count - 8 :]

    @pl.when(step == 0)
    def _():
        tail_out[...] = tail_next[...]


def run_backward(
    begin, end, raw_q, edge_q, raw, edge, taps, same, beta, cum_col, cum_row, t_part, p_part,
    s_part, state_in, d_out, adjoint, carried, tap_grads, passed, head_count, substeps, width,
):
    count = raw.shape[0]
    columns = taps.shape[1]
    chunks = count // BLOCK
    rows = BLOCK * substeps
    begin, end, chunks = begin // PAIR, end // PAIR, chunks // PAIR
    per_halo = PAIR * BLOCK // HALO
    per_eight = PAIR * BLOCK // 8
    tokens = lambda cols: pl.BlockSpec((PAIR * BLOCK, cols), lambda c: (end - 1 - c, 0))
    halo = lambda cols: pl.BlockSpec(
        (HALO, cols), lambda c: (jnp.maximum((end - 1 - c) * per_halo - 1, 0), 0)
    )
    tiles = lambda *shape: pl.BlockSpec((PAIR, head_count) + shape, lambda c: (end - 1 - c, 0, 0, 0))
    anywhere = pl.BlockSpec(memory_space=pl.ANY)
    state = (head_count, width, width)
    sources = []
    for array in (raw_q, raw):
        cols = array.shape[1]
        sources += [tokens(cols), halo(cols), whole_spec(HALO, cols)]
    return pl.pallas_call(
        functools.partial(backward_kernel, head_count, substeps, width, end),
        grid=(end - begin,),
        in_specs=sources
        + [
            whole_spec(*taps.shape),
            tokens(same.shape[1]),
            pl.BlockSpec(
                (8, same.shape[1]),
                lambda c: (jnp.minimum((end - c) * per_eight, chunks * per_eight - 1), 0),
            ),
            tokens(beta.shape[1]),
            tokens(head_count),
            pl.BlockSpec((PAIR, head_count, rows), lambda c: (end - 1 - c, 0, 0)),
            tiles(rows, rows),
            tiles(width, width),
            tiles(width, width),
            whole_spec(*state),
            tokens(head_count * width),
            whole_spec(*state),
            whole_spec(8, columns),
            whole_spec(*taps.shape),
        ]
        + [anywhere] * len(passed),
        out_specs=[
            tokens(columns),
            tokens(head_count * substeps),
            whole_spec(8, columns),
            whole_spec(*state),
            whole_spec(8, columns),
            whole_spec(*taps.shape),
        ],
        out_shape=[
            jax.ShapeDtypeStruct((count, columns), BF16),
            jax.ShapeDtypeStruct((count, head_count * substeps), F32),
            jax.ShapeDtypeStruct((8, columns), F32),
            jax.ShapeDtypeStruct(state, F32),
            jax.ShapeDtypeStruct((8, columns), F32),
            jax.ShapeDtypeStruct(taps.shape, F32),
        ],
        scratch_shapes=[pltpu.VMEM((8, columns), F32)],
        input_output_aliases={20 + k: k for k in range(len(passed))},
        compiler_params=pltpu.CompilerParams(
            dimension_semantics=("arbitrary",), vmem_limit_bytes=VMEM_BYTES
        ),
        name="mixer_backward",
    )(
        raw_q, raw_q, edge_q, raw, raw, edge, taps, same, same, beta, cum_col, cum_row,
        t_part, p_part, s_part, state_in, d_out, adjoint, carried, tap_grads, *passed,
    )


def row_scale_of(values):
    return lax.rsqrt(jnp.mean(values * values, axis=-1, keepdims=True) + NORM_EPS)


def project_kernel(parts, raw_cols, inputs, edge, gain, *refs):
    weights, outs = refs[:parts], refs[parts:]
    normed_out, edge_normed, raw_out, edge_out, extra_out = outs
    gain_row = gain[...]

    def rows_of(values):
        values = values.astype(F32)
        return low(values * row_scale_of(values) * gain_row)

    def fill(normed, raw_ref, extra_ref):
        at = 0
        for weight in weights:
            cols = weight.shape[1]
            both = product(normed, weight[...])
            raw_part = min(cols, raw_cols - at)
            raw_ref[:, at : at + raw_part] = low(both[:, :raw_part])
            if extra_ref is not None and raw_part < cols:
                extra_ref[...] = jax.nn.sigmoid(both[:, raw_part:])
            at += cols

    normed = rows_of(inputs[...])
    normed_out[...] = normed
    fill(normed, raw_out, extra_out)

    @pl.when(pl.program_id(0) == 0)
    def _():
        normed_edge = rows_of(edge[...])
        edge_normed[...] = normed_edge
        fill(normed_edge, edge_out, None)


def once(shape):
    return pl.BlockSpec(shape, lambda *c: (0,) * len(shape), pipeline_mode=pl.Buffered(1))


def run_project(inputs, edge, gain, weights, raw_cols, extra):
    count, features = inputs.shape
    tile = min(TILE, count)
    tokens = lambda cols: pl.BlockSpec((tile, cols), lambda c: (c, 0))
    return pl.pallas_call(
        functools.partial(project_kernel, len(weights), raw_cols),
        grid=(count // tile,),
        in_specs=[tokens(features), whole_spec(HALO, features), whole_spec(1, features)]
        + [once(weight.shape) for weight in weights],
        out_specs=[
            tokens(features), whole_spec(HALO, features), tokens(raw_cols),
            whole_spec(HALO, raw_cols), tokens(extra),
        ],
        out_shape=[
            jax.ShapeDtypeStruct((count, features), BF16),
            jax.ShapeDtypeStruct((HALO, features), BF16),
            jax.ShapeDtypeStruct((count, raw_cols), BF16),
            jax.ShapeDtypeStruct((HALO, raw_cols), BF16),
            jax.ShapeDtypeStruct((count, extra), F32),
        ],
        compiler_params=pltpu.CompilerParams(
            dimension_semantics=("arbitrary",), vmem_limit_bytes=VMEM_BYTES
        ),
        name="project",
    )(inputs, edge, gain, *weights)


def project_side_kernel(normed, edge, query_w, gate_w, raw_out, edge_out, gate_out):
    raw_out[...] = low(product(normed[...], query_w[...]))
    gate_out[...] = product(normed[...], gate_w[...])

    @pl.when(pl.program_id(0) == 0)
    def _():
        edge_out[...] = low(product(edge[...], query_w[...]))


def run_project_side(normed, edge, query_w, gate_w):
    count, features = normed.shape
    cols = query_w.shape[1]
    tile = min(TILE, count)
    tokens = lambda cols: pl.BlockSpec((tile, cols), lambda c: (c, 0))
    return pl.pallas_call(
        project_side_kernel,
        grid=(count // tile,),
        in_specs=[
            tokens(features), whole_spec(HALO, features), once(query_w.shape), once(gate_w.shape)
        ],
        out_specs=[tokens(cols), whole_spec(HALO, cols), tokens(cols)],
        out_shape=[
            jax.ShapeDtypeStruct((count, cols), BF16),
            jax.ShapeDtypeStruct((HALO, cols), BF16),
            jax.ShapeDtypeStruct((count, cols), F32),
        ],
        compiler_params=pltpu.CompilerParams(
            dimension_semantics=("arbitrary",), vmem_limit_bytes=VMEM_BYTES
        ),
        name="project_side",
    )(normed, edge, query_w, gate_w)


def heads_kernel(
    head_count, width,
    local, reach, state, gate, gain, weight,
    mixer_out, heads_out, own_out, low_out,
):
    gain_row = gain[...]
    for h in range(head_count):
        at = slice(h * width, (h + 1) * width)
        mixer = local[:, at] + product(reach[:, at], state[h])
        logit = gate[:, at]
        mixer_out[:, at] = mixer
        heads_out[:, at] = low(
            mixer * row_scale_of(mixer) * gain_row * (logit * jax.nn.sigmoid(logit))
        )
    branch = times_transposed(heads_out[...], weight[...])
    own_out[...] = branch
    low_out[...] = low(branch)


def run_heads(local, reach, state, gate, gain, weight, head_count, width):
    count, cols = local.shape
    features = weight.shape[0]
    tile = min(TILE, count)
    tokens = lambda cols: pl.BlockSpec((tile, cols), lambda c: (c, 0))
    return pl.pallas_call(
        functools.partial(heads_kernel, head_count, width),
        grid=(count // tile,),
        in_specs=[
            tokens(cols), tokens(cols), whole_spec(*state.shape), tokens(cols),
            whole_spec(*gain.shape), once(weight.shape),
        ],
        out_specs=[tokens(cols), tokens(cols), tokens(features), tokens(features)],
        out_shape=[
            jax.ShapeDtypeStruct((count, cols), F32),
            jax.ShapeDtypeStruct((count, cols), BF16),
            jax.ShapeDtypeStruct((count, features), F32),
            jax.ShapeDtypeStruct((count, features), BF16),
        ],
        compiler_params=pltpu.CompilerParams(
            dimension_semantics=("arbitrary",), vmem_limit_bytes=VMEM_BYTES
        ),
        name="heads",
    )(local, reach, state, gate, gain, weight)


def lay_copies(view, other, own, short, rows, scratch, semaphores):
    run = short * rows
    copies = []
    for block in range(view.shape[0] // run):
        for side, at in ((view, own), (other, 1 - own)):
            row = pl.multiple_of((2 * block + at) * run, run)
            copies.append(
                pltpu.make_async_copy(
                    side.at[pl.ds(block * run, run)],
                    scratch.at[pl.ds(row, run)],
                    semaphores.at[len(copies)],
                )
            )
    return copies


def feed_kernel(runs, rows, me, inputs, own, other, gain, cotangent, *refs):
    halves, outs, rest = refs[:6], refs[6:14], refs[14:]
    hidden_out, normed_out, act_out, d_gate_out, d_up_out, branch_out, own_out, low_out = outs
    gate_w, up_w, down_w = rest[:3]

    @pl.when(pl.program_id(0) == 0)
    def _():
        copies = []
        for k, short in enumerate(runs):
            copies += lay_copies(
                halves[2 * k], halves[2 * k + 1], (me[0] // short) % 2, short, rows, rest[k],
                rest[3 + k],
            )
        for copy in copies:
            copy.start()
        for copy in copies:
            copy.wait()

    hidden = inputs[...].astype(F32) + own[...] + other[...].astype(F32)
    hidden_out[...] = hidden
    normed = low(hidden * row_scale_of(hidden) * gain[...])
    normed_out[...] = normed
    gate = product(normed, gate_w[...])
    up = product(normed, up_w[...])
    d_act = product(cotangent[...], down_w[...])
    sigma = jax.nn.sigmoid(gate)
    act = gate * sigma
    activation = low(act * up)
    d_up = low(d_act * act)
    d_gate = low(d_act * up * silu_slope(gate, sigma))
    act_out[...] = activation
    d_gate_out[...] = d_gate
    d_up_out[...] = d_up
    branch_out[...] = low(times_transposed(activation, down_w[...]))
    d_normed = times_transposed(d_gate, gate_w[...]) + times_transposed(d_up, up_w[...])
    own_out[...] = d_normed
    low_out[...] = low(d_normed)


def run_feed(inputs, own, other, gain, cotangent, views, others, distances):
    rows = views[0].shape[-2]
    if rows < HALO:
        full = gather_end([gather_join(*part) for part in zip(views, others, distances)])
        half = full[0].shape[0] // 2
        views, others = [w[:half] for w in full], [w[half:] for w in full]
        distances, rows, me = [1] * 3, half, jnp.zeros((1,), jnp.int32)
    else:
        views, others = gather_end(views), gather_end(others)
        me = lax.axis_index("seq").astype(jnp.int32).reshape(1)
    halves = [half for pair in zip(views, others) for half in pair]
    count, features = inputs.shape
    cols = views[0].shape[1]
    tile = min(TILE, count)
    tokens = lambda cols: pl.BlockSpec((tile, cols), lambda c: (c, 0))
    shape = lambda cols, kind: jax.ShapeDtypeStruct((count, cols), kind)
    return pl.pallas_call(
        functools.partial(feed_kernel, distances, rows),
        grid=(count // tile,),
        in_specs=[pl.BlockSpec(memory_space=pltpu.SMEM)]
        + [tokens(features)] * 3
        + [whole_spec(1, features), tokens(features)]
        + [pl.BlockSpec(memory_space=pl.ANY)] * 6,
        scratch_shapes=[pltpu.VMEM((2 * view.shape[0], cols), BF16) for view in views]
        + [
            pltpu.SemaphoreType.DMA((2 * (view.shape[0] // (short * rows)),))
            for view, short in zip(views, distances)
        ],
        out_specs=[tokens(features)] * 2 + [tokens(cols)] * 3 + [tokens(features)] * 3,
        out_shape=[shape(features, F32), shape(features, BF16)]
        + [shape(cols, BF16)] * 3
        + [shape(features, BF16), shape(features, F32), shape(features, BF16)],
        compiler_params=pltpu.CompilerParams(
            dimension_semantics=("arbitrary",), vmem_limit_bytes=VMEM_BYTES
        ),
        name="feed",
    )(me, inputs, own, other, gain, cotangent, *halves)


def turn_kernel(
    head_count, width,
    hidden, own, other, gain, cotangent, weight, mixer_in, gate, head_gain, reach,
    d_hidden_out, d_low_out, d_gate_out, d_mixer_out, state_out, feed_gain_out, head_gain_out,
):
    @pl.when(pl.program_id(0) == 0)
    def _():
        state_out[...] = jnp.zeros(state_out.shape, F32)
        feed_gain_out[...] = jnp.zeros(feed_gain_out.shape, F32)
        head_gain_out[...] = jnp.zeros(head_gain_out.shape, F32)

    d_normed = own[...] + other[...].astype(F32)
    back, terms = norm_back(hidden[...], gain[...], d_normed)
    feed_gain_out[...] += jnp.sum(terms, axis=0, keepdims=True)
    d_hidden = cotangent[...].astype(F32) + back
    d_hidden_out[...] = d_hidden
    d_low = low(d_hidden)
    d_low_out[...] = d_low
    d_heads = product(d_low, weight[...])
    gain_row = head_gain[...]
    for h in range(head_count):
        at = slice(h * width, (h + 1) * width)
        mixer = mixer_in[:, at]
        unit = mixer * row_scale_of(mixer)
        logit = gate[:, at]
        sigma = jax.nn.sigmoid(logit)
        d_head = d_heads[:, at]
        d_gate_out[:, at] = low(d_head * (unit * gain_row) * silu_slope(logit, sigma))
        d_mixer, head_terms = norm_back(mixer, gain_row, d_head * (logit * sigma))
        head_gain_out[...] += jnp.sum(head_terms, axis=0, keepdims=True)
        d_mixer_low = low(d_mixer)
        d_mixer_out[:, at] = d_mixer_low
        state_out[h] += inner_rows(reach[:, at], d_mixer_low)


def run_turn(
    hidden, own, other, gain, cotangent, weight, mixer, gate, head_gain, reach, head_count, width
):
    count, features = hidden.shape
    cols = mixer.shape[1]
    tile = min(TILE, count)
    tokens = lambda cols: pl.BlockSpec((tile, cols), lambda c: (c, 0))
    shape = lambda cols, kind: jax.ShapeDtypeStruct((count, cols), kind)
    state = (head_count, width, width)
    return pl.pallas_call(
        functools.partial(turn_kernel, head_count, width),
        grid=(count // tile,),
        in_specs=[tokens(features)] * 3
        + [whole_spec(1, features), tokens(features), once(weight.shape)]
        + [tokens(cols), tokens(cols), whole_spec(1, width), tokens(cols)],
        out_specs=[tokens(features)] * 2
        + [tokens(cols)] * 2
        + [whole_spec(*state), whole_spec(1, features), whole_spec(1, width)],
        out_shape=[shape(features, F32), shape(features, BF16)]
        + [shape(cols, BF16)] * 2
        + [
            jax.ShapeDtypeStruct(state, F32),
            jax.ShapeDtypeStruct((1, features), F32),
            jax.ShapeDtypeStruct((1, width), F32),
        ],
        compiler_params=pltpu.CompilerParams(
            dimension_semantics=("arbitrary",), vmem_limit_bytes=VMEM_BYTES
        ),
        name="turn",
    )(hidden, own, other, gain, cotangent, weight, mixer, gate, head_gain, reach)


def back_project_kernel(extra, inputs, d_raw, d_extra, d_gate, query_w, gate_w, *refs):
    weights, (out, gain_out) = refs[:-2], refs[-2:]
    at = query_w.shape[1]
    total = times_transposed(d_raw[:, :at], query_w[...])
    for k, weight in enumerate(weights):
        size = weight.shape[1] - (extra if k == len(weights) - 1 else 0)
        total += times_transposed(d_raw[:, at : at + size], weight[:, :size])
        at += size
    total += times_transposed(d_extra[...], weights[-1][:, -extra:])
    total += times_transposed(d_gate[...], gate_w[...])
    total = low(total)
    out[...] = total

    @pl.when(pl.program_id(0) == 0)
    def _():
        gain_out[...] = jnp.zeros(gain_out.shape, F32)

    values = inputs[...].astype(F32)
    gain_out[...] += jnp.sum(
        total.astype(F32) * (values * row_scale_of(values)), axis=0, keepdims=True
    )


def run_back_project(inputs, d_raw, d_extra, d_gate, weights):
    count, features = inputs.shape
    tile = min(TILE, count)
    tokens = lambda cols: pl.BlockSpec((tile, cols), lambda c: (c, 0))
    return pl.pallas_call(
        functools.partial(back_project_kernel, d_extra.shape[1]),
        grid=(count // tile,),
        in_specs=[tokens(array.shape[1]) for array in (inputs, d_raw, d_extra, d_gate)]
        + [once(weight.shape) for weight in weights],
        out_specs=[tokens(features), whole_spec(1, features)],
        out_shape=[
            jax.ShapeDtypeStruct((count, features), BF16),
            jax.ShapeDtypeStruct((1, features), F32),
        ],
        compiler_params=pltpu.CompilerParams(
            dimension_semantics=("arbitrary",), vmem_limit_bytes=VMEM_BYTES
        ),
        name="back_project",
    )(inputs, d_raw, d_extra, d_gate, *weights)


def shift_seq(array, by):
    count = lax.axis_size("seq")
    return lax.ppermute(
        array, "seq", [(i, i + by) for i in range(count) if 0 <= i + by < count]
    )


def swap_seq(array, distance):
    return lax.ppermute(array, "seq", [(i, i ^ distance) for i in range(lax.axis_size("seq"))])


def swap_head(array):
    return lax.ppermute(array, "head", [(0, 1), (1, 0)])


def head_sum(array):
    return array + swap_head(array)


def fine_low(form, former, latter):
    high, rest = split(former)
    return form(high, latter) + form(rest, latter)


def fine_first(form, former, latter):
    high, rest = split(latter)
    return form(former, high) + form(former, rest)


def join_kernel(final, upper, group, other, before, group_out, low_out, before_out):
    heads, width, _ = group.shape

    @pl.when(upper[0] == 1)
    def _():
        for head in range(heads):
            theirs = other[head]
            reach = fine_low(product, before[head, :, :width], theirs)
            before_out[head, :, :width] = reach[:, :width]
            before_out[head, :, width:] = reach[:, width:] + before[head, :, width:]
            if not final:
                mine = fine_low(product, group[head, :, :width], theirs)
                group_out[head, :, :width] = mine[:, :width]
                group_out[head, :, width:] = mine[:, width:] + group[head, :, width:]

    @pl.when(upper[0] == 0)
    def _():
        before_out[...] = before[...]
        if not final:
            for head in range(heads):
                theirs = other[head]
                mine = fine_first(product, theirs[:, :width], group[head])
                group_out[head, :, :width] = mine[:, :width]
                group_out[head, :, width:] = mine[:, width:] + theirs[:, width:].astype(F32)

    low_out[...] = low(group_out[...]) if not final else low(before_out[...])


def join_groups(final, upper, group, other, before):
    whole = pl.BlockSpec(memory_space=pltpu.VMEM)
    full = jax.ShapeDtypeStruct(group.shape, F32)
    return pl.pallas_call(
        functools.partial(join_kernel, final),
        in_specs=[pl.BlockSpec(memory_space=pltpu.SMEM), whole, whole, whole],
        out_specs=[whole, whole, whole],
        out_shape=[full, jax.ShapeDtypeStruct(group.shape, BF16), full],
        compiler_params=pltpu.CompilerParams(vmem_limit_bytes=VMEM_BYTES),
        name="join_groups",
    )(upper, group, other, before)


def back_kernel(final, upper, group, other, after, group_map, other_map, after_map, *outs):
    group_out, low_out, after_out, after_map_out = outs
    heads, width, _ = group.shape
    after_out[...] = after[...]
    after_map_out[...] = after_map[...]
    if final:
        group_out[...] = group[...]

    @pl.when(upper[0] == 1)
    def _():
        if not final:
            for head in range(heads):
                theirs = other_map[head, :, :width]
                group_out[head] = other[head].astype(F32) + fine_first(
                    inner_rows, theirs, group[head]
                )

    @pl.when(upper[0] == 0)
    def _():
        for head in range(heads):
            theirs = other[head]
            after_out[head] += fine_low(inner_rows, after_map[head], theirs)
            if not final:
                group_out[head] = group[head] + fine_low(
                    inner_rows, group_map[head, :, :width], theirs
                )
                after_map_out[head] = fine_first(
                    product, other_map[head, :, :width], after_map[head]
                )

    low_out[...] = low(group_out[...])


def join_back(final, upper, group, other, after, group_map, other_map, after_map):
    whole = pl.BlockSpec(memory_space=pltpu.VMEM)
    full = jax.ShapeDtypeStruct(group.shape, F32)
    return pl.pallas_call(
        functools.partial(back_kernel, final),
        in_specs=[pl.BlockSpec(memory_space=pltpu.SMEM)] + [whole] * 6,
        out_specs=[whole] * 4,
        out_shape=[full, jax.ShapeDtypeStruct(group.shape, BF16), full, full],
        compiler_params=pltpu.CompilerParams(vmem_limit_bytes=VMEM_BYTES),
        name="join_back",
    )(upper, group, other, after, group_map, other_map, after_map)


def states_before(group, eye, beside):
    count, mine = lax.axis_size("seq"), lax.axis_index("seq")
    before = jnp.concatenate([eye, jnp.zeros_like(eye)], 2)
    group_low = low(group)
    kept = []
    distance = 1
    while distance < count:
        other = swap_seq(group_low, distance)
        if distance in beside:
            other, _ = tied(other, beside[distance]())
        upper = ((mine // distance) % 2).astype(jnp.int32).reshape(1)
        kept.append((group, other, upper))
        final = 2 * distance >= count
        group, group_low, before = join_groups(final, upper, group, other, before)
        distance *= 2
    return group_low[:, :, group.shape[1] :], kept


def adjoints_after(own, kept, eye):
    group, group_low = own, low(own)
    after, after_map = jnp.zeros_like(own), eye
    distance = 1
    for group_map, other_map, upper in kept:
        other = swap_seq(group_low, distance)
        final = 2 * distance >= lax.axis_size("seq")
        group, group_low, after, after_map = join_back(
            final, upper, group, other, after, group_map, other_map, after_map
        )
        distance *= 2
    return after


def bit_orders(count):
    distances = [1 << k for k in range(count.bit_length() - 1)]
    near, far = distances[:3], distances[3:]
    return [near[k:] + near[:k] for k in range(len(near))], far


def scatter_view(array):
    count = lax.axis_size("seq")
    bits = count.bit_length() - 1
    return array.reshape((2,) * bits + (array.shape[0] // count, array.shape[1]))


def swap_all(arrays, distances):
    return [swap_seq(array, distance) for array, distance in zip(arrays, distances)]


def halve_all(terms, distances):
    keeps, sends = [], []
    for arrays, distance in zip(terms, distances):
        axis = arrays[0].ndim - 2 - distance.bit_length()
        own = (lax.axis_index("seq") // distance) % 2
        cut = lambda array, at: lax.dynamic_slice_in_dim(array, at, 1, axis).astype(F32)
        keeps.append(low(functools.reduce(jnp.add, [cut(array, own) for array in arrays])))
        sends.append(low(functools.reduce(jnp.add, [cut(array, 1 - own) for array in arrays])))
    return keeps, sends


def block_at(me, q, have, free, flipped):
    index, left = 0, len(free)
    for distance in have:
        if distance in free:
            left -= 1
            digit = (q // (1 << left)) % 2
        else:
            digit = (me // distance) % 2
            digit = 1 - digit if distance == flipped else digit
        index = index * 2 + digit
    return index


def halve_kernel(counts, me, *refs):
    ins, outs = refs[: 2 * sum(counts)], refs[2 * sum(counts) :]
    for part, count in enumerate(counts):
        for side in range(2):
            total = ins[0][...].astype(F32)
            for ref in ins[1:count]:
                total = total + ref[...].astype(F32)
            outs[2 * part + side][...] = low(total)
            ins = ins[count:]


def halve_parts(terms, haves, distances):
    rows = terms[0][0].shape[-2]
    arrays, specs, out_specs, shapes = [], [], [], []
    blocks = 1 << (min(len(have) for have in haves[0]) - 1)
    for part, part_haves, distance in zip(terms, haves, distances):
        free = [d for d in min(part_haves, key=len) if d != distance]
        columns = part[0].shape[-1]
        for flipped in (None, distance):
            for array, have in zip(part, part_haves):
                arrays.append(array.reshape(-1, columns))
                specs.append(
                    pl.BlockSpec(
                        (rows, columns),
                        lambda q, me, have=have, free=free, flipped=flipped: (
                            block_at(me[0], q, have, free, flipped), 0
                        ),
                    )
                )
            out_specs.append(pl.BlockSpec((rows, columns), lambda q, me: (q, 0)))
            shapes.append(jax.ShapeDtypeStruct((blocks * rows, columns), BF16))
    outs = pl.pallas_call(
        functools.partial(halve_kernel, [len(part) for part in terms]),
        grid_spec=pltpu.PrefetchScalarGridSpec(
            num_scalar_prefetch=1, grid=(blocks,), in_specs=specs, out_specs=out_specs
        ),
        out_shape=shapes,
        compiler_params=pltpu.CompilerParams(
            dimension_semantics=("arbitrary",), vmem_limit_bytes=VMEM_BYTES
        ),
        name="halve",
    )(lax.axis_index("seq").astype(jnp.int32).reshape(1), *arrays)
    return outs[0::2], outs[1::2]


def far_steps(terms, distances):
    for distance in distances:
        keeps, sends = halve_all(terms, [distance] * len(terms))
        merged = swap_seq(jnp.concatenate(sends, -1), distance)
        others, start = [], 0
        for send in sends:
            wide = send.shape[-1]
            others.append(lax.slice_in_dim(merged, start, start + wide, axis=merged.ndim - 1))
            start += wide
        terms = list(zip(keeps, others))
    return [
        functools.reduce(jnp.add, [a.astype(F32) for a in arrays]).reshape(arrays[0].shape[-2:])
        for arrays in terms
    ]


def gather_join(view, other, distance):
    axis = view.ndim - 2 - distance.bit_length()
    upper = (lax.axis_index("seq") // distance) % 2 == 1
    return jnp.concatenate(
        [jnp.where(upper, other, view), jnp.where(upper, view, other)], axis
    )


def lay_kernel(distances, me, *refs):
    parts = len(distances)
    for k, distance in enumerate(distances):
        upper = (me[0] // distance) % 2 == 1
        view, other, out = refs[2 * k], refs[2 * k + 1], refs[2 * parts + k]
        out[:, 0] = jnp.where(upper, other[...], view[...])
        out[:, 1] = jnp.where(upper, view[...], other[...])


def gather_lay(views, others, distances):
    rows = views[0].shape[-2]
    if rows < HALO:
        return [gather_join(*part) for part in zip(views, others, distances)]
    arrays, specs, out_specs, shapes, full = [], [], [], [], []
    for view, other, distance in zip(views, others, distances):
        axis = view.ndim - 2 - distance.bit_length()
        before, after = view.shape[:axis], view.shape[axis + 1 :]
        high = functools.reduce(lambda a, b: a * b, before, 1)
        short = functools.reduce(lambda a, b: a * b, after[:-2], 1)
        columns = view.shape[-1]
        group = max(1, high * short // 4)
        near_rows, far_rows = min(short, group), max(1, group // short)
        steps = short // near_rows
        place = lambda q, me, steps=steps: (q // steps, q % steps, 0, 0)
        specs += [pl.BlockSpec((far_rows, near_rows, rows, columns), place)] * 2
        out_specs.append(
            pl.BlockSpec(
                (far_rows, 2, near_rows, rows, columns),
                lambda q, me, steps=steps: (q // steps, 0, q % steps, 0, 0),
            )
        )
        arrays += [array.reshape(high, short, rows, columns) for array in (view, other)]
        shapes.append(jax.ShapeDtypeStruct((high, 2, short, rows, columns), BF16))
        full.append(before + (2,) + after)
        blocks = high * short // group
    outs = pl.pallas_call(
        functools.partial(lay_kernel, distances),
        grid_spec=pltpu.PrefetchScalarGridSpec(
            num_scalar_prefetch=1, grid=(blocks,), in_specs=specs, out_specs=out_specs
        ),
        out_shape=shapes,
        compiler_params=pltpu.CompilerParams(
            dimension_semantics=("arbitrary",), vmem_limit_bytes=VMEM_BYTES
        ),
        name="lay",
    )(lax.axis_index("seq").astype(jnp.int32).reshape(1), *arrays)
    return [out.reshape(shape) for out, shape in zip(outs, full)]


def gather_far(pack, distances):
    bits = lax.axis_size("seq").bit_length() - 1
    view = pack.reshape((1,) * bits + pack.shape)
    for distance in distances[::-1]:
        view = gather_join(view, swap_seq(view, distance), distance)
    return view


def gather_cut(view, widths):
    parts, at = [], 0
    for wide in widths:
        parts.append(lax.slice_in_dim(view, at, at + wide, axis=view.ndim - 1))
        at += wide
    return parts


def gather_end(views):
    return [view.reshape(-1, view.shape[-1]) for view in views]


def tied(*values):
    return lax.optimization_barrier(values)


def per_device(
    activations,
    log_decay,
    doc_starts,
    query_weight,
    key_weight,
    value_weight,
    beta_weight,
    gate_weight,
    out_weight,
    query_taps,
    key_taps,
    value_taps,
    mixer_gain,
    head_gain,
    feed_gain,
    feed_gate,
    feed_up,
    feed_down,
    cotangent,
):
    count, features = activations.shape
    tap_count = query_taps.shape[0]
    width = head_gain.shape[0]
    query_cols = query_weight.shape[1]
    key_cols = key_weight.shape[1]
    conv_cols = query_cols + 2 * key_cols
    hidden_cols = feed_gate.shape[1]
    head_count = query_cols // width
    beta_cols = beta_weight.shape[1]
    substeps = beta_cols // head_count
    device_rank = lax.axis_index("seq")
    head_rank = lax.axis_index("head")
    extra = 128
    shard_rows = query_weight.shape[0]
    orders, far = bit_orders(lax.axis_size("seq"))
    at_step = lambda k: [order[k] for order in orders]
    gather_at = lambda k: [order[2 - k] for order in orders]
    pad = jnp.zeros((shard_rows, extra - beta_cols - 2), BF16)
    kv_pack = jnp.concatenate(
        [key_weight, value_weight, beta_weight, mixer_gain[:, None], feed_gain[:, None], pad], 1
    )
    side_pack = jnp.concatenate([query_weight, gate_weight, out_weight.T], 1)
    feed_pack = jnp.concatenate([feed_gate, feed_up, feed_down.T], 1)
    third = -(-kv_pack.shape[1] // (3 * width)) * width
    input_edge = shift_seq(activations[count - HALO :], 1)
    kv_view = gather_far(kv_pack, far)
    kv_view, side_pack = tied(kv_view, side_pack)
    kv_parts = gather_cut(kv_view, [third, third, kv_pack.shape[1] - 2 * third])
    side_view = gather_far(side_pack, far)
    for k in range(3):
        others = swap_all(kv_parts, gather_at(k))
        kv_parts = [gather_join(v, o, d) for v, o, d in zip(kv_parts, others, gather_at(k))]
    side_parts = gather_cut(side_view, [query_cols] * 3)
    weights_kv = gather_end(kv_parts)
    weights_kv, side_parts, feed_pack, input_edge = tied(
        weights_kv, side_parts, feed_pack, input_edge
    )
    gains = weights_kv[2][:, -extra + beta_cols : -extra + beta_cols + 2].T.astype(F32)
    gain_one, gain_two = gains[0:1], gains[1:2]

    token_position = device_rank * count + jnp.arange(count, dtype=jnp.int32)
    is_start = jnp.any(token_position[:, None] == doc_starts[None, :], axis=1)

    def same_docs(position):
        doc = lambda p: jnp.sum((p[:, None] >= doc_starts[None, :]).astype(jnp.int32), axis=1)
        own = doc(position)
        return jnp.stack(
            [
                ((doc(position - offset) == own) & (position >= offset)).astype(F32)
                for offset in range(tap_count)
            ],
            1,
        )

    same = same_docs(token_position)
    log_gate = log_decay - RESET * is_start.astype(F32)[:, None]
    chunks = count // BLOCK
    cumulative = jnp.cumsum(log_gate.reshape(chunks, BLOCK, head_count), axis=1)
    cum_col = cumulative.reshape(count, head_count)
    cum_row = jnp.concatenate([jnp.swapaxes(cumulative, 1, 2)] * substeps, 2)
    taps_all = jnp.concatenate([query_taps, key_taps, value_taps], 1).astype(F32)

    side_others = swap_all(side_parts, gather_at(0))
    feed_view = gather_far(feed_pack, far)
    normed, edge_normed, raw_kv, edge_kv, sigmas = run_project(
        activations, input_edge, gain_one, weights_kv, 2 * key_cols, extra
    )
    beta_gate = sigmas[:, :beta_cols]
    eye = jnp.broadcast_to(jnp.eye(width, dtype=F32), (head_count, width, width))
    chain = jnp.concatenate([eye, jnp.zeros_like(eye)], 2)
    passed = ()
    feed_parts = None
    side_at, feed_at = 1, 0
    sides = [gather_join(v, o, d) for v, o, d in zip(side_parts, side_others, gather_at(0))]
    marks = [(chunks * k) // (AHEAD_CALLS * PAIR) * PAIR for k in range(AHEAD_CALLS + 1)]
    sends, distances = sides, gather_at(1)
    for call in range(AHEAD_CALLS):
        chain, sends = tied(chain, sends)
        others = swap_all(sends, distances)
        *passed, chain = run_forward(
            marks[call], marks[call + 1], raw_kv, edge_kv, taps_all, same, beta_gate, cum_col,
            cum_row, chain, tuple(passed), head_count, substeps, width,
        )
        if call == 0:
            chain, others, feed_view = tied(chain, others, feed_view)
        else:
            chain, others = tied(chain, others)
        sided = 3 if call < 2 else 0
        joined = [
            gather_join(v, o, d)
            for v, o, d in zip(sends[:sided], others[:sided], distances[:sided])
        ]
        if call > 0:
            joined += gather_lay(sends[sided:], others[sided:], distances[sided:])
        if call == 0:
            feed_parts = gather_cut(feed_view, [hidden_cols] * 3)
            sends, distances = joined + feed_parts, gather_at(2) + gather_at(0)
        elif call == 1:
            sides, sends, distances = joined[:3], joined[3:], gather_at(1)
        else:
            feed_parts = joined
    t_part, p_part, s_part, key_rows, solved = passed
    weight_query, weight_gate, weight_out = gather_end(sides)

    held = {}

    def first():
        held["side"] = run_project_side(normed, edge_normed, weight_query, weight_gate)
        return held["side"]

    state_low, kept = states_before(chain, eye, {2: first})
    raw_query, edge_query, gate_view = held["side"]
    state_low, feed_parts = tied(state_low, feed_parts)
    others = swap_all(feed_parts, gather_at(2))
    q_reach, local_out = run_query(
        raw_query, edge_query, taps_all[:, :query_cols], same, cum_col, cum_row, key_rows, solved,
        p_part, s_part, head_count, substeps, width,
    )
    head_gain_row = head_gain.astype(F32)[None]
    mixer_out, heads_out, branch_own, branch_low = run_heads(
        local_out, q_reach, state_low, gate_view, head_gain_row, weight_out, head_count, width
    )
    branch_low, others = tied(branch_low, others)
    (
        hidden, normed_ffn, activation, d_gate, d_up, branch_two, d_normed_own, d_normed_low,
    ) = run_feed(
        activations, branch_own, swap_head(branch_low), gain_two, cotangent,
        feed_parts, others, gather_at(2),
    )
    half = features // lax.axis_size("head")
    own_half = lambda array: lax.dynamic_slice_in_dim(array, head_rank * half, half, 1)
    other_half = lambda array: lax.dynamic_slice_in_dim(array, (1 - head_rank) * half, half, 1)
    output = low(
        own_half(hidden)
        + own_half(branch_two).astype(F32)
        + swap_head(other_half(branch_two)).astype(F32)
    )

    near = orders[0]
    grad_orders = [
        [near[1], near[2], near[0]],
        [near[0], near[1], near[2]],
        [near[2], near[0], near[1]],
        [near[2], near[0], near[1]],
        [near[2], near[1], near[0]],
    ]
    down_grad = scatter_view(low(inner_rows(cotangent, activation)))
    _, down_send = halve_all([(down_grad,)], [grad_orders[2][0]])
    d_normed_other, down_send = tied(swap_head(d_normed_low), down_send)
    down_other = swap_all(down_send, [grad_orders[2][0]])[0]
    (
        d_hidden, grad_mixer, d_gate_logit, d_mixer_low, own_part, grad_feed_gain, head_gain_part,
    ) = run_turn(
        hidden, d_normed_own, d_normed_other, gain_two, cotangent, weight_out,
        mixer_out, gate_view, head_gain_row, q_reach, head_count, width,
    )
    grad_feed_gain, head_gain_part = grad_feed_gain[0], head_gain_part[0]
    adjoint = adjoints_after(own_part, kept, eye)
    terms = [
        (scatter_view(low(inner_rows(normed_ffn, d_gate))),),
        (scatter_view(low(inner_rows(normed_ffn, d_up))),),
        (scatter_view(low(inner_rows(grad_mixer, heads_out))),),
        (scatter_view(low(inner_rows(normed, d_gate_logit))),),
    ]
    down_other, adjoint = tied(down_other, adjoint)
    marks = [chunks, (3 * chunks // 8) // PAIR * PAIR, (chunks // 8) // PAIR * PAIR, 0]
    carried = jnp.zeros((8, conv_cols), F32)
    tap_grads = jnp.zeros((tap_count, conv_cols), F32)
    passed = ()
    every = [1 << k for k in range(lax.axis_size("seq").bit_length() - 1)][::-1]
    left = [every] * 5
    haves = [[every]] * 5
    down_terms = (down_grad, down_other)
    bits = len(every)
    for call in range(3):
        distances = [order[call] for order in grad_orders]
        if call == 0:
            kinds = [0, 1, 3, 4]
            sends = halve_all(terms, [distances[k] for k in kinds])[1]
            keeps = [part[0] for part in terms]
            distances = [distances[k] for k in kinds]
        elif shard_rows < HALO:
            views = [
                (
                    [array.reshape((2,) * len(have) + array.shape[-2:]) for array, have in zip(*p)],
                    p[1],
                )
                for p in zip(terms, haves)
            ]
            sums = []
            for part, part_haves in views:
                small_have = min(part_haves, key=len)
                total = None
                for array, have in zip(part, part_haves):
                    for axis, d in reversed(list(enumerate(have))):
                        if d not in small_have:
                            array = lax.dynamic_index_in_dim(
                                array, (lax.axis_index("seq") // d) % 2, axis, keepdims=False
                            )
                    array = array.astype(F32)
                    total = array if total is None else total + array
                sums.append((total, small_have))
            keeps, sends = [], []
            for (total, have), d in zip(sums, distances):
                own = (lax.axis_index("seq") // d) % 2
                columns = total.shape[-1]
                pick = lambda at: low(
                    lax.dynamic_index_in_dim(total, at, have.index(d), keepdims=False)
                ).reshape(-1, columns)
                keeps.append(pick(own))
                sends.append(pick(1 - own))
        else:
            keeps, sends = halve_parts(terms, haves, distances)
        adjoint, sends, keeps = tied(adjoint, sends, keeps)
        others = swap_all(sends, distances)
        d_raw, d_beta_logit, new_tail, adjoint, carried, tap_grads = run_backward(
            marks[call + 1], marks[call],
            raw_query, edge_query, raw_kv, edge_kv, taps_all, same, beta_gate, cum_col, cum_row,
            t_part, p_part, s_part, state_low, d_mixer_low, adjoint, carried, tap_grads, passed,
            head_count, substeps, width,
        )
        if call == 0:
            tail = new_tail
        adjoint, carried, others = tied(adjoint, carried, others)
        passed = (d_raw, d_beta_logit)
        terms = [
            (k.reshape(-1, k.shape[-1]), o.reshape(-1, o.shape[-1])) for k, o in zip(keeps, others)
        ]
        if call == 0:
            down = tuple(array.reshape(-1, array.shape[-1]) for array in down_terms)
            terms = terms[:2] + [down] + terms[2:]
        left = [[d for d in l if d != order[call]] for l, order in zip(left, grad_orders)]
        haves = [[every if call == 0 else l, l] for l in left]
        cube = lambda a: a.reshape(-1, shard_rows, a.shape[-1])
        terms = [tuple(cube(a) for a in part) for part in terms]
    ones = (1,) * (bits - len(far))
    terms = [
        tuple(a.reshape((2,) * len(far) + ones + (shard_rows, a.shape[-1])) for a in part)
        for part in terms
    ]
    first_rows = carried
    zh_keeps, zh_sends = halve_all(terms, [far[0]] * len(terms))
    zh_other = swap_seq(jnp.concatenate(zh_sends, -1), far[0])
    returned = shift_seq(first_rows, -1)
    same_after = same_docs(token_position[-1] + 1 + jnp.arange(8, dtype=jnp.int32))
    spread = jnp.zeros_like(tail)
    for offset in range(1, tap_count):
        masked = returned * same_after[:, offset : offset + 1] * taps_all[offset]
        spread = spread + jnp.pad(masked[:offset], ((8 - offset, 0), (0, 0)))
    d_raw = lax.dynamic_update_slice(d_raw, low(tail + spread), (count - 8, 0))
    d_beta_low = low(d_beta_logit)
    fifth = -(-conv_cols // (5 * width)) * width
    conv_marks = [0, 2 * fifth, 4 * fifth, conv_cols]
    keeps, sends = halve_all(
        [
            (scatter_view(low(inner_rows(normed, d_raw[:, a:b]))),)
            for a, b in zip(conv_marks[:-1], conv_marks[1:])
        ],
        at_step(0),
    )
    d_raw, d_beta_low, sends, keeps = tied(d_raw, d_beta_low, sends, keeps)
    others = swap_all(sends, at_step(0))
    d_extra = jnp.pad(d_beta_low, ((0, 0), (0, extra - beta_cols)))
    d_low, gain_part = run_back_project(
        activations, d_raw, d_extra, d_gate_logit, [weight_query, weight_gate, *weights_kv]
    )
    d_low, gain_part, others, zh_other = tied(d_low, gain_part, others, zh_other)
    start, feed_sums = 0, []
    for keep in zh_keeps:
        wide = keep.shape[-1]
        other = lax.slice_in_dim(zh_other, start, start + wide, axis=zh_other.ndim - 1)
        feed_sums.append((keep, other))
        start += wide
    feed_sums = far_steps(feed_sums, far[1:])
    both_heads = jnp.concatenate([gain_part[0], head_gain_part])
    both_heads = both_heads + swap_head(both_heads)
    d_other = swap_head(d_low)
    small = jnp.concatenate(
        [
            inner_rows(d_beta_low, normed).reshape(-1),
            both_heads[:features],
            grad_feed_gain,
            tap_grads.reshape(-1),
            both_heads[features:],
        ]
    )
    small = jnp.pad(small, (0, -small.shape[0] % 1024)).reshape(-1, 128)
    for at in (1, 2):
        keeps, sends = halve_all(list(zip(keeps, others)), at_step(at))
        small, sends, keeps = tied(small, sends, keeps)
        others = swap_all(sends, at_step(at))
        small = small + swap_seq(small, near[at - 1])
        if at == 1:
            d_normed = d_low.astype(F32) + d_other.astype(F32)
            d_input_norm, _ = norm_back(activations.astype(F32), gain_one, d_normed)
            grad_input = own_half(d_hidden + d_input_norm)
            grad_input, small, others = tied(grad_input, small, others)
        else:
            small, others = tied(small, others)
    conv_sum = jnp.concatenate(far_steps(list(zip(keeps, others)), far), 1)
    for distance in near[2:] + far:
        small = small + swap_seq(small, distance)
    small = small.reshape(-1)
    ends, at = [], 0
    for size in (beta_cols * features, features, features, tap_count * conv_cols, width):
        ends.append(small[at : at + size])
        at += size
    own_rows = lambda vector: lax.dynamic_slice_in_dim(
        vector, device_rank * shard_rows, shard_rows, vector.ndim - 1
    )
    tap_total = ends[3].reshape(tap_count, conv_cols)
    cut = lambda array, start, size: array[:, start : start + size]
    return (
        output,
        grad_input,
        cut(conv_sum, 0, query_cols),
        cut(conv_sum, query_cols, key_cols),
        cut(conv_sum, query_cols + key_cols, key_cols),
        own_rows(ends[0].reshape(beta_cols, features)).T,
        feed_sums[4],
        feed_sums[3].T,
        cut(tap_total, 0, query_cols),
        cut(tap_total, query_cols, key_cols),
        cut(tap_total, query_cols + key_cols, key_cols),
        own_rows(ends[1]),
        ends[4],
        own_rows(ends[2]),
        feed_sums[0],
        feed_sums[1],
        feed_sums[2].T,
    )


def solution(mesh):
    in_specs = (
        P("seq", None),
        P("seq", "head"),
        P(),
        P("seq", "head"),
        P("seq", "head"),
        P("seq", "head"),
        P("seq", "head"),
        P("seq", "head"),
        P("head", "seq"),
        P(None, "head"),
        P(None, "head"),
        P(None, "head"),
        P("seq"),
        P(),
        P("seq"),
        P("seq", "head"),
        P("seq", "head"),
        P("head", "seq"),
        P("seq", None),
    )
    out_specs = (
        P("seq", "head"),
        P("seq", "head"),
        P("seq", "head"),
        P("seq", "head"),
        P("seq", "head"),
        P("seq", "head"),
        P("seq", "head"),
        P("head", "seq"),
        P(None, "head"),
        P(None, "head"),
        P(None, "head"),
        P("seq"),
        P(),
        P("seq"),
        P("seq", "head"),
        P("seq", "head"),
        P("head", "seq"),
    )
    return jax.shard_map(
        per_device, mesh=mesh, in_specs=in_specs, out_specs=out_specs, check_vma=False
    )
```

```python
import functools

import jax
import jax.numpy as jnp
from jax import lax
from jax.experimental import pallas as pl
from jax.experimental.pallas import tpu as pltpu
from jax.sharding import PartitionSpec as P

BLOCK = 64
RESET = 256.0
HALO = 16
VMEM_BYTES = 63 * 1024 * 1024
PAIR = 2
QUERY_CHUNKS = 2
TILE = 256
AHEAD_CALLS = 3
NORM_EPS = 1e-05
UNIT_EPS = 1e-06
F32 = jnp.float32
BF16 = jnp.bfloat16


def product(former, latter):
    return jnp.dot(former, latter, preferred_element_type=F32)


def inner_rows(former, latter):
    return lax.dot_general(former, latter, (((0,), (0,)), ((), ())), preferred_element_type=F32)


def times_transposed(former, latter):
    return lax.dot_general(former, latter, (((1,), (1,)), ((), ())), preferred_element_type=F32)


def low(values):
    return values.astype(BF16)


def split(values):
    high = values.astype(BF16)
    return high, (values - high.astype(F32)).astype(BF16)


def fine(form, former, latter):
    a_high, a_low = split(former)
    b_high, b_low = split(latter)
    return form(a_high, b_high) + (form(a_low, b_high) + form(a_high, b_low))


def silu_slope(values, sigma):
    return sigma * (1.0 + values * (1.0 - sigma))


def norm_back(values, gain_vector, gradient):
    row_scale = lax.rsqrt(jnp.mean(values * values, axis=-1, keepdims=True) + NORM_EPS)
    unit_value = values * row_scale
    scaled_grad = gradient * gain_vector
    back_value = row_scale * (
        scaled_grad - unit_value * jnp.mean(scaled_grad * unit_value, axis=-1, keepdims=True)
    )
    return (back_value, gradient * unit_value)


def row_maps(rows):
    row = lax.broadcasted_iota(jnp.int32, (rows, rows), 0)
    col = lax.broadcasted_iota(jnp.int32, (rows, rows), 1)
    return row % BLOCK, col % BLOCK, row // BLOCK, col // BLOCK


def lower_inverses(systems, apart):
    rows = systems[0].shape[0]
    row = lax.broadcasted_iota(jnp.int32, (rows, rows), 0)
    col = lax.broadcasted_iota(jnp.int32, (rows, rows), 1)
    eye = jnp.where(row == col, 1.0, 0.0)
    inverses = [eye - jnp.where(apart == 0, system, 0.0) for system in systems]
    level = 0
    while (1 << level) < BLOCK:
        joins = (apart >> level) == 1
        joints = [low(jnp.where(joins, system, 0.0)) for system in systems]
        lows = [low(inverse) for inverse in inverses]
        halves = [low(product(a, b)) for a, b in zip(lows, joints)]
        inverses = [c - product(a, b) for a, b, c in zip(halves, lows, inverses)]
        level += 1
    return inverses


def conv_rows(tile, halo, taps, same):
    count = tile.shape[0]
    extended = jnp.concatenate([halo, tile], 0)
    windows = [tile] + [
        pltpu.roll(extended, offset, 0)[8:] for offset in range(1, taps.shape[0])
    ]
    outcome = tile * taps[0:1]
    for offset in range(1, taps.shape[0]):
        outcome = outcome + windows[offset] * taps[offset : offset + 1] * same[:, offset : offset + 1]
    return outcome, windows


def unit_scale(values):
    return lax.rsqrt(jnp.sum(values * values, axis=-1, keepdims=True) + UNIT_EPS)


def pieces_of(head, head_count, substeps, width):
    query = [(head * width, width)]
    keys = [((head_count + head * substeps + n) * width, width) for n in range(substeps)]
    values = [
        ((head_count + (head_count + head) * substeps + n) * width, width) for n in range(substeps)
    ]
    return query + keys + values


def conv_of(source, first, start, size, taps, same_rows):
    tile_ref, before, edge, offset = source
    columns = slice(start - offset, start - offset + size)
    halo = jnp.where(first, edge[:, columns], before[:, columns]).astype(F32)[HALO - 8 :]
    return conv_rows(
        tile_ref[:, columns].astype(F32), halo, taps[:, start : start + size], same_rows
    )


def beta_rows(beta, head, substeps):
    columns = [beta[:, head * substeps + n : head * substeps + n + 1] for n in range(substeps)]
    return jnp.concatenate(columns, 0)


def forward_kernel(
    head_count, substeps, width, begin,
    raw, before, edge, taps, same, beta, cum_col, cum_row, chain_in, *refs,
):
    t_out, p_out, s_out, key_out, solved_out, chain = refs[-6:]
    step = pl.program_id(0)
    first = step + begin == 0
    rows = BLOCK * substeps
    row_token, col_token, row_step, col_step = row_maps(rows)
    upto = col_token <= row_token
    earlier = (col_token < row_token) | ((col_token == row_token) & (col_step < row_step))
    apart = row_token ^ col_token
    eye = jnp.where(
        lax.broadcasted_iota(jnp.int32, (width, width), 0)
        == lax.broadcasted_iota(jnp.int32, (width, width), 1),
        1.0,
        0.0,
    )
    same_rows = same[...]

    @pl.when(step == 0)
    def _():
        chain[...] = chain_in[...]

    heads = range(head_count)
    offset = head_count * width
    source = (raw, before, edge, offset)
    units = [(j, h) for j in range(PAIR) for h in heads]
    rows_at = [slice(j * BLOCK, (j + 1) * BLOCK) for j in range(PAIR)]
    keys, values, betas = {}, {}, {}
    for head in heads:
        acts = []
        for start, size in pieces_of(head, head_count, substeps, width)[1:]:
            pre, _ = conv_of(source, first, start, size, taps, same_rows)
            acts.append(pre * jax.nn.sigmoid(pre))
        acts = [a * unit_scale(a) for a in acts[:substeps]] + acts[substeps:]
        acts = [low(a) for a in acts]
        for j, at in enumerate(rows_at):
            keys[j, head] = jnp.concatenate([a[at] for a in acts[:substeps]], 0)
            values[j, head] = jnp.concatenate([a[at] for a in acts[substeps:]], 0)
            betas[j, head] = beta_rows(beta[at], head, substeps)
    keys, values, betas = ([held[u] for u in units] for held in (keys, values, betas))
    cum_rows = [jnp.concatenate([cum_col[rows_at[j], h : h + 1]] * substeps, 0) for j, h in units]
    cum_cols = [cum_row[j, h : h + 1, :] for j, h in units]
    lasts = [c[:, BLOCK - 1 : BLOCK] for c in cum_cols]
    ratios = [jnp.exp(jnp.where(upto, a - b, -1e4)) for a, b in zip(cum_rows, cum_cols)]
    grams = [times_transposed(key, key) for key in keys]
    systems = [
        jnp.where(earlier, beta_col * ratio * gram, 0.0)
        for beta_col, ratio, gram in zip(betas, ratios, grams)
    ]
    inverses = [low(inverse) for inverse in lower_inverses(systems, apart)]
    rights = [
        jnp.concatenate(
            [
                low(beta_col * jnp.exp(cum) * key.astype(F32)),
                low(beta_col * value.astype(F32)),
            ],
            1,
        )
        for beta_col, cum, key, value in zip(betas, cum_rows, keys, values)
    ]
    solved = [low(product(inverse, right)) for inverse, right in zip(inverses, rights)]
    ends = [
        low(jnp.exp(last - cum) * key.astype(F32))
        for last, cum, key in zip(lasts, cum_rows, keys)
    ]
    moved = [inner_rows(end, both) for end, both in zip(ends, solved)]
    step_maps = [split(jnp.exp(last) * eye - move[:, :width]) for last, move in zip(lasts, moved)]
    chains = [chain[head] for head in heads]
    for at, (j, head) in enumerate(units):
        t_out[j, head] = inverses[at]
        key_out[j, head] = keys[at]
        solved_out[j, head] = solved[at]
    for j in range(PAIR):
        at = j * head_count
        splits = [split(chained) for chained in chains]
        for head in heads:
            p_out[j, head] = splits[head][0][:, :width]
            s_out[j, head] = splits[head][0][:, width:]
        chains = [
            product(step_maps[at + h][0], splits[h][0])
            + (product(step_maps[at + h][1], splits[h][0]) + product(step_maps[at + h][0], splits[h][1]))
            for h in heads
        ]
        chains = [
            jnp.concatenate([c[:, :width], c[:, width:] + moved[at + h][:, width:]], 1)
            for h, c in enumerate(chains)
        ]
    for head in heads:
        chain[head] = chains[head]


def whole_spec(*shape):
    return pl.BlockSpec(shape, lambda *c: (0,) * len(shape))


def run_forward(
    begin, end, raw, edge, taps, same, beta, cum_col, cum_row, chain, passed,
    head_count, substeps, width,
):
    count, columns = raw.shape
    chunks = count // BLOCK
    rows = BLOCK * substeps
    begin, end = begin // PAIR, end // PAIR
    per_halo = PAIR * BLOCK // HALO
    tokens = lambda cols: pl.BlockSpec((PAIR * BLOCK, cols), lambda c: (c + begin, 0))
    tiles = lambda *shape: pl.BlockSpec((PAIR, head_count) + shape, lambda c: (c + begin, 0, 0, 0))
    shapes = [(rows, rows), (width, width), (width, width), (rows, width), (rows, 2 * width)]
    anywhere = pl.BlockSpec(memory_space=pl.ANY)
    return pl.pallas_call(
        functools.partial(forward_kernel, head_count, substeps, width, begin),
        grid=(end - begin,),
        in_specs=[
            tokens(columns),
            pl.BlockSpec(
                (HALO, columns), lambda c: (jnp.maximum((c + begin) * per_halo - 1, 0), 0)
            ),
            whole_spec(HALO, columns),
            whole_spec(*taps.shape),
            tokens(same.shape[1]),
            tokens(beta.shape[1]),
            tokens(head_count),
            pl.BlockSpec((PAIR, head_count, rows), lambda c: (c + begin, 0, 0)),
            whole_spec(*chain.shape),
        ]
        + [anywhere] * len(passed),
        out_specs=[tiles(*shape) for shape in shapes] + [whole_spec(*chain.shape)],
        out_shape=[
            jax.ShapeDtypeStruct((chunks, head_count) + shape, BF16) for shape in shapes
        ]
        + [jax.ShapeDtypeStruct(chain.shape, F32)],
        input_output_aliases={9 + k: k for k in range(len(passed))},
        compiler_params=pltpu.CompilerParams(
            dimension_semantics=("arbitrary",), vmem_limit_bytes=VMEM_BYTES
        ),
        name="mixer_forward",
    )(raw, raw, edge, taps, same, beta, cum_col, cum_row, chain, *passed)


def query_kernel(
    head_count, substeps, width,
    raw, before, edge, taps, same, cum_col, cum_row, key_in, solved_in, p_in, s_in,
    qtil_out, local_out,
):
    first = pl.program_id(0) == 0
    rows = BLOCK * substeps
    row_token, col_token, _, _ = row_maps(rows)
    upto = (col_token <= row_token)[:BLOCK]
    same_rows = same[...]
    heads = range(head_count)
    units = [(j, h) for j in range(QUERY_CHUNKS) for h in heads]
    rows_at = [slice(j * BLOCK, (j + 1) * BLOCK) for j in range(QUERY_CHUNKS)]
    queries = []
    for head in heads:
        start, size = pieces_of(head, head_count, substeps, width)[0]
        pre, _ = conv_of((raw, before, edge, 0), first, start, size, taps, same_rows)
        act = pre * jax.nn.sigmoid(pre)
        queries.append(low(act * unit_scale(act) * width ** (-0.5)))
    queries = [queries[h][rows_at[j]] for j, h in units]
    cum_rows = [cum_col[rows_at[j], h : h + 1] for j, h in units]
    ratios = [
        jnp.exp(jnp.where(upto, cum - cum_row[j, h : h + 1, :], -1e4))
        for cum, (j, h) in zip(cum_rows, units)
    ]
    scores = [times_transposed(query, key_in[j, h]) for query, (j, h) in zip(queries, units)]
    seen = [
        product(low(ratio * score), solved_in[j, h])
        for ratio, score, (j, h) in zip(ratios, scores, units)
    ]
    effective = [
        low(jnp.exp(cum) * query.astype(F32) - see[:, :width])
        for cum, query, see in zip(cum_rows, queries, seen)
    ]
    reached = [
        (product(eff, p_in[j, h]), product(eff, s_in[j, h]))
        for eff, (j, h) in zip(effective, units)
    ]
    for k, (j, h) in enumerate(units):
        at = slice(h * width, (h + 1) * width)
        qtil_out[rows_at[j], at] = low(reached[k][0])
        local_out[rows_at[j], at] = reached[k][1] + seen[k][:, width:]


def run_query(
    raw, edge, taps, same, cum_col, cum_row, key_rows, solved, p_part, s_part,
    head_count, substeps, width,
):
    count, columns = raw.shape
    chunks = count // BLOCK
    rows = BLOCK * substeps
    per_halo = QUERY_CHUNKS * BLOCK // HALO
    tokens = lambda cols: pl.BlockSpec((QUERY_CHUNKS * BLOCK, cols), lambda c: (c, 0))
    tiles = lambda *shape: pl.BlockSpec((QUERY_CHUNKS, head_count) + shape, lambda c: (c, 0, 0, 0))
    return pl.pallas_call(
        functools.partial(query_kernel, head_count, substeps, width),
        grid=(chunks // QUERY_CHUNKS,),
        in_specs=[
            tokens(columns),
            pl.BlockSpec((HALO, columns), lambda c: (jnp.maximum(c * per_halo - 1, 0), 0)),
            whole_spec(HALO, columns),
            whole_spec(*taps.shape),
            tokens(same.shape[1]),
            tokens(head_count),
            pl.BlockSpec((QUERY_CHUNKS, head_count, rows), lambda c: (c, 0, 0)),
            tiles(rows, width),
            tiles(rows, 2 * width),
            tiles(width, width),
            tiles(width, width),
        ],
        out_specs=[tokens(columns), tokens(columns)],
        out_shape=[
            jax.ShapeDtypeStruct((count, columns), BF16),
            jax.ShapeDtypeStruct((count, columns), F32),
        ],
        compiler_params=pltpu.CompilerParams(
            dimension_semantics=("arbitrary",), vmem_limit_bytes=VMEM_BYTES
        ),
        name="mixer_query",
    )(raw, raw, edge, taps, same, cum_col, cum_row, key_rows, solved, p_part, s_part)


def backward_kernel(
    head_count, substeps, width, end,
    raw_q, before_q, edge_q, raw, before, edge, taps, same, same_next, beta, cum_col, cum_row,
    t_in, p_in, s_in, state_in, d_out, adjoint_in, carried_in, tap_in, *refs,
):
    d_raw, d_logit, tail_out, adjoint, carried, tap_out, tail_next = refs[-7:]
    step = pl.program_id(0)
    pair = end - 1 - step
    rows = BLOCK * substeps
    tap_count = taps.shape[0]
    count = PAIR * BLOCK
    row_token, col_token, row_step, col_step = row_maps(rows)
    upto = col_token <= row_token
    earlier = (col_token < row_token) | ((col_token == row_token) & (col_step < row_step))
    same_rows = same[...]
    same_long = jnp.concatenate([same_rows, same_next[...]], 0)

    @pl.when(step == 0)
    def _():
        adjoint[...] = adjoint_in[...]
        carried[...] = carried_in[...]
        tap_out[...] = tap_in[...]

    heads = range(head_count)
    units_at = [(j, h) for j in range(PAIR) for h in heads]
    rows_at = [slice(j * BLOCK, (j + 1) * BLOCK) for j in range(PAIR)]
    pieces = [pieces_of(head, head_count, substeps, width) for head in heads]
    pres, sigmas, scales, units = [], [], [], []
    queries, keys, values, betas = {}, {}, {}, {}
    key_start = head_count * width
    sources = [(raw_q, before_q, edge_q, 0), (raw, before, edge, key_start)]

    def windows_of(start, size):
        return conv_of(sources[int(start >= key_start)], pair == 0, start, size, taps, same_rows)

    for head in heads:
        pre = [windows_of(start, size)[0] for start, size in pieces[head]]
        sigma = [jax.nn.sigmoid(p) for p in pre]
        acts = [p * s for p, s in zip(pre, sigma)]
        pres.append(pre)
        sigmas.append(sigma)
        scales.append([unit_scale(a) for a in acts[: 1 + substeps]])
        units.append([a * s for a, s in zip(acts[: 1 + substeps], scales[head])])
        query = low(units[head][0] * width ** (-0.5))
        key = [low(unit) for unit in units[head][1:]]
        value = [low(act) for act in acts[1 + substeps :]]
        for j, at in enumerate(rows_at):
            queries[j, head] = query[at]
            keys[j, head] = jnp.concatenate([k[at] for k in key], 0)
            values[j, head] = jnp.concatenate([v[at] for v in value], 0)
            betas[j, head] = beta_rows(beta[at], head, substeps)
    queries, keys, values, betas = (
        [held[u] for u in units_at] for held in (queries, keys, values, betas)
    )
    cum_rows = [
        jnp.concatenate([cum_col[rows_at[j], h : h + 1]] * substeps, 0) for j, h in units_at
    ]
    cum_cols = [cum_row[j, h : h + 1, :] for j, h in units_at]
    lasts = [c[:, BLOCK - 1 : BLOCK] for c in cum_cols]
    ratios = [jnp.exp(jnp.where(upto, a - b, -1e4)) for a, b in zip(cum_rows, cum_cols)]
    carries = [jnp.exp(c) for c in cum_rows]
    end_ratios = [jnp.exp(last - c) for last, c in zip(lasts, cum_rows)]
    inverses = [t_in[j, h] for j, h in units_at]
    d_mixes = [d_out[rows_at[j], h * width : (h + 1) * width] for j, h in units_at]
    states = [
        low(s_in[j, h].astype(F32) + product(p_in[j, h], state_in[h])) for j, h in units_at
    ]
    stacks = [jnp.concatenate([query, key], 0) for query, key in zip(queries, keys)]
    both_grams = [times_transposed(stack, key) for stack, key in zip(stacks, keys)]
    grams = [both[BLOCK:] for both in both_grams]
    masks = [low(ratio[:BLOCK] * both[:BLOCK]) for ratio, both in zip(ratios, both_grams)]
    d_both = [
        inner_rows(
            jnp.concatenate([mask, low(carry[:BLOCK] * query.astype(F32))], 1), d_mix
        )
        for mask, carry, query, d_mix in zip(masks, carries, queries, d_mixes)
    ]
    d_seen = [both[:rows] for both in d_both]
    d_reach = [both[rows:] for both in d_both]
    end_keys = [low(end * key.astype(F32)) for end, key in zip(end_ratios, keys)]
    start_keys = [
        low((beta_col * carry) * key.astype(F32))
        for beta_col, carry, key in zip(betas, carries, keys)
    ]
    freshes = [
        value.astype(F32) - carry * product(key, state)
        for value, carry, key, state in zip(values, carries, keys, states)
    ]
    updates = [
        low(product(inverse, low(beta_col * fresh)))
        for inverse, beta_col, fresh in zip(inverses, betas, freshes)
    ]
    laters_low, d_rights, d_rights_low = {}, {}, {}
    for j in range(PAIR - 1, -1, -1):
        ids = [j * head_count + h for h in heads]
        laters = [adjoint[h] for h in heads]
        for h, at in enumerate(ids):
            laters_low[at] = low(laters[h])
        d_updates = [low(d_seen[at] + product(end_keys[at], laters_low[at])) for at in ids]
        for h, at in enumerate(ids):
            d_rights[at] = inner_rows(inverses[at], d_updates[h])
            d_rights_low[at] = low(d_rights[at])
        for h, at in enumerate(ids):
            adjoint[h] = (
                jnp.exp(lasts[at]) * laters[h]
                + d_reach[at]
                - inner_rows(start_keys[at], d_rights_low[at])
            )
    ids = range(len(units_at))
    outer = [jnp.concatenate([d_mixes[at], d_rights_low[at]], 0) for at in ids]
    by_update = [times_transposed(outer[at], updates[at]) for at in ids]
    by_state = [times_transposed(outer[at], states[at]) for at in ids]
    d_systems = [
        jnp.where(earlier, -by_update[at][BLOCK:] * ratios[at], 0.0) for at in ids
    ]
    d_scores = [by_update[at][:BLOCK] * ratios[at][:BLOCK] for at in ids]
    d_grams = [betas[at] * d_systems[at] for at in ids]
    d_scores = [low(d_score) for d_score in d_scores]
    d_grams = [low(d_gram + jnp.transpose(d_gram)) for d_gram in d_grams]
    d_betas = [
        jnp.sum(d_rights[at] * freshes[at], axis=-1, keepdims=True)
        + jnp.sum(d_systems[at] * grams[at], axis=-1, keepdims=True)
        for at in ids
    ]
    d_queries = [
        carries[at][:BLOCK] * by_state[at][:BLOCK] + product(d_scores[at], keys[at])
        for at in ids
    ]
    d_keys = [
        inner_rows(jnp.concatenate([d_scores[at], d_grams[at]], 0), stacks[at])
        + end_ratios[at] * times_transposed(updates[at], laters_low[at])
        - (betas[at] * carries[at]) * by_state[at][BLOCK:]
        for at in ids
    ]
    for j in range(PAIR):
        logit_cols = []
        for h in heads:
            at = j * head_count + h
            logits = d_betas[at] * betas[at] * (1.0 - betas[at])
            logit_cols += [logits[n * BLOCK : (n + 1) * BLOCK] for n in range(substeps)]
        d_logit[rows_at[j], :] = jnp.concatenate(logit_cols, 1)

    for head in heads:
        mine = [j * head_count + head for j in range(PAIR)]
        step_rows = lambda arrays, n: jnp.concatenate(
            [array[n * BLOCK : (n + 1) * BLOCK] for array in arrays], 0
        )
        d_value = [betas[at] * d_rights[at] for at in mine]
        grads = [width ** (-0.5) * jnp.concatenate([d_queries[at] for at in mine], 0)]
        grads += [step_rows([d_keys[at] for at in mine], n) for n in range(substeps)]
        grads += [step_rows(d_value, n) for n in range(substeps)]
        for at, (start, size) in enumerate(pieces[head]):
            grad = grads[at]
            if at <= substeps:
                unit = units[head][at]
                grad = scales[head][at] * (
                    grad - unit * jnp.sum(grad * unit, axis=-1, keepdims=True)
                )
            grad = grad * silu_slope(pres[head][at], sigmas[head][at])
            windows = windows_of(start, size)[1]
            long = jnp.concatenate([grad, carried[:, start : start + size]], 0)
            tap = taps[:, start : start + size]
            spread = grad * tap[0:1]
            sums = [jnp.sum(grad * windows[0], axis=0, keepdims=True)]
            for offset in range(1, tap_count):
                masked = long * same_long[:, offset : offset + 1]
                spread = spread + (
                    pltpu.roll(masked, count + 8 - offset, 0)[:count] * tap[offset : offset + 1]
                )
                sums.append(jnp.sum(masked[:count] * windows[offset], axis=0, keepdims=True))
            carried[:, start : start + size] = grad[:8]
            tap_out[:, start : start + size] += jnp.concatenate(sums, 0)
            d_raw[:, start : start + size] = low(spread)
            tail_next[:, start : start + size] = spread[count - 8 :]

    @pl.when(step == 0)
    def _():
        tail_out[...] = tail_next[...]


def run_backward(
    begin, end, raw_q, edge_q, raw, edge, taps, same, beta, cum_col, cum_row, t_part, p_part,
    s_part, state_in, d_out, adjoint, carried, tap_grads, passed, head_count, substeps, width,
):
    count = raw.shape[0]
    columns = taps.shape[1]
    chunks = count // BLOCK
    rows = BLOCK * substeps
    begin, end, chunks = begin // PAIR, end // PAIR, chunks // PAIR
    per_halo = PAIR * BLOCK // HALO
    per_eight = PAIR * BLOCK // 8
    tokens = lambda cols: pl.BlockSpec((PAIR * BLOCK, cols), lambda c: (end - 1 - c, 0))
    halo = lambda cols: pl.BlockSpec(
        (HALO, cols), lambda c: (jnp.maximum((end - 1 - c) * per_halo - 1, 0), 0)
    )
    tiles = lambda *shape: pl.BlockSpec((PAIR, head_count) + shape, lambda c: (end - 1 - c, 0, 0, 0))
    anywhere = pl.BlockSpec(memory_space=pl.ANY)
    state = (head_count, width, width)
    sources = []
    for array in (raw_q, raw):
        cols = array.shape[1]
        sources += [tokens(cols), halo(cols), whole_spec(HALO, cols)]
    return pl.pallas_call(
        functools.partial(backward_kernel, head_count, substeps, width, end),
        grid=(end - begin,),
        in_specs=sources
        + [
            whole_spec(*taps.shape),
            tokens(same.shape[1]),
            pl.BlockSpec(
                (8, same.shape[1]),
                lambda c: (jnp.minimum((end - c) * per_eight, chunks * per_eight - 1), 0),
            ),
            tokens(beta.shape[1]),
            tokens(head_count),
            pl.BlockSpec((PAIR, head_count, rows), lambda c: (end - 1 - c, 0, 0)),
            tiles(rows, rows),
            tiles(width, width),
            tiles(width, width),
            whole_spec(*state),
            tokens(head_count * width),
            whole_spec(*state),
            whole_spec(8, columns),
            whole_spec(*taps.shape),
        ]
        + [anywhere] * len(passed),
        out_specs=[
            tokens(columns),
            tokens(head_count * substeps),
            whole_spec(8, columns),
            whole_spec(*state),
            whole_spec(8, columns),
            whole_spec(*taps.shape),
        ],
        out_shape=[
            jax.ShapeDtypeStruct((count, columns), BF16),
            jax.ShapeDtypeStruct((count, head_count * substeps), F32),
            jax.ShapeDtypeStruct((8, columns), F32),
            jax.ShapeDtypeStruct(state, F32),
            jax.ShapeDtypeStruct((8, columns), F32),
            jax.ShapeDtypeStruct(taps.shape, F32),
        ],
        scratch_shapes=[pltpu.VMEM((8, columns), F32)],
        input_output_aliases={20 + k: k for k in range(len(passed))},
        compiler_params=pltpu.CompilerParams(
            dimension_semantics=("arbitrary",), vmem_limit_bytes=VMEM_BYTES
        ),
        name="mixer_backward",
    )(
        raw_q, raw_q, edge_q, raw, raw, edge, taps, same, same, beta, cum_col, cum_row,
        t_part, p_part, s_part, state_in, d_out, adjoint, carried, tap_grads, *passed,
    )


def row_scale_of(values):
    return lax.rsqrt(jnp.mean(values * values, axis=-1, keepdims=True) + NORM_EPS)


def project_kernel(parts, raw_cols, inputs, edge, gain, *refs):
    weights, outs = refs[:parts], refs[parts:]
    normed_out, edge_normed, raw_out, edge_out, extra_out = outs
    gain_row = gain[...]

    def rows_of(values):
        values = values.astype(F32)
        return low(values * row_scale_of(values) * gain_row)

    def fill(normed, raw_ref, extra_ref):
        at = 0
        for weight in weights:
            cols = weight.shape[1]
            both = product(normed, weight[...])
            raw_part = min(cols, raw_cols - at)
            raw_ref[:, at : at + raw_part] = low(both[:, :raw_part])
            if extra_ref is not None and raw_part < cols:
                extra_ref[...] = jax.nn.sigmoid(both[:, raw_part:])
            at += cols

    normed = rows_of(inputs[...])
    normed_out[...] = normed
    fill(normed, raw_out, extra_out)

    @pl.when(pl.program_id(0) == 0)
    def _():
        normed_edge = rows_of(edge[...])
        edge_normed[...] = normed_edge
        fill(normed_edge, edge_out, None)


def once(shape):
    return pl.BlockSpec(shape, lambda *c: (0,) * len(shape), pipeline_mode=pl.Buffered(1))


def run_project(inputs, edge, gain, weights, raw_cols, extra):
    count, features = inputs.shape
    tile = min(TILE, count)
    tokens = lambda cols: pl.BlockSpec((tile, cols), lambda c: (c, 0))
    return pl.pallas_call(
        functools.partial(project_kernel, len(weights), raw_cols),
        grid=(count // tile,),
        in_specs=[tokens(features), whole_spec(HALO, features), whole_spec(1, features)]
        + [once(weight.shape) for weight in weights],
        out_specs=[
            tokens(features), whole_spec(HALO, features), tokens(raw_cols),
            whole_spec(HALO, raw_cols), tokens(extra),
        ],
        out_shape=[
            jax.ShapeDtypeStruct((count, features), BF16),
            jax.ShapeDtypeStruct((HALO, features), BF16),
            jax.ShapeDtypeStruct((count, raw_cols), BF16),
            jax.ShapeDtypeStruct((HALO, raw_cols), BF16),
            jax.ShapeDtypeStruct((count, extra), F32),
        ],
        compiler_params=pltpu.CompilerParams(
            dimension_semantics=("arbitrary",), vmem_limit_bytes=VMEM_BYTES
        ),
        name="project",
    )(inputs, edge, gain, *weights)


def project_side_kernel(normed, edge, query_w, gate_w, raw_out, edge_out, gate_out):
    raw_out[...] = low(product(normed[...], query_w[...]))
    gate_out[...] = product(normed[...], gate_w[...])

    @pl.when(pl.program_id(0) == 0)
    def _():
        edge_out[...] = low(product(edge[...], query_w[...]))


def run_project_side(normed, edge, query_w, gate_w):
    count, features = normed.shape
    cols = query_w.shape[1]
    tile = min(TILE, count)
    tokens = lambda cols: pl.BlockSpec((tile, cols), lambda c: (c, 0))
    return pl.pallas_call(
        project_side_kernel,
        grid=(count // tile,),
        in_specs=[
            tokens(features), whole_spec(HALO, features), once(query_w.shape), once(gate_w.shape)
        ],
        out_specs=[tokens(cols), whole_spec(HALO, cols), tokens(cols)],
        out_shape=[
            jax.ShapeDtypeStruct((count, cols), BF16),
            jax.ShapeDtypeStruct((HALO, cols), BF16),
            jax.ShapeDtypeStruct((count, cols), F32),
        ],
        compiler_params=pltpu.CompilerParams(
            dimension_semantics=("arbitrary",), vmem_limit_bytes=VMEM_BYTES
        ),
        name="project_side",
    )(normed, edge, query_w, gate_w)


def heads_kernel(
    head_count, width,
    local, reach, state, gate, gain, weight,
    mixer_out, heads_out, own_out, low_out,
):
    gain_row = gain[...]
    for h in range(head_count):
        at = slice(h * width, (h + 1) * width)
        mixer = local[:, at] + product(reach[:, at], state[h])
        logit = gate[:, at]
        mixer_out[:, at] = mixer
        heads_out[:, at] = low(
            mixer * row_scale_of(mixer) * gain_row * (logit * jax.nn.sigmoid(logit))
        )
    branch = times_transposed(heads_out[...], weight[...])
    own_out[...] = branch
    low_out[...] = low(branch)


def run_heads(local, reach, state, gate, gain, weight, head_count, width):
    count, cols = local.shape
    features = weight.shape[0]
    tile = min(TILE, count)
    tokens = lambda cols: pl.BlockSpec((tile, cols), lambda c: (c, 0))
    return pl.pallas_call(
        functools.partial(heads_kernel, head_count, width),
        grid=(count // tile,),
        in_specs=[
            tokens(cols), tokens(cols), whole_spec(*state.shape), tokens(cols),
            whole_spec(*gain.shape), once(weight.shape),
        ],
        out_specs=[tokens(cols), tokens(cols), tokens(features), tokens(features)],
        out_shape=[
            jax.ShapeDtypeStruct((count, cols), F32),
            jax.ShapeDtypeStruct((count, cols), BF16),
            jax.ShapeDtypeStruct((count, features), F32),
            jax.ShapeDtypeStruct((count, features), BF16),
        ],
        compiler_params=pltpu.CompilerParams(
            dimension_semantics=("arbitrary",), vmem_limit_bytes=VMEM_BYTES
        ),
        name="heads",
    )(local, reach, state, gate, gain, weight)


def lay_copies(view, other, own, short, rows, scratch, semaphores):
    run = short * rows
    copies = []
    for block in range(view.shape[0] // run):
        for side, at in ((view, own), (other, 1 - own)):
            row = pl.multiple_of((2 * block + at) * run, run)
            copies.append(
                pltpu.make_async_copy(
                    side.at[pl.ds(block * run, run)],
                    scratch.at[pl.ds(row, run)],
                    semaphores.at[len(copies)],
                )
            )
    return copies


def feed_kernel(runs, rows, me, inputs, own, other, gain, cotangent, *refs):
    halves, outs, rest = refs[:6], refs[6:14], refs[14:]
    hidden_out, normed_out, act_out, d_gate_out, d_up_out, branch_out, own_out, low_out = outs
    gate_w, up_w, down_w = rest[:3]

    @pl.when(pl.program_id(0) == 0)
    def _():
        copies = []
        for k, short in enumerate(runs):
            copies += lay_copies(
                halves[2 * k], halves[2 * k + 1], (me[0] // short) % 2, short, rows, rest[k],
                rest[3 + k],
            )
        for copy in copies:
            copy.start()
        for copy in copies:
            copy.wait()

    hidden = inputs[...].astype(F32) + own[...] + other[...].astype(F32)
    hidden_out[...] = hidden
    normed = low(hidden * row_scale_of(hidden) * gain[...])
    normed_out[...] = normed
    gate = product(normed, gate_w[...])
    up = product(normed, up_w[...])
    d_act = product(cotangent[...], down_w[...])
    sigma = jax.nn.sigmoid(gate)
    act = gate * sigma
    activation = low(act * up)
    d_up = low(d_act * act)
    d_gate = low(d_act * up * silu_slope(gate, sigma))
    act_out[...] = activation
    d_gate_out[...] = d_gate
    d_up_out[...] = d_up
    branch_out[...] = low(times_transposed(activation, down_w[...]))
    d_normed = times_transposed(d_gate, gate_w[...]) + times_transposed(d_up, up_w[...])
    own_out[...] = d_normed
    low_out[...] = low(d_normed)


def run_feed(inputs, own, other, gain, cotangent, views, others, distances):
    rows = views[0].shape[-2]
    if rows < HALO:
        full = gather_end([gather_join(*part) for part in zip(views, others, distances)])
        half = full[0].shape[0] // 2
        views, others = [w[:half] for w in full], [w[half:] for w in full]
        distances, rows, me = [1] * 3, half, jnp.zeros((1,), jnp.int32)
    else:
        views, others = gather_end(views), gather_end(others)
        me = lax.axis_index("seq").astype(jnp.int32).reshape(1)
    halves = [half for pair in zip(views, others) for half in pair]
    count, features = inputs.shape
    cols = views[0].shape[1]
    tile = min(TILE, count)
    tokens = lambda cols: pl.BlockSpec((tile, cols), lambda c: (c, 0))
    shape = lambda cols, kind: jax.ShapeDtypeStruct((count, cols), kind)
    return pl.pallas_call(
        functools.partial(feed_kernel, distances, rows),
        grid=(count // tile,),
        in_specs=[pl.BlockSpec(memory_space=pltpu.SMEM)]
        + [tokens(features)] * 3
        + [whole_spec(1, features), tokens(features)]
        + [pl.BlockSpec(memory_space=pl.ANY)] * 6,
        scratch_shapes=[pltpu.VMEM((2 * view.shape[0], cols), BF16) for view in views]
        + [
            pltpu.SemaphoreType.DMA((2 * (view.shape[0] // (short * rows)),))
            for view, short in zip(views, distances)
        ],
        out_specs=[tokens(features)] * 2 + [tokens(cols)] * 3 + [tokens(features)] * 3,
        out_shape=[shape(features, F32), shape(features, BF16)]
        + [shape(cols, BF16)] * 3
        + [shape(features, BF16), shape(features, F32), shape(features, BF16)],
        compiler_params=pltpu.CompilerParams(
            dimension_semantics=("arbitrary",), vmem_limit_bytes=VMEM_BYTES
        ),
        name="feed",
    )(me, inputs, own, other, gain, cotangent, *halves)


def turn_kernel(
    head_count, width,
    hidden, own, other, gain, cotangent, weight, mixer_in, gate, head_gain, reach,
    d_hidden_out, d_low_out, d_gate_out, d_mixer_out, state_out, feed_gain_out, head_gain_out,
):
    @pl.when(pl.program_id(0) == 0)
    def _():
        state_out[...] = jnp.zeros(state_out.shape, F32)
        feed_gain_out[...] = jnp.zeros(feed_gain_out.shape, F32)
        head_gain_out[...] = jnp.zeros(head_gain_out.shape, F32)

    d_normed = own[...] + other[...].astype(F32)
    back, terms = norm_back(hidden[...], gain[...], d_normed)
    feed_gain_out[...] += jnp.sum(terms, axis=0, keepdims=True)
    d_hidden = cotangent[...].astype(F32) + back
    d_hidden_out[...] = d_hidden
    d_low = low(d_hidden)
    d_low_out[...] = d_low
    d_heads = product(d_low, weight[...])
    gain_row = head_gain[...]
    for h in range(head_count):
        at = slice(h * width, (h + 1) * width)
        mixer = mixer_in[:, at]
        unit = mixer * row_scale_of(mixer)
        logit = gate[:, at]
        sigma = jax.nn.sigmoid(logit)
        d_head = d_heads[:, at]
        d_gate_out[:, at] = low(d_head * (unit * gain_row) * silu_slope(logit, sigma))
        d_mixer, head_terms = norm_back(mixer, gain_row, d_head * (logit * sigma))
        head_gain_out[...] += jnp.sum(head_terms, axis=0, keepdims=True)
        d_mixer_low = low(d_mixer)
        d_mixer_out[:, at] = d_mixer_low
        state_out[h] += inner_rows(reach[:, at], d_mixer_low)


def run_turn(
    hidden, own, other, gain, cotangent, weight, mixer, gate, head_gain, reach, head_count, width
):
    count, features = hidden.shape
    cols = mixer.shape[1]
    tile = min(TILE, count)
    tokens = lambda cols: pl.BlockSpec((tile, cols), lambda c: (c, 0))
    shape = lambda cols, kind: jax.ShapeDtypeStruct((count, cols), kind)
    state = (head_count, width, width)
    return pl.pallas_call(
        functools.partial(turn_kernel, head_count, width),
        grid=(count // tile,),
        in_specs=[tokens(features)] * 3
        + [whole_spec(1, features), tokens(features), once(weight.shape)]
        + [tokens(cols), tokens(cols), whole_spec(1, width), tokens(cols)],
        out_specs=[tokens(features)] * 2
        + [tokens(cols)] * 2
        + [whole_spec(*state), whole_spec(1, features), whole_spec(1, width)],
        out_shape=[shape(features, F32), shape(features, BF16)]
        + [shape(cols, BF16)] * 2
        + [
            jax.ShapeDtypeStruct(state, F32),
            jax.ShapeDtypeStruct((1, features), F32),
            jax.ShapeDtypeStruct((1, width), F32),
        ],
        compiler_params=pltpu.CompilerParams(
            dimension_semantics=("arbitrary",), vmem_limit_bytes=VMEM_BYTES
        ),
        name="turn",
    )(hidden, own, other, gain, cotangent, weight, mixer, gate, head_gain, reach)


def back_project_kernel(extra, inputs, d_raw, d_extra, d_gate, query_w, gate_w, *refs):
    weights, (out, gain_out) = refs[:-2], refs[-2:]
    at = query_w.shape[1]
    total = times_transposed(d_raw[:, :at], query_w[...])
    for k, weight in enumerate(weights):
        size = weight.shape[1] - (extra if k == len(weights) - 1 else 0)
        total += times_transposed(d_raw[:, at : at + size], weight[:, :size])
        at += size
    total += times_transposed(d_extra[...], weights[-1][:, -extra:])
    total += times_transposed(d_gate[...], gate_w[...])
    total = low(total)
    out[...] = total

    @pl.when(pl.program_id(0) == 0)
    def _():
        gain_out[...] = jnp.zeros(gain_out.shape, F32)

    values = inputs[...].astype(F32)
    gain_out[...] += jnp.sum(
        total.astype(F32) * (values * row_scale_of(values)), axis=0, keepdims=True
    )


def run_back_project(inputs, d_raw, d_extra, d_gate, weights):
    count, features = inputs.shape
    tile = min(TILE, count)
    tokens = lambda cols: pl.BlockSpec((tile, cols), lambda c: (c, 0))
    return pl.pallas_call(
        functools.partial(back_project_kernel, d_extra.shape[1]),
        grid=(count // tile,),
        in_specs=[tokens(array.shape[1]) for array in (inputs, d_raw, d_extra, d_gate)]
        + [once(weight.shape) for weight in weights],
        out_specs=[tokens(features), whole_spec(1, features)],
        out_shape=[
            jax.ShapeDtypeStruct((count, features), BF16),
            jax.ShapeDtypeStruct((1, features), F32),
        ],
        compiler_params=pltpu.CompilerParams(
            dimension_semantics=("arbitrary",), vmem_limit_bytes=VMEM_BYTES
        ),
        name="back_project",
    )(inputs, d_raw, d_extra, d_gate, *weights)


def mend_kernel(d_raw_in, tail, returned, same_after, taps, d_raw):
    row = lax.broadcasted_iota(jnp.int32, (8, 1), 0)
    spread = tail[...]
    for offset in range(1, taps.shape[0]):
        masked = returned[...] * same_after[:, offset : offset + 1] * taps[offset : offset + 1]
        moved = pltpu.roll(masked, 8 - offset, 0)
        spread = spread + jnp.where(row >= 8 - offset, moved, 0.0)
    d_raw[...] = low(jnp.concatenate([d_raw_in[...].astype(F32)[: HALO - 8], spread], 0))


def mend(d_raw, tail, returned, same_after, taps):
    count, columns = d_raw.shape
    last = count // HALO - 1
    rows = pl.BlockSpec((HALO, columns), lambda c: (last, 0))
    return pl.pallas_call(
        mend_kernel,
        grid=(1,),
        in_specs=[rows, whole_spec(8, columns), whole_spec(8, columns)]
        + [whole_spec(*same_after.shape), whole_spec(*taps.shape)],
        out_specs=rows,
        out_shape=jax.ShapeDtypeStruct(d_raw.shape, BF16),
        input_output_aliases={0: 0},
        compiler_params=pltpu.CompilerParams(dimension_semantics=("arbitrary",)),
        name="mend",
    )(d_raw, tail, returned, same_after, taps)


def shift_seq(array, by):
    count = lax.axis_size("seq")
    return lax.ppermute(
        array, "seq", [(i, i + by) for i in range(count) if 0 <= i + by < count]
    )


def swap_seq(array, distance):
    return lax.ppermute(array, "seq", [(i, i ^ distance) for i in range(lax.axis_size("seq"))])


def swap_head(array):
    return lax.ppermute(array, "head", [(0, 1), (1, 0)])


def head_sum(array):
    return array + swap_head(array)


def fine_low(form, former, latter):
    high, rest = split(former)
    return form(high, latter) + form(rest, latter)


def fine_first(form, former, latter):
    high, rest = split(latter)
    return form(former, high) + form(former, rest)


def join_kernel(final, shift_next, upper, group, other, before, group_out, low_out, before_out):
    heads, width, _ = group.shape

    @pl.when(upper[0] == 1)
    def _():
        lefts = [before] if final else [before, group]
        stacked = []
        for head in range(heads):
            pieces = []
            for left in lefts:
                pieces += list(split(left[head, :, :width]))
            stacked.append(product(jnp.concatenate(pieces, 0), other[head]))
        for head in range(heads):
            if final:
                before_out[head, :, :width] = before[head, :, :width]
                before_out[head, :, width:] = before[head, :, width:] + (
                    stacked[head][:width] + stacked[head][width:]
                )
                continue
            for at, (left, out) in enumerate(zip(lefts, (before_out, group_out))):
                start = 2 * at * width
                both = stacked[head][start : start + width]
                both = both + stacked[head][start + width : start + 2 * width]
                out[head, :, :width] = both[:, :width]
                out[head, :, width:] = both[:, width:] + left[head, :, width:]

    @pl.when(upper[0] == 0)
    def _():
        before_out[...] = before[...]
        if not final:
            for head in range(heads):
                theirs = other[head]
                mine = fine_first(product, theirs[:, :width], group[head])
                group_out[head, :, :width] = mine[:, :width]
                group_out[head, :, width:] = mine[:, width:] + theirs[:, width:].astype(F32)

    if final:
        low_out[...] = low(before_out[:, :, width:])
    else:
        low_out[...] = low(group_out[:, :, width:] if shift_next else group_out[...])


def join_groups(final, shift_next, upper, group, other, before):
    whole = pl.BlockSpec(memory_space=pltpu.VMEM)
    full = jax.ShapeDtypeStruct(group.shape, F32)
    sent = group.shape[1] if final or shift_next else group.shape[2]
    return pl.pallas_call(
        functools.partial(join_kernel, final, shift_next),
        in_specs=[pl.BlockSpec(memory_space=pltpu.SMEM), whole, whole, whole],
        out_specs=[whole, whole, whole],
        out_shape=[full, jax.ShapeDtypeStruct(group.shape[:2] + (sent,), BF16), full],
        compiler_params=pltpu.CompilerParams(vmem_limit_bytes=8 * 1024 * 1024),
        name="join_groups",
    )(upper, group, other, before)


def back_kernel(final, upper, group, other, after, group_map, other_map, after_map, *outs):
    group_out, low_out, after_out, after_map_out = outs
    heads, width, _ = group.shape
    after_out[...] = after[...]
    after_map_out[...] = after_map[...]
    if final:
        group_out[...] = group[...]

    @pl.when(upper[0] == 1)
    def _():
        if not final:
            for head in range(heads):
                theirs = other_map[head, :, :width]
                group_out[head] = other[head].astype(F32) + fine_first(
                    inner_rows, theirs, group[head]
                )

    @pl.when(upper[0] == 0)
    def _():
        stacked = []
        for head in range(heads):
            pieces = list(split(after_map[head]))
            if not final:
                pieces += list(split(group_map[head, :, :width]))
            stacked.append(inner_rows(jnp.concatenate(pieces, 1), other[head]))
        for head in range(heads):
            quarter = lambda k: stacked[head][k * width : (k + 1) * width]
            after_out[head] += quarter(0) + quarter(1)
            if not final:
                group_out[head] = group[head] + (quarter(2) + quarter(3))
                after_map_out[head] = fine_first(
                    product, other_map[head, :, :width], after_map[head]
                )

    low_out[...] = low(group_out[...])


def join_back(final, upper, group, other, after, group_map, other_map, after_map):
    whole = pl.BlockSpec(memory_space=pltpu.VMEM)
    full = jax.ShapeDtypeStruct(group.shape, F32)
    return pl.pallas_call(
        functools.partial(back_kernel, final),
        in_specs=[pl.BlockSpec(memory_space=pltpu.SMEM)] + [whole] * 6,
        out_specs=[whole] * 4,
        out_shape=[full, jax.ShapeDtypeStruct(group.shape, BF16), full, full],
        compiler_params=pltpu.CompilerParams(vmem_limit_bytes=8 * 1024 * 1024),
        name="join_back",
    )(upper, group, other, after, group_map, other_map, after_map)


def states_before(group, eye, beside):
    count, mine = lax.axis_size("seq"), lax.axis_index("seq")
    before = jnp.concatenate([eye, jnp.zeros_like(eye)], 2)
    group_low = low(group)
    kept = []
    distance = 1
    while distance < count:
        other = swap_seq(group_low, distance)
        if distance in beside:
            other, _ = tied(other, beside[distance]())
        upper = ((mine // distance) % 2).astype(jnp.int32).reshape(1)
        kept.append((group, other, upper))
        final = 2 * distance >= count
        group, group_low, before = join_groups(
            final, 4 * distance >= count, upper, group, other, before
        )
        distance *= 2
    return group_low, kept


def adjoints_after(own, kept, eye):
    group, group_low = own, low(own)
    after, after_map = jnp.zeros_like(own), eye
    distance = 1
    for group_map, other_map, upper in kept:
        other = swap_seq(group_low, distance)
        final = 2 * distance >= lax.axis_size("seq")
        group, group_low, after, after_map = join_back(
            final, upper, group, other, after, group_map, other_map, after_map
        )
        distance *= 2
    return after


def bit_orders(count):
    distances = [1 << k for k in range(count.bit_length() - 1)]
    near, far = distances[:3], distances[3:]
    return [near[k:] + near[:k] for k in range(len(near))], far


def scatter_view(array):
    count = lax.axis_size("seq")
    bits = count.bit_length() - 1
    return array.reshape((2,) * bits + (array.shape[0] // count, array.shape[1]))


def swap_all(arrays, distances):
    return [swap_seq(array, distance) for array, distance in zip(arrays, distances)]


def halve_all(terms, distances):
    keeps, sends = [], []
    for arrays, distance in zip(terms, distances):
        axis = arrays[0].ndim - 2 - distance.bit_length()
        own = (lax.axis_index("seq") // distance) % 2
        cut = lambda array, at: lax.dynamic_slice_in_dim(array, at, 1, axis).astype(F32)
        keeps.append(low(functools.reduce(jnp.add, [cut(array, own) for array in arrays])))
        sends.append(low(functools.reduce(jnp.add, [cut(array, 1 - own) for array in arrays])))
    return keeps, sends


def block_at(me, q, have, free, flipped):
    index, left = 0, len(free)
    for distance in have:
        if distance in free:
            left -= 1
            digit = (q // (1 << left)) % 2
        else:
            digit = (me // distance) % 2
            digit = 1 - digit if distance == flipped else digit
        index = index * 2 + digit
    return index


def halve_kernel(counts, me, *refs):
    ins, outs = refs[: 2 * sum(counts)], refs[2 * sum(counts) :]
    for part, count in enumerate(counts):
        for side in range(2):
            total = ins[0][...].astype(F32)
            for ref in ins[1:count]:
                total = total + ref[...].astype(F32)
            outs[2 * part + side][...] = low(total)
            ins = ins[count:]


def halve_parts(terms, haves, distances):
    rows = terms[0][0].shape[-2]
    arrays, specs, out_specs, shapes = [], [], [], []
    blocks = 1 << (min(len(have) for have in haves[0]) - 1)
    for part, part_haves, distance in zip(terms, haves, distances):
        free = [d for d in min(part_haves, key=len) if d != distance]
        columns = part[0].shape[-1]
        for flipped in (None, distance):
            for array, have in zip(part, part_haves):
                arrays.append(array.reshape(-1, columns))
                specs.append(
                    pl.BlockSpec(
                        (rows, columns),
                        lambda q, me, have=have, free=free, flipped=flipped: (
                            block_at(me[0], q, have, free, flipped), 0
                        ),
                    )
                )
            out_specs.append(pl.BlockSpec((rows, columns), lambda q, me: (q, 0)))
            shapes.append(jax.ShapeDtypeStruct((blocks * rows, columns), BF16))
    outs = pl.pallas_call(
        functools.partial(halve_kernel, [len(part) for part in terms]),
        grid_spec=pltpu.PrefetchScalarGridSpec(
            num_scalar_prefetch=1, grid=(blocks,), in_specs=specs, out_specs=out_specs
        ),
        out_shape=shapes,
        compiler_params=pltpu.CompilerParams(
            dimension_semantics=("arbitrary",), vmem_limit_bytes=VMEM_BYTES
        ),
        name="halve",
    )(lax.axis_index("seq").astype(jnp.int32).reshape(1), *arrays)
    return outs[0::2], outs[1::2]


def far_steps(terms, distances):
    for distance in distances:
        keeps, sends = halve_all(terms, [distance] * len(terms))
        merged = swap_seq(jnp.concatenate(sends, -1), distance)
        others, start = [], 0
        for send in sends:
            wide = send.shape[-1]
            others.append(lax.slice_in_dim(merged, start, start + wide, axis=merged.ndim - 1))
            start += wide
        terms = list(zip(keeps, others))
    return [
        functools.reduce(jnp.add, [a.astype(F32) for a in arrays]).reshape(arrays[0].shape[-2:])
        for arrays in terms
    ]


def gather_join(view, other, distance):
    axis = view.ndim - 2 - distance.bit_length()
    upper = (lax.axis_index("seq") // distance) % 2 == 1
    return jnp.concatenate(
        [jnp.where(upper, other, view), jnp.where(upper, view, other)], axis
    )


def lay_kernel(distances, me, *refs):
    parts = len(distances)
    for k, distance in enumerate(distances):
        upper = (me[0] // distance) % 2 == 1
        view, other, out = refs[2 * k], refs[2 * k + 1], refs[2 * parts + k]
        out[:, 0] = jnp.where(upper, other[...], view[...])
        out[:, 1] = jnp.where(upper, view[...], other[...])


def gather_lay(views, others, distances):
    rows = views[0].shape[-2]
    if rows < HALO:
        return [gather_join(*part) for part in zip(views, others, distances)]
    arrays, specs, out_specs, shapes, full = [], [], [], [], []
    for view, other, distance in zip(views, others, distances):
        axis = view.ndim - 2 - distance.bit_length()
        before, after = view.shape[:axis], view.shape[axis + 1 :]
        high = functools.reduce(lambda a, b: a * b, before, 1)
        short = functools.reduce(lambda a, b: a * b, after[:-2], 1)
        columns = view.shape[-1]
        group = max(1, high * short // 4)
        near_rows, far_rows = min(short, group), max(1, group // short)
        steps = short // near_rows
        place = lambda q, me, steps=steps: (q // steps, q % steps, 0, 0)
        specs += [pl.BlockSpec((far_rows, near_rows, rows, columns), place)] * 2
        out_specs.append(
            pl.BlockSpec(
                (far_rows, 2, near_rows, rows, columns),
                lambda q, me, steps=steps: (q // steps, 0, q % steps, 0, 0),
            )
        )
        arrays += [array.reshape(high, short, rows, columns) for array in (view, other)]
        shapes.append(jax.ShapeDtypeStruct((high, 2, short, rows, columns), BF16))
        full.append(before + (2,) + after)
        blocks = high * short // group
    outs = pl.pallas_call(
        functools.partial(lay_kernel, distances),
        grid_spec=pltpu.PrefetchScalarGridSpec(
            num_scalar_prefetch=1, grid=(blocks,), in_specs=specs, out_specs=out_specs
        ),
        out_shape=shapes,
        compiler_params=pltpu.CompilerParams(
            dimension_semantics=("arbitrary",), vmem_limit_bytes=VMEM_BYTES
        ),
        name="lay",
    )(lax.axis_index("seq").astype(jnp.int32).reshape(1), *arrays)
    return [out.reshape(shape) for out, shape in zip(outs, full)]


def gather_far(pack, distances):
    bits = lax.axis_size("seq").bit_length() - 1
    view = pack.reshape((1,) * bits + pack.shape)
    for distance in distances[::-1]:
        view = gather_join(view, swap_seq(view, distance), distance)
    return view


def gather_cut(view, widths):
    parts, at = [], 0
    for wide in widths:
        parts.append(lax.slice_in_dim(view, at, at + wide, axis=view.ndim - 1))
        at += wide
    return parts


def gather_end(views):
    return [view.reshape(-1, view.shape[-1]) for view in views]


def tied(*values):
    return lax.optimization_barrier(values)


def per_device(
    activations,
    log_decay,
    doc_starts,
    query_weight,
    key_weight,
    value_weight,
    beta_weight,
    gate_weight,
    out_weight,
    query_taps,
    key_taps,
    value_taps,
    mixer_gain,
    head_gain,
    feed_gain,
    feed_gate,
    feed_up,
    feed_down,
    cotangent,
):
    count, features = activations.shape
    tap_count = query_taps.shape[0]
    width = head_gain.shape[0]
    query_cols = query_weight.shape[1]
    key_cols = key_weight.shape[1]
    conv_cols = query_cols + 2 * key_cols
    hidden_cols = feed_gate.shape[1]
    head_count = query_cols // width
    beta_cols = beta_weight.shape[1]
    substeps = beta_cols // head_count
    device_rank = lax.axis_index("seq")
    head_rank = lax.axis_index("head")
    extra = 128
    shard_rows = query_weight.shape[0]
    orders, far = bit_orders(lax.axis_size("seq"))
    at_step = lambda k: [order[k] for order in orders]
    gather_at = lambda k: [order[2 - k] for order in orders]
    pad = jnp.zeros((shard_rows, extra - beta_cols - 2), BF16)
    kv_pack = jnp.concatenate(
        [key_weight, value_weight, beta_weight, mixer_gain[:, None], feed_gain[:, None], pad], 1
    )
    side_pack = jnp.concatenate([query_weight, gate_weight, out_weight.T], 1)
    feed_pack = jnp.concatenate([feed_gate, feed_up, feed_down.T], 1)
    third = -(-kv_pack.shape[1] // (3 * width)) * width
    input_edge = shift_seq(activations[count - HALO :], 1)
    kv_view = gather_far(kv_pack, far)
    kv_view, side_pack = tied(kv_view, side_pack)
    kv_parts = gather_cut(kv_view, [third, third, kv_pack.shape[1] - 2 * third])
    side_view = gather_far(side_pack, far)
    for k in range(3):
        others = swap_all(kv_parts, gather_at(k))
        kv_parts = [gather_join(v, o, d) for v, o, d in zip(kv_parts, others, gather_at(k))]
    side_parts = gather_cut(side_view, [query_cols] * 3)
    weights_kv = gather_end(kv_parts)
    weights_kv, side_parts, feed_pack, input_edge = tied(
        weights_kv, side_parts, feed_pack, input_edge
    )
    gains = weights_kv[2][:, -extra + beta_cols : -extra + beta_cols + 2].T.astype(F32)
    gain_one, gain_two = gains[0:1], gains[1:2]

    token_position = device_rank * count + jnp.arange(count, dtype=jnp.int32)
    is_start = jnp.any(token_position[:, None] == doc_starts[None, :], axis=1)

    def same_docs(position):
        doc = lambda p: jnp.sum((p[:, None] >= doc_starts[None, :]).astype(jnp.int32), axis=1)
        own = doc(position)
        return jnp.stack(
            [
                ((doc(position - offset) == own) & (position >= offset)).astype(F32)
                for offset in range(tap_count)
            ],
            1,
        )

    same = same_docs(token_position)
    log_gate = log_decay - RESET * is_start.astype(F32)[:, None]
    chunks = count // BLOCK
    cumulative = jnp.cumsum(log_gate.reshape(chunks, BLOCK, head_count), axis=1)
    cum_col = cumulative.reshape(count, head_count)
    cum_row = jnp.concatenate([jnp.swapaxes(cumulative, 1, 2)] * substeps, 2)
    taps_all = jnp.concatenate([query_taps, key_taps, value_taps], 1).astype(F32)

    side_others = swap_all(side_parts, gather_at(0))
    feed_view = gather_far(feed_pack, far)
    normed, edge_normed, raw_kv, edge_kv, sigmas = run_project(
        activations, input_edge, gain_one, weights_kv, 2 * key_cols, extra
    )
    beta_gate = sigmas[:, :beta_cols]
    eye = jnp.broadcast_to(jnp.eye(width, dtype=F32), (head_count, width, width))
    chain = jnp.concatenate([eye, jnp.zeros_like(eye)], 2)
    passed = ()
    feed_parts = None
    side_at, feed_at = 1, 0
    sides = [gather_join(v, o, d) for v, o, d in zip(side_parts, side_others, gather_at(0))]
    marks = [(chunks * k) // (AHEAD_CALLS * PAIR) * PAIR for k in range(AHEAD_CALLS + 1)]
    sends, distances = sides, gather_at(1)
    for call in range(AHEAD_CALLS):
        chain, sends = tied(chain, sends)
        others = swap_all(sends, distances)
        *passed, chain = run_forward(
            marks[call], marks[call + 1], raw_kv, edge_kv, taps_all, same, beta_gate, cum_col,
            cum_row, chain, tuple(passed), head_count, substeps, width,
        )
        if call == 0:
            chain, others, feed_view = tied(chain, others, feed_view)
        else:
            chain, others = tied(chain, others)
        sided = 3 if call < 2 else 0
        joined = [
            gather_join(v, o, d)
            for v, o, d in zip(sends[:sided], others[:sided], distances[:sided])
        ]
        if call > 0:
            joined += gather_lay(sends[sided:], others[sided:], distances[sided:])
        if call == 0:
            feed_parts = gather_cut(feed_view, [hidden_cols] * 3)
            sends, distances = joined + feed_parts, gather_at(2) + gather_at(0)
        elif call == 1:
            sides, sends, distances = joined[:3], joined[3:], gather_at(1)
        else:
            feed_parts = joined
    t_part, p_part, s_part, key_rows, solved = passed
    weight_query, weight_gate, weight_out = gather_end(sides)

    held = {}

    def first():
        held["side"] = run_project_side(normed, edge_normed, weight_query, weight_gate)
        return held["side"]

    state_low, kept = states_before(chain, eye, {2: first})
    raw_query, edge_query, gate_view = held["side"]
    state_low, feed_parts = tied(state_low, feed_parts)
    others = swap_all(feed_parts, gather_at(2))
    q_reach, local_out = run_query(
        raw_query, edge_query, taps_all, same, cum_col, cum_row, key_rows, solved,
        p_part, s_part, head_count, substeps, width,
    )
    head_gain_row = head_gain.astype(F32)[None]
    mixer_out, heads_out, branch_own, branch_low = run_heads(
        local_out, q_reach, state_low, gate_view, head_gain_row, weight_out, head_count, width
    )
    branch_low, others = tied(branch_low, others)
    (
        hidden, normed_ffn, activation, d_gate, d_up, branch_two, d_normed_own, d_normed_low,
    ) = run_feed(
        activations, branch_own, swap_head(branch_low), gain_two, cotangent,
        feed_parts, others, gather_at(2),
    )
    half = features // lax.axis_size("head")
    own_half = lambda array: lax.dynamic_slice_in_dim(array, head_rank * half, half, 1)
    other_half = lambda array: lax.dynamic_slice_in_dim(array, (1 - head_rank) * half, half, 1)
    output = low(
        own_half(hidden)
        + own_half(branch_two).astype(F32)
        + swap_head(other_half(branch_two)).astype(F32)
    )

    near = orders[0]
    grad_orders = [
        [near[1], near[2], near[0]],
        [near[0], near[1], near[2]],
        [near[2], near[0], near[1]],
        [near[2], near[0], near[1]],
        [near[2], near[1], near[0]],
    ]
    down_grad = scatter_view(low(inner_rows(cotangent, activation)))
    _, down_send = halve_all([(down_grad,)], [grad_orders[2][0]])
    d_normed_other, down_send = tied(swap_head(d_normed_low), down_send)
    down_other = swap_all(down_send, [grad_orders[2][0]])[0]
    (
        d_hidden, grad_mixer, d_gate_logit, d_mixer_low, own_part, grad_feed_gain, head_gain_part,
    ) = run_turn(
        hidden, d_normed_own, d_normed_other, gain_two, cotangent, weight_out,
        mixer_out, gate_view, head_gain_row, q_reach, head_count, width,
    )
    grad_feed_gain, head_gain_part = grad_feed_gain[0], head_gain_part[0]
    adjoint = adjoints_after(own_part, kept, eye)
    terms = [
        (scatter_view(low(inner_rows(normed_ffn, d_gate))),),
        (scatter_view(low(inner_rows(normed_ffn, d_up))),),
        (scatter_view(low(inner_rows(grad_mixer, heads_out))),),
        (scatter_view(low(inner_rows(normed, d_gate_logit))),),
    ]
    down_other, adjoint = tied(down_other, adjoint)
    marks = [chunks, (3 * chunks // 8) // PAIR * PAIR, (chunks // 8) // PAIR * PAIR, 0]
    carried = jnp.zeros((8, conv_cols), F32)
    tap_grads = jnp.zeros((tap_count, conv_cols), F32)
    passed = ()
    every = [1 << k for k in range(lax.axis_size("seq").bit_length() - 1)][::-1]
    left = [every] * 5
    haves = [[every]] * 5
    down_terms = (down_grad, down_other)
    bits = len(every)
    for call in range(3):
        distances = [order[call] for order in grad_orders]
        if call == 0:
            kinds = [0, 1, 3, 4]
            sends = halve_all(terms, [distances[k] for k in kinds])[1]
            keeps = [part[0] for part in terms]
            distances = [distances[k] for k in kinds]
        elif shard_rows < HALO:
            views = [
                (
                    [array.reshape((2,) * len(have) + array.shape[-2:]) for array, have in zip(*p)],
                    p[1],
                )
                for p in zip(terms, haves)
            ]
            sums = []
            for part, part_haves in views:
                small_have = min(part_haves, key=len)
                total = None
                for array, have in zip(part, part_haves):
                    for axis, d in reversed(list(enumerate(have))):
                        if d not in small_have:
                            array = lax.dynamic_index_in_dim(
                                array, (lax.axis_index("seq") // d) % 2, axis, keepdims=False
                            )
                    array = array.astype(F32)
                    total = array if total is None else total + array
                sums.append((total, small_have))
            keeps, sends = [], []
            for (total, have), d in zip(sums, distances):
                own = (lax.axis_index("seq") // d) % 2
                columns = total.shape[-1]
                pick = lambda at: low(
                    lax.dynamic_index_in_dim(total, at, have.index(d), keepdims=False)
                ).reshape(-1, columns)
                keeps.append(pick(own))
                sends.append(pick(1 - own))
        else:
            keeps, sends = halve_parts(terms, haves, distances)
        adjoint, sends, keeps = tied(adjoint, sends, keeps)
        others = swap_all(sends, distances)
        d_raw, d_beta_logit, new_tail, adjoint, carried, tap_grads = run_backward(
            marks[call + 1], marks[call],
            raw_query, edge_query, raw_kv, edge_kv, taps_all, same, beta_gate, cum_col, cum_row,
            t_part, p_part, s_part, state_low, d_mixer_low, adjoint, carried, tap_grads, passed,
            head_count, substeps, width,
        )
        if call == 0:
            tail = new_tail
        adjoint, carried, others = tied(adjoint, carried, others)
        passed = (d_raw, d_beta_logit)
        terms = [
            (k.reshape(-1, k.shape[-1]), o.reshape(-1, o.shape[-1])) for k, o in zip(keeps, others)
        ]
        if call == 0:
            down = tuple(array.reshape(-1, array.shape[-1]) for array in down_terms)
            terms = terms[:2] + [down] + terms[2:]
        left = [[d for d in l if d != order[call]] for l, order in zip(left, grad_orders)]
        haves = [[every if call == 0 else l, l] for l in left]
        cube = lambda a: a.reshape(-1, shard_rows, a.shape[-1])
        terms = [tuple(cube(a) for a in part) for part in terms]
    ones = (1,) * (bits - len(far))
    terms = [
        tuple(a.reshape((2,) * len(far) + ones + (shard_rows, a.shape[-1])) for a in part)
        for part in terms
    ]
    first_rows = carried
    zh_keeps, zh_sends = halve_all(terms, [far[0]] * len(terms))
    zh_other = swap_seq(jnp.concatenate(zh_sends, -1), far[0])
    returned = shift_seq(first_rows, -1)
    same_after = same_docs(token_position[-1] + 1 + jnp.arange(8, dtype=jnp.int32))
    d_raw = mend(d_raw, tail, returned, same_after, taps_all)
    d_beta_low = low(d_beta_logit)
    fifth = -(-conv_cols // (5 * width)) * width
    conv_marks = [0, 2 * fifth, 4 * fifth, conv_cols]
    keeps, sends = halve_all(
        [
            (scatter_view(low(inner_rows(normed, d_raw[:, a:b]))),)
            for a, b in zip(conv_marks[:-1], conv_marks[1:])
        ],
        at_step(0),
    )
    d_raw, d_beta_low, sends = tied(d_raw, d_beta_low, sends)
    others = swap_all(sends, at_step(0))
    d_extra = jnp.pad(d_beta_low, ((0, 0), (0, extra - beta_cols)))
    d_low, gain_part = run_back_project(
        activations, d_raw, d_extra, d_gate_logit, [weight_query, weight_gate, *weights_kv]
    )
    d_low, gain_part, others, zh_other = tied(d_low, gain_part, others, zh_other)
    start, feed_sums = 0, []
    for keep in zh_keeps:
        wide = keep.shape[-1]
        other = lax.slice_in_dim(zh_other, start, start + wide, axis=zh_other.ndim - 1)
        feed_sums.append((keep, other))
        start += wide
    feed_sums = far_steps(feed_sums, far[1:])
    both_heads = jnp.concatenate([gain_part[0], head_gain_part])
    both_heads = both_heads + swap_head(both_heads)
    d_other = swap_head(d_low)
    small = jnp.concatenate(
        [
            inner_rows(d_beta_low, normed).reshape(-1),
            both_heads[:features],
            grad_feed_gain,
            tap_grads.reshape(-1),
            both_heads[features:],
        ]
    )
    small = jnp.pad(small, (0, -small.shape[0] % 1024)).reshape(-1, 128)
    for at in (1, 2):
        keeps, sends = halve_all(list(zip(keeps, others)), at_step(at))
        small, sends, keeps = tied(small, sends, keeps)
        others = swap_all(sends, at_step(at))
        small = small + swap_seq(small, near[at - 1])
        if at == 1:
            d_normed = d_low.astype(F32) + d_other.astype(F32)
            d_input_norm, _ = norm_back(activations.astype(F32), gain_one, d_normed)
            grad_input = own_half(d_hidden + d_input_norm)
            grad_input, small, others = tied(grad_input, small, others)
        else:
            small, others = tied(small, others)
    conv_sum = jnp.concatenate(far_steps(list(zip(keeps, others)), far), 1)
    for distance in near[2:] + far:
        small = small + swap_seq(small, distance)
    small = small.reshape(-1)
    ends, at = [], 0
    for size in (beta_cols * features, features, features, tap_count * conv_cols, width):
        ends.append(small[at : at + size])
        at += size
    own_rows = lambda vector: lax.dynamic_slice_in_dim(
        vector, device_rank * shard_rows, shard_rows, vector.ndim - 1
    )
    tap_total = ends[3].reshape(tap_count, conv_cols)
    cut = lambda array, start, size: array[:, start : start + size]
    return (
        output,
        grad_input,
        cut(conv_sum, 0, query_cols),
        cut(conv_sum, query_cols, key_cols),
        cut(conv_sum, query_cols + key_cols, key_cols),
        own_rows(ends[0].reshape(beta_cols, features)).T,
        feed_sums[4],
        feed_sums[3].T,
        cut(tap_total, 0, query_cols),
        cut(tap_total, query_cols, key_cols),
        cut(tap_total, query_cols + key_cols, key_cols),
        own_rows(ends[1]),
        ends[4],
        own_rows(ends[2]),
        feed_sums[0],
        feed_sums[1],
        feed_sums[2].T,
    )


def solution(mesh):
    in_specs = (
        P("seq", None),
        P("seq", "head"),
        P(),
        P("seq", "head"),
        P("seq", "head"),
        P("seq", "head"),
        P("seq", "head"),
        P("seq", "head"),
        P("head", "seq"),
        P(None, "head"),
        P(None, "head"),
        P(None, "head"),
        P("seq"),
        P(),
        P("seq"),
        P("seq", "head"),
        P("seq", "head"),
        P("head", "seq"),
        P("seq", None),
    )
    out_specs = (
        P("seq", "head"),
        P("seq", "head"),
        P("seq", "head"),
        P("seq", "head"),
        P("seq", "head"),
        P("seq", "head"),
        P("seq", "head"),
        P("head", "seq"),
        P(None, "head"),
        P(None, "head"),
        P(None, "head"),
        P("seq"),
        P(),
        P("seq"),
        P("seq", "head"),
        P("seq", "head"),
        P("head", "seq"),
    )
    return jax.shard_map(
        per_device, mesh=mesh, in_specs=in_specs, out_specs=out_specs, check_vma=False
    )
```

```python
import functools

import jax
import jax.numpy as jnp
from jax import lax
from jax.experimental import pallas as pl
from jax.experimental.pallas import tpu as pltpu
from jax.sharding import PartitionSpec as P

BLOCK = 64
RESET = 256.0
HALO = 16
VMEM_BYTES = 63 * 1024 * 1024
PAIR = 2
QUERY_CHUNKS = 2
TILE = 256
LONG_TILE = 512
AHEAD_CALLS = 3
NORM_EPS = 1e-05
UNIT_EPS = 1e-06
F32 = jnp.float32
BF16 = jnp.bfloat16


def product(former, latter):
    return jnp.dot(former, latter, preferred_element_type=F32)


def inner_rows(former, latter):
    return lax.dot_general(former, latter, (((0,), (0,)), ((), ())), preferred_element_type=F32)


def times_transposed(former, latter):
    return lax.dot_general(former, latter, (((1,), (1,)), ((), ())), preferred_element_type=F32)


def low(values):
    return values.astype(BF16)


def split(values):
    high = values.astype(BF16)
    return high, (values - high.astype(F32)).astype(BF16)


def fine(form, former, latter):
    a_high, a_low = split(former)
    b_high, b_low = split(latter)
    return form(a_high, b_high) + (form(a_low, b_high) + form(a_high, b_low))


def silu_slope(values, sigma):
    return sigma * (1.0 + values * (1.0 - sigma))


def norm_back(values, gain_vector, gradient):
    row_scale = lax.rsqrt(jnp.mean(values * values, axis=-1, keepdims=True) + NORM_EPS)
    unit_value = values * row_scale
    scaled_grad = gradient * gain_vector
    back_value = row_scale * (
        scaled_grad - unit_value * jnp.mean(scaled_grad * unit_value, axis=-1, keepdims=True)
    )
    return (back_value, gradient * unit_value)


def row_maps(rows):
    row = lax.broadcasted_iota(jnp.int32, (rows, rows), 0)
    col = lax.broadcasted_iota(jnp.int32, (rows, rows), 1)
    return row % BLOCK, col % BLOCK, row // BLOCK, col // BLOCK


def lower_inverses(systems, apart):
    rows = systems[0].shape[0]
    row = lax.broadcasted_iota(jnp.int32, (rows, rows), 0)
    col = lax.broadcasted_iota(jnp.int32, (rows, rows), 1)
    eye = jnp.where(row == col, 1.0, 0.0)
    inverses = [eye - jnp.where(apart == 0, system, 0.0) for system in systems]
    level = 0
    while (1 << level) < BLOCK:
        joins = (apart >> level) == 1
        joints = [low(jnp.where(joins, system, 0.0)) for system in systems]
        lows = [low(inverse) for inverse in inverses]
        halves = [low(product(a, b)) for a, b in zip(lows, joints)]
        inverses = [c - product(a, b) for a, b, c in zip(halves, lows, inverses)]
        level += 1
    return inverses


def conv_rows(tile, halo, taps, same):
    count = tile.shape[0]
    extended = jnp.concatenate([halo, tile], 0)
    windows = [tile] + [
        pltpu.roll(extended, offset, 0)[8:] for offset in range(1, taps.shape[0])
    ]
    outcome = tile * taps[0:1]
    for offset in range(1, taps.shape[0]):
        outcome = outcome + windows[offset] * taps[offset : offset + 1] * same[:, offset : offset + 1]
    return outcome, windows


def unit_scale(values):
    return lax.rsqrt(jnp.sum(values * values, axis=-1, keepdims=True) + UNIT_EPS)


def pieces_of(head, head_count, substeps, width):
    query = [(head * width, width)]
    keys = [((head_count + head * substeps + n) * width, width) for n in range(substeps)]
    values = [
        ((head_count + (head_count + head) * substeps + n) * width, width) for n in range(substeps)
    ]
    return query + keys + values


def conv_of(source, first, start, size, taps, same_rows):
    tile_ref, before, edge, offset = source
    columns = slice(start - offset, start - offset + size)
    halo = jnp.where(first, edge[:, columns], before[:, columns]).astype(F32)[HALO - 8 :]
    return conv_rows(
        tile_ref[:, columns].astype(F32), halo, taps[:, start : start + size], same_rows
    )


def beta_rows(beta, head, substeps):
    columns = [beta[:, head * substeps + n : head * substeps + n + 1] for n in range(substeps)]
    return jnp.concatenate(columns, 0)


def forward_kernel(
    head_count, substeps, width, begin,
    raw, before, edge, taps, same, beta, cum_col, cum_row, chain_in, *refs,
):
    t_out, p_out, s_out, key_out, solved_out, chain = refs[-6:]
    step = pl.program_id(0)
    first = step + begin == 0
    rows = BLOCK * substeps
    row_token, col_token, row_step, col_step = row_maps(rows)
    upto = col_token <= row_token
    earlier = (col_token < row_token) | ((col_token == row_token) & (col_step < row_step))
    apart = row_token ^ col_token
    eye = jnp.where(
        lax.broadcasted_iota(jnp.int32, (width, width), 0)
        == lax.broadcasted_iota(jnp.int32, (width, width), 1),
        1.0,
        0.0,
    )
    same_rows = same[...]

    @pl.when(step == 0)
    def _():
        chain[...] = chain_in[...]

    heads = range(head_count)
    offset = head_count * width
    source = (raw, before, edge, offset)
    units = [(j, h) for j in range(PAIR) for h in heads]
    rows_at = [slice(j * BLOCK, (j + 1) * BLOCK) for j in range(PAIR)]
    keys, values, betas = {}, {}, {}
    for head in heads:
        acts = []
        for start, size in pieces_of(head, head_count, substeps, width)[1:]:
            pre, _ = conv_of(source, first, start, size, taps, same_rows)
            acts.append(pre * jax.nn.sigmoid(pre))
        acts = [a * unit_scale(a) for a in acts[:substeps]] + acts[substeps:]
        acts = [low(a) for a in acts]
        for j, at in enumerate(rows_at):
            keys[j, head] = jnp.concatenate([a[at] for a in acts[:substeps]], 0)
            values[j, head] = jnp.concatenate([a[at] for a in acts[substeps:]], 0)
            betas[j, head] = beta_rows(beta[at], head, substeps)
    keys, values, betas = ([held[u] for u in units] for held in (keys, values, betas))
    cum_rows = [jnp.concatenate([cum_col[rows_at[j], h : h + 1]] * substeps, 0) for j, h in units]
    cum_cols = [cum_row[j, h : h + 1, :] for j, h in units]
    lasts = [c[:, BLOCK - 1 : BLOCK] for c in cum_cols]
    ratios = [jnp.exp(jnp.where(upto, a - b, -1e4)) for a, b in zip(cum_rows, cum_cols)]
    grams = [times_transposed(key, key) for key in keys]
    systems = [
        jnp.where(earlier, beta_col * ratio * gram, 0.0)
        for beta_col, ratio, gram in zip(betas, ratios, grams)
    ]
    inverses = [low(inverse) for inverse in lower_inverses(systems, apart)]
    rights = [
        jnp.concatenate(
            [
                low(beta_col * jnp.exp(cum) * key.astype(F32)),
                low(beta_col * value.astype(F32)),
            ],
            1,
        )
        for beta_col, cum, key, value in zip(betas, cum_rows, keys, values)
    ]
    solved = [low(product(inverse, right)) for inverse, right in zip(inverses, rights)]
    ends = [
        low(jnp.exp(last - cum) * key.astype(F32))
        for last, cum, key in zip(lasts, cum_rows, keys)
    ]
    moved = [inner_rows(end, both) for end, both in zip(ends, solved)]
    step_maps = [split(jnp.exp(last) * eye - move[:, :width]) for last, move in zip(lasts, moved)]
    chains = [chain[head] for head in heads]
    for at, (j, head) in enumerate(units):
        t_out[j, head] = inverses[at]
        key_out[j, head] = keys[at]
        solved_out[j, head] = solved[at]
    for j in range(PAIR):
        at = j * head_count
        splits = [split(chained) for chained in chains]
        for head in heads:
            p_out[j, head] = splits[head][0][:, :width]
            s_out[j, head] = splits[head][0][:, width:]
        chains = [
            product(step_maps[at + h][0], splits[h][0])
            + (product(step_maps[at + h][1], splits[h][0]) + product(step_maps[at + h][0], splits[h][1]))
            for h in heads
        ]
        chains = [
            jnp.concatenate([c[:, :width], c[:, width:] + moved[at + h][:, width:]], 1)
            for h, c in enumerate(chains)
        ]
    for head in heads:
        chain[head] = chains[head]


def whole_spec(*shape):
    return pl.BlockSpec(shape, lambda *c: (0,) * len(shape))


def run_forward(
    begin, end, raw, edge, taps, same, beta, cum_col, cum_row, chain, passed,
    head_count, substeps, width,
):
    count, columns = raw.shape
    chunks = count // BLOCK
    rows = BLOCK * substeps
    begin, end = begin // PAIR, end // PAIR
    per_halo = PAIR * BLOCK // HALO
    tokens = lambda cols: pl.BlockSpec((PAIR * BLOCK, cols), lambda c: (c + begin, 0))
    tiles = lambda *shape: pl.BlockSpec((PAIR, head_count) + shape, lambda c: (c + begin, 0, 0, 0))
    shapes = [(rows, rows), (width, width), (width, width), (rows, width), (rows, 2 * width)]
    anywhere = pl.BlockSpec(memory_space=pl.ANY)
    return pl.pallas_call(
        functools.partial(forward_kernel, head_count, substeps, width, begin),
        grid=(end - begin,),
        in_specs=[
            tokens(columns),
            pl.BlockSpec(
                (HALO, columns), lambda c: (jnp.maximum((c + begin) * per_halo - 1, 0), 0)
            ),
            whole_spec(HALO, columns),
            whole_spec(*taps.shape),
            tokens(same.shape[1]),
            tokens(beta.shape[1]),
            tokens(head_count),
            pl.BlockSpec((PAIR, head_count, rows), lambda c: (c + begin, 0, 0)),
            whole_spec(*chain.shape),
        ]
        + [anywhere] * len(passed),
        out_specs=[tiles(*shape) for shape in shapes] + [whole_spec(*chain.shape)],
        out_shape=[
            jax.ShapeDtypeStruct((chunks, head_count) + shape, BF16) for shape in shapes
        ]
        + [jax.ShapeDtypeStruct(chain.shape, F32)],
        input_output_aliases={9 + k: k for k in range(len(passed))},
        compiler_params=pltpu.CompilerParams(
            dimension_semantics=("arbitrary",), vmem_limit_bytes=VMEM_BYTES
        ),
        name="mixer_forward",
    )(raw, raw, edge, taps, same, beta, cum_col, cum_row, chain, *passed)


def query_kernel(
    head_count, substeps, width,
    raw, before, edge, taps, same, cum_col, cum_row, key_in, solved_in, p_in, s_in,
    qtil_out, local_out,
):
    first = pl.program_id(0) == 0
    rows = BLOCK * substeps
    row_token, col_token, _, _ = row_maps(rows)
    upto = (col_token <= row_token)[:BLOCK]
    same_rows = same[...]
    heads = range(head_count)
    units = [(j, h) for j in range(QUERY_CHUNKS) for h in heads]
    rows_at = [slice(j * BLOCK, (j + 1) * BLOCK) for j in range(QUERY_CHUNKS)]
    queries = []
    for head in heads:
        start, size = pieces_of(head, head_count, substeps, width)[0]
        pre, _ = conv_of((raw, before, edge, 0), first, start, size, taps, same_rows)
        act = pre * jax.nn.sigmoid(pre)
        queries.append(low(act * unit_scale(act) * width ** (-0.5)))
    queries = [queries[h][rows_at[j]] for j, h in units]
    cum_rows = [cum_col[rows_at[j], h : h + 1] for j, h in units]
    ratios = [
        jnp.exp(jnp.where(upto, cum - cum_row[j, h : h + 1, :], -1e4))
        for cum, (j, h) in zip(cum_rows, units)
    ]
    scores = [times_transposed(query, key_in[j, h]) for query, (j, h) in zip(queries, units)]
    seen = [
        product(low(ratio * score), solved_in[j, h])
        for ratio, score, (j, h) in zip(ratios, scores, units)
    ]
    effective = [
        low(jnp.exp(cum) * query.astype(F32) - see[:, :width])
        for cum, query, see in zip(cum_rows, queries, seen)
    ]
    reached = [
        (product(eff, p_in[j, h]), product(eff, s_in[j, h]))
        for eff, (j, h) in zip(effective, units)
    ]
    for k, (j, h) in enumerate(units):
        at = slice(h * width, (h + 1) * width)
        qtil_out[rows_at[j], at] = low(reached[k][0])
        local_out[rows_at[j], at] = reached[k][1] + seen[k][:, width:]


def run_query(
    raw, edge, taps, same, cum_col, cum_row, key_rows, solved, p_part, s_part,
    head_count, substeps, width,
):
    count, columns = raw.shape
    chunks = count // BLOCK
    rows = BLOCK * substeps
    per_halo = QUERY_CHUNKS * BLOCK // HALO
    tokens = lambda cols: pl.BlockSpec((QUERY_CHUNKS * BLOCK, cols), lambda c: (c, 0))
    tiles = lambda *shape: pl.BlockSpec((QUERY_CHUNKS, head_count) + shape, lambda c: (c, 0, 0, 0))
    return pl.pallas_call(
        functools.partial(query_kernel, head_count, substeps, width),
        grid=(chunks // QUERY_CHUNKS,),
        in_specs=[
            tokens(columns),
            pl.BlockSpec((HALO, columns), lambda c: (jnp.maximum(c * per_halo - 1, 0), 0)),
            whole_spec(HALO, columns),
            whole_spec(*taps.shape),
            tokens(same.shape[1]),
            tokens(head_count),
            pl.BlockSpec((QUERY_CHUNKS, head_count, rows), lambda c: (c, 0, 0)),
            tiles(rows, width),
            tiles(rows, 2 * width),
            tiles(width, width),
            tiles(width, width),
        ],
        out_specs=[tokens(columns), tokens(columns)],
        out_shape=[
            jax.ShapeDtypeStruct((count, columns), BF16),
            jax.ShapeDtypeStruct((count, columns), F32),
        ],
        compiler_params=pltpu.CompilerParams(
            dimension_semantics=("arbitrary",), vmem_limit_bytes=VMEM_BYTES
        ),
        name="mixer_query",
    )(raw, raw, edge, taps, same, cum_col, cum_row, key_rows, solved, p_part, s_part)


def backward_kernel(
    head_count, substeps, width, end,
    raw_q, before_q, edge_q, raw, before, edge, taps, same, same_next, beta, cum_col, cum_row,
    t_in, p_in, s_in, state_in, d_out, adjoint_in, carried_in, tap_in, *refs,
):
    d_raw, d_logit, tail_out, adjoint, carried, tap_out, tail_next = refs[-7:]
    step = pl.program_id(0)
    pair = end - 1 - step
    rows = BLOCK * substeps
    tap_count = taps.shape[0]
    count = PAIR * BLOCK
    row_token, col_token, row_step, col_step = row_maps(rows)
    upto = col_token <= row_token
    earlier = (col_token < row_token) | ((col_token == row_token) & (col_step < row_step))
    same_rows = same[...]
    same_long = jnp.concatenate([same_rows, same_next[...]], 0)

    @pl.when(step == 0)
    def _():
        adjoint[...] = adjoint_in[...]
        carried[...] = carried_in[...]
        tap_out[...] = tap_in[...]

    heads = range(head_count)
    units_at = [(j, h) for j in range(PAIR) for h in heads]
    rows_at = [slice(j * BLOCK, (j + 1) * BLOCK) for j in range(PAIR)]
    pieces = [pieces_of(head, head_count, substeps, width) for head in heads]
    pres, sigmas, scales, units = [], [], [], []
    queries, keys, values, betas = {}, {}, {}, {}
    key_start = head_count * width
    sources = [(raw_q, before_q, edge_q, 0), (raw, before, edge, key_start)]

    def windows_of(start, size):
        return conv_of(sources[int(start >= key_start)], pair == 0, start, size, taps, same_rows)

    for head in heads:
        pre = [windows_of(start, size)[0] for start, size in pieces[head]]
        sigma = [jax.nn.sigmoid(p) for p in pre]
        acts = [p * s for p, s in zip(pre, sigma)]
        pres.append(pre)
        sigmas.append(sigma)
        scales.append([unit_scale(a) for a in acts[: 1 + substeps]])
        units.append([a * s for a, s in zip(acts[: 1 + substeps], scales[head])])
        query = low(units[head][0] * width ** (-0.5))
        key = [low(unit) for unit in units[head][1:]]
        value = [low(act) for act in acts[1 + substeps :]]
        for j, at in enumerate(rows_at):
            queries[j, head] = query[at]
            keys[j, head] = jnp.concatenate([k[at] for k in key], 0)
            values[j, head] = jnp.concatenate([v[at] for v in value], 0)
            betas[j, head] = beta_rows(beta[at], head, substeps)
    queries, keys, values, betas = (
        [held[u] for u in units_at] for held in (queries, keys, values, betas)
    )
    cum_rows = [
        jnp.concatenate([cum_col[rows_at[j], h : h + 1]] * substeps, 0) for j, h in units_at
    ]
    cum_cols = [cum_row[j, h : h + 1, :] for j, h in units_at]
    lasts = [c[:, BLOCK - 1 : BLOCK] for c in cum_cols]
    ratios = [jnp.exp(jnp.where(upto, a - b, -1e4)) for a, b in zip(cum_rows, cum_cols)]
    carries = [jnp.exp(c) for c in cum_rows]
    end_ratios = [jnp.exp(last - c) for last, c in zip(lasts, cum_rows)]
    inverses = [t_in[j, h] for j, h in units_at]
    d_mixes = [d_out[rows_at[j], h * width : (h + 1) * width] for j, h in units_at]
    states = [
        low(s_in[j, h].astype(F32) + product(p_in[j, h], state_in[h])) for j, h in units_at
    ]
    stacks = [jnp.concatenate([query, key], 0) for query, key in zip(queries, keys)]
    both_grams = [times_transposed(stack, key) for stack, key in zip(stacks, keys)]
    grams = [both[BLOCK:] for both in both_grams]
    masks = [low(ratio[:BLOCK] * both[:BLOCK]) for ratio, both in zip(ratios, both_grams)]
    d_both = [
        inner_rows(
            jnp.concatenate([mask, low(carry[:BLOCK] * query.astype(F32))], 1), d_mix
        )
        for mask, carry, query, d_mix in zip(masks, carries, queries, d_mixes)
    ]
    d_seen = [both[:rows] for both in d_both]
    d_reach = [both[rows:] for both in d_both]
    end_keys = [low(end * key.astype(F32)) for end, key in zip(end_ratios, keys)]
    start_keys = [
        low((beta_col * carry) * key.astype(F32))
        for beta_col, carry, key in zip(betas, carries, keys)
    ]
    freshes = [
        value.astype(F32) - carry * product(key, state)
        for value, carry, key, state in zip(values, carries, keys, states)
    ]
    updates = [
        low(product(inverse, low(beta_col * fresh)))
        for inverse, beta_col, fresh in zip(inverses, betas, freshes)
    ]
    laters_low, d_rights, d_rights_low = {}, {}, {}
    for j in range(PAIR - 1, -1, -1):
        ids = [j * head_count + h for h in heads]
        laters = [adjoint[h] for h in heads]
        for h, at in enumerate(ids):
            laters_low[at] = low(laters[h])
        d_updates = [low(d_seen[at] + product(end_keys[at], laters_low[at])) for at in ids]
        for h, at in enumerate(ids):
            d_rights[at] = inner_rows(inverses[at], d_updates[h])
            d_rights_low[at] = low(d_rights[at])
        for h, at in enumerate(ids):
            adjoint[h] = (
                jnp.exp(lasts[at]) * laters[h]
                + d_reach[at]
                - inner_rows(start_keys[at], d_rights_low[at])
            )
    ids = range(len(units_at))
    outer = [jnp.concatenate([d_mixes[at], d_rights_low[at]], 0) for at in ids]
    by_update = [times_transposed(outer[at], updates[at]) for at in ids]
    by_state = [times_transposed(outer[at], states[at]) for at in ids]
    d_systems = [
        jnp.where(earlier, -by_update[at][BLOCK:] * ratios[at], 0.0) for at in ids
    ]
    d_scores = [by_update[at][:BLOCK] * ratios[at][:BLOCK] for at in ids]
    d_grams = [betas[at] * d_systems[at] for at in ids]
    d_scores = [low(d_score) for d_score in d_scores]
    d_grams = [low(d_gram + jnp.transpose(d_gram)) for d_gram in d_grams]
    d_betas = [
        jnp.sum(d_rights[at] * freshes[at], axis=-1, keepdims=True)
        + jnp.sum(d_systems[at] * grams[at], axis=-1, keepdims=True)
        for at in ids
    ]
    d_queries = [
        carries[at][:BLOCK] * by_state[at][:BLOCK] + product(d_scores[at], keys[at])
        for at in ids
    ]
    d_keys = [
        inner_rows(jnp.concatenate([d_scores[at], d_grams[at]], 0), stacks[at])
        + end_ratios[at] * times_transposed(updates[at], laters_low[at])
        - (betas[at] * carries[at]) * by_state[at][BLOCK:]
        for at in ids
    ]
    for j in range(PAIR):
        logit_cols = []
        for h in heads:
            at = j * head_count + h
            logits = d_betas[at] * betas[at] * (1.0 - betas[at])
            logit_cols += [logits[n * BLOCK : (n + 1) * BLOCK] for n in range(substeps)]
        logit_cols.append(jnp.zeros((BLOCK, width - len(logit_cols)), F32))
        d_logit[rows_at[j], :] = low(jnp.concatenate(logit_cols, 1))

    for head in heads:
        mine = [j * head_count + head for j in range(PAIR)]
        step_rows = lambda arrays, n: jnp.concatenate(
            [array[n * BLOCK : (n + 1) * BLOCK] for array in arrays], 0
        )
        d_value = [betas[at] * d_rights[at] for at in mine]
        grads = [width ** (-0.5) * jnp.concatenate([d_queries[at] for at in mine], 0)]
        grads += [step_rows([d_keys[at] for at in mine], n) for n in range(substeps)]
        grads += [step_rows(d_value, n) for n in range(substeps)]
        for at, (start, size) in enumerate(pieces[head]):
            grad = grads[at]
            if at <= substeps:
                unit = units[head][at]
                grad = scales[head][at] * (
                    grad - unit * jnp.sum(grad * unit, axis=-1, keepdims=True)
                )
            grad = grad * silu_slope(pres[head][at], sigmas[head][at])
            windows = windows_of(start, size)[1]
            long = jnp.concatenate([grad, carried[:, start : start + size]], 0)
            tap = taps[:, start : start + size]
            spread = grad * tap[0:1]
            sums = [jnp.sum(grad * windows[0], axis=0, keepdims=True)]
            for offset in range(1, tap_count):
                masked = long * same_long[:, offset : offset + 1]
                spread = spread + (
                    pltpu.roll(masked, count + 8 - offset, 0)[:count] * tap[offset : offset + 1]
                )
                sums.append(jnp.sum(masked[:count] * windows[offset], axis=0, keepdims=True))
            carried[:, start : start + size] = grad[:8]
            tap_out[:, start : start + size] += jnp.concatenate(sums, 0)
            d_raw[:, start : start + size] = low(spread)
            tail_next[:, start : start + size] = spread[count - 8 :]

    @pl.when(step == 0)
    def _():
        tail_out[...] = tail_next[...]


def run_backward(
    begin, end, raw_q, edge_q, raw, edge, taps, same, beta, cum_col, cum_row, t_part, p_part,
    s_part, state_in, d_out, adjoint, carried, tap_grads, passed, head_count, substeps, width,
):
    count = raw.shape[0]
    columns = taps.shape[1]
    chunks = count // BLOCK
    rows = BLOCK * substeps
    begin, end, chunks = begin // PAIR, end // PAIR, chunks // PAIR
    per_halo = PAIR * BLOCK // HALO
    per_eight = PAIR * BLOCK // 8
    tokens = lambda cols: pl.BlockSpec((PAIR * BLOCK, cols), lambda c: (end - 1 - c, 0))
    halo = lambda cols: pl.BlockSpec(
        (HALO, cols), lambda c: (jnp.maximum((end - 1 - c) * per_halo - 1, 0), 0)
    )
    tiles = lambda *shape: pl.BlockSpec((PAIR, head_count) + shape, lambda c: (end - 1 - c, 0, 0, 0))
    anywhere = pl.BlockSpec(memory_space=pl.ANY)
    state = (head_count, width, width)
    sources = []
    for array in (raw_q, raw):
        cols = array.shape[1]
        sources += [tokens(cols), halo(cols), whole_spec(HALO, cols)]
    return pl.pallas_call(
        functools.partial(backward_kernel, head_count, substeps, width, end),
        grid=(end - begin,),
        in_specs=sources
        + [
            whole_spec(*taps.shape),
            tokens(same.shape[1]),
            pl.BlockSpec(
                (8, same.shape[1]),
                lambda c: (jnp.minimum((end - c) * per_eight, chunks * per_eight - 1), 0),
            ),
            tokens(beta.shape[1]),
            tokens(head_count),
            pl.BlockSpec((PAIR, head_count, rows), lambda c: (end - 1 - c, 0, 0)),
            tiles(rows, rows),
            tiles(width, width),
            tiles(width, width),
            whole_spec(*state),
            tokens(head_count * width),
            whole_spec(*state),
            whole_spec(8, columns),
            whole_spec(*taps.shape),
        ]
        + [anywhere] * len(passed),
        out_specs=[
            tokens(columns),
            tokens(width),
            whole_spec(8, columns),
            whole_spec(*state),
            whole_spec(8, columns),
            whole_spec(*taps.shape),
        ],
        out_shape=[
            jax.ShapeDtypeStruct((count, columns), BF16),
            jax.ShapeDtypeStruct((count, width), BF16),
            jax.ShapeDtypeStruct((8, columns), F32),
            jax.ShapeDtypeStruct(state, F32),
            jax.ShapeDtypeStruct((8, columns), F32),
            jax.ShapeDtypeStruct(taps.shape, F32),
        ],
        scratch_shapes=[pltpu.VMEM((8, columns), F32)],
        input_output_aliases={20 + k: k for k in range(len(passed))},
        compiler_params=pltpu.CompilerParams(
            dimension_semantics=("arbitrary",), vmem_limit_bytes=VMEM_BYTES
        ),
        name="mixer_backward",
    )(
        raw_q, raw_q, edge_q, raw, raw, edge, taps, same, same, beta, cum_col, cum_row,
        t_part, p_part, s_part, state_in, d_out, adjoint, carried, tap_grads, *passed,
    )


def row_scale_of(values):
    return lax.rsqrt(jnp.mean(values * values, axis=-1, keepdims=True) + NORM_EPS)


def project_kernel(parts, raw_cols, inputs, edge, gain, *refs):
    weights, outs = refs[:parts], refs[parts:]
    normed_out, edge_normed, raw_out, edge_out, extra_out = outs
    gain_row = gain[...]

    def rows_of(values):
        values = values.astype(F32)
        return low(values * row_scale_of(values) * gain_row)

    def fill(normed, raw_ref, extra_ref):
        at = 0
        for weight in weights:
            cols = weight.shape[1]
            both = product(normed, weight[...])
            raw_part = min(cols, raw_cols - at)
            raw_ref[:, at : at + raw_part] = low(both[:, :raw_part])
            if extra_ref is not None and raw_part < cols:
                extra_ref[...] = jax.nn.sigmoid(both[:, raw_part:])
            at += cols

    normed = rows_of(inputs[...])
    normed_out[...] = normed
    fill(normed, raw_out, extra_out)

    @pl.when(pl.program_id(0) == 0)
    def _():
        normed_edge = rows_of(edge[...])
        edge_normed[...] = normed_edge
        fill(normed_edge, edge_out, None)


def once(shape):
    return pl.BlockSpec(shape, lambda *c: (0,) * len(shape), pipeline_mode=pl.Buffered(1))


def run_project(inputs, edge, gain, weights, raw_cols, extra):
    count, features = inputs.shape
    tile = min(TILE, count)
    tokens = lambda cols: pl.BlockSpec((tile, cols), lambda c: (c, 0))
    return pl.pallas_call(
        functools.partial(project_kernel, len(weights), raw_cols),
        grid=(count // tile,),
        in_specs=[tokens(features), whole_spec(HALO, features), whole_spec(1, features)]
        + [once(weight.shape) for weight in weights],
        out_specs=[
            tokens(features), whole_spec(HALO, features), tokens(raw_cols),
            whole_spec(HALO, raw_cols), tokens(extra),
        ],
        out_shape=[
            jax.ShapeDtypeStruct((count, features), BF16),
            jax.ShapeDtypeStruct((HALO, features), BF16),
            jax.ShapeDtypeStruct((count, raw_cols), BF16),
            jax.ShapeDtypeStruct((HALO, raw_cols), BF16),
            jax.ShapeDtypeStruct((count, extra), F32),
        ],
        compiler_params=pltpu.CompilerParams(
            dimension_semantics=("arbitrary",), vmem_limit_bytes=VMEM_BYTES
        ),
        name="project",
    )(inputs, edge, gain, *weights)


def project_side_kernel(normed, edge, query_w, gate_w, raw_out, edge_out, gate_out):
    raw_out[...] = low(product(normed[...], query_w[...]))
    gate_out[...] = product(normed[...], gate_w[...])

    @pl.when(pl.program_id(0) == 0)
    def _():
        edge_out[...] = low(product(edge[...], query_w[...]))


def run_project_side(normed, edge, query_w, gate_w):
    count, features = normed.shape
    cols = query_w.shape[1]
    tile = min(LONG_TILE, count)
    tokens = lambda cols: pl.BlockSpec((tile, cols), lambda c: (c, 0))
    return pl.pallas_call(
        project_side_kernel,
        grid=(count // tile,),
        in_specs=[
            tokens(features), whole_spec(HALO, features), once(query_w.shape), once(gate_w.shape)
        ],
        out_specs=[tokens(cols), whole_spec(HALO, cols), tokens(cols)],
        out_shape=[
            jax.ShapeDtypeStruct((count, cols), BF16),
            jax.ShapeDtypeStruct((HALO, cols), BF16),
            jax.ShapeDtypeStruct((count, cols), F32),
        ],
        compiler_params=pltpu.CompilerParams(
            dimension_semantics=("arbitrary",), vmem_limit_bytes=VMEM_BYTES
        ),
        name="project_side",
    )(normed, edge, query_w, gate_w)


def heads_kernel(
    head_count, width,
    local, reach, state, gate, gain, weight,
    mixer_out, heads_out, own_out, low_out,
):
    gain_row = gain[...]
    for h in range(head_count):
        at = slice(h * width, (h + 1) * width)
        mixer = local[:, at] + product(reach[:, at], state[h])
        logit = gate[:, at]
        mixer_out[:, at] = mixer
        heads_out[:, at] = low(
            mixer * row_scale_of(mixer) * gain_row * (logit * jax.nn.sigmoid(logit))
        )
    branch = times_transposed(heads_out[...], weight[...])
    own_out[...] = branch
    low_out[...] = low(branch)


def run_heads(local, reach, state, gate, gain, weight, head_count, width):
    count, cols = local.shape
    features = weight.shape[0]
    tile = min(LONG_TILE, count)
    tokens = lambda cols: pl.BlockSpec((tile, cols), lambda c: (c, 0))
    return pl.pallas_call(
        functools.partial(heads_kernel, head_count, width),
        grid=(count // tile,),
        in_specs=[
            tokens(cols), tokens(cols), whole_spec(*state.shape), tokens(cols),
            whole_spec(*gain.shape), once(weight.shape),
        ],
        out_specs=[tokens(cols), tokens(cols), tokens(features), tokens(features)],
        out_shape=[
            jax.ShapeDtypeStruct((count, cols), F32),
            jax.ShapeDtypeStruct((count, cols), BF16),
            jax.ShapeDtypeStruct((count, features), F32),
            jax.ShapeDtypeStruct((count, features), BF16),
        ],
        compiler_params=pltpu.CompilerParams(
            dimension_semantics=("arbitrary",), vmem_limit_bytes=VMEM_BYTES
        ),
        name="heads",
    )(local, reach, state, gate, gain, weight)


def lay_copies(view, other, own, short, rows, scratch, semaphores):
    run = short * rows
    copies = []
    for block in range(view.shape[0] // run):
        for side, at in ((view, own), (other, 1 - own)):
            row = pl.multiple_of((2 * block + at) * run, run)
            copies.append(
                pltpu.make_async_copy(
                    side.at[pl.ds(block * run, run)],
                    scratch.at[pl.ds(row, run)],
                    semaphores.at[len(copies)],
                )
            )
    return copies


def feed_kernel(runs, rows, me, inputs, own, other, gain, cotangent, *refs):
    halves, outs, rest = refs[:6], refs[6:14], refs[14:]
    hidden_out, normed_out, act_out, d_gate_out, d_up_out, branch_out, own_out, low_out = outs
    gate_w, up_w, down_w = rest[:3]

    @pl.when(pl.program_id(0) == 0)
    def _():
        copies = []
        for k, short in enumerate(runs):
            copies += lay_copies(
                halves[2 * k], halves[2 * k + 1], (me[0] // short) % 2, short, rows, rest[k],
                rest[3 + k],
            )
        for copy in copies:
            copy.start()
        for copy in copies:
            copy.wait()

    hidden = inputs[...].astype(F32) + own[...] + other[...].astype(F32)
    hidden_out[...] = hidden
    normed = low(hidden * row_scale_of(hidden) * gain[...])
    normed_out[...] = normed
    gate = product(normed, gate_w[...])
    up = product(normed, up_w[...])
    d_act = product(cotangent[...], down_w[...])
    sigma = jax.nn.sigmoid(gate)
    act = gate * sigma
    activation = low(act * up)
    d_up = low(d_act * act)
    d_gate = low(d_act * up * silu_slope(gate, sigma))
    act_out[...] = activation
    d_gate_out[...] = d_gate
    d_up_out[...] = d_up
    branch_out[...] = low(times_transposed(activation, down_w[...]))
    d_normed = times_transposed(d_gate, gate_w[...]) + times_transposed(d_up, up_w[...])
    own_out[...] = d_normed
    low_out[...] = low(d_normed)


def run_feed(inputs, own, other, gain, cotangent, views, others, distances):
    rows = views[0].shape[-2]
    if rows < HALO:
        full = gather_end([gather_join(*part) for part in zip(views, others, distances)])
        half = full[0].shape[0] // 2
        views, others = [w[:half] for w in full], [w[half:] for w in full]
        distances, rows, me = [1] * 3, half, jnp.zeros((1,), jnp.int32)
    else:
        views, others = gather_end(views), gather_end(others)
        me = lax.axis_index("seq").astype(jnp.int32).reshape(1)
    halves = [half for pair in zip(views, others) for half in pair]
    count, features = inputs.shape
    cols = views[0].shape[1]
    tile = min(TILE, count)
    tokens = lambda cols: pl.BlockSpec((tile, cols), lambda c: (c, 0))
    shape = lambda cols, kind: jax.ShapeDtypeStruct((count, cols), kind)
    return pl.pallas_call(
        functools.partial(feed_kernel, distances, rows),
        grid=(count // tile,),
        in_specs=[pl.BlockSpec(memory_space=pltpu.SMEM)]
        + [tokens(features)] * 3
        + [whole_spec(1, features), tokens(features)]
        + [pl.BlockSpec(memory_space=pl.ANY)] * 6,
        scratch_shapes=[pltpu.VMEM((2 * view.shape[0], cols), BF16) for view in views]
        + [
            pltpu.SemaphoreType.DMA((2 * (view.shape[0] // (short * rows)),))
            for view, short in zip(views, distances)
        ],
        out_specs=[tokens(features)] * 2 + [tokens(cols)] * 3 + [tokens(features)] * 3,
        out_shape=[shape(features, F32), shape(features, BF16)]
        + [shape(cols, BF16)] * 3
        + [shape(features, BF16), shape(features, F32), shape(features, BF16)],
        compiler_params=pltpu.CompilerParams(
            dimension_semantics=("arbitrary",), vmem_limit_bytes=VMEM_BYTES
        ),
        name="feed",
    )(me, inputs, own, other, gain, cotangent, *halves)


def turn_kernel(
    head_count, width,
    hidden, own, other, gain, cotangent, weight, mixer_in, gate, head_gain, reach,
    d_hidden_out, d_low_out, d_gate_out, d_mixer_out, state_out, feed_gain_out, head_gain_out,
):
    @pl.when(pl.program_id(0) == 0)
    def _():
        state_out[...] = jnp.zeros(state_out.shape, F32)
        feed_gain_out[...] = jnp.zeros(feed_gain_out.shape, F32)
        head_gain_out[...] = jnp.zeros(head_gain_out.shape, F32)

    d_normed = own[...] + other[...].astype(F32)
    back, terms = norm_back(hidden[...], gain[...], d_normed)
    feed_gain_out[...] += jnp.sum(terms, axis=0, keepdims=True)
    d_hidden = cotangent[...].astype(F32) + back
    d_hidden_out[...] = d_hidden
    d_low = low(d_hidden)
    d_low_out[...] = d_low
    d_heads = product(d_low, weight[...])
    gain_row = head_gain[...]
    for h in range(head_count):
        at = slice(h * width, (h + 1) * width)
        mixer = mixer_in[:, at]
        unit = mixer * row_scale_of(mixer)
        logit = gate[:, at]
        sigma = jax.nn.sigmoid(logit)
        d_head = d_heads[:, at]
        d_gate_out[:, at] = low(d_head * (unit * gain_row) * silu_slope(logit, sigma))
        d_mixer, head_terms = norm_back(mixer, gain_row, d_head * (logit * sigma))
        head_gain_out[...] += jnp.sum(head_terms, axis=0, keepdims=True)
        d_mixer_low = low(d_mixer)
        d_mixer_out[:, at] = d_mixer_low
        state_out[h] += inner_rows(reach[:, at], d_mixer_low)


def run_turn(
    hidden, own, other, gain, cotangent, weight, mixer, gate, head_gain, reach, head_count, width
):
    count, features = hidden.shape
    cols = mixer.shape[1]
    tile = min(LONG_TILE, count)
    tokens = lambda cols: pl.BlockSpec((tile, cols), lambda c: (c, 0))
    shape = lambda cols, kind: jax.ShapeDtypeStruct((count, cols), kind)
    state = (head_count, width, width)
    return pl.pallas_call(
        functools.partial(turn_kernel, head_count, width),
        grid=(count // tile,),
        in_specs=[tokens(features)] * 3
        + [whole_spec(1, features), tokens(features), once(weight.shape)]
        + [tokens(cols), tokens(cols), whole_spec(1, width), tokens(cols)],
        out_specs=[tokens(features)] * 2
        + [tokens(cols)] * 2
        + [whole_spec(*state), whole_spec(1, features), whole_spec(1, width)],
        out_shape=[shape(features, F32), shape(features, BF16)]
        + [shape(cols, BF16)] * 2
        + [
            jax.ShapeDtypeStruct(state, F32),
            jax.ShapeDtypeStruct((1, features), F32),
            jax.ShapeDtypeStruct((1, width), F32),
        ],
        compiler_params=pltpu.CompilerParams(
            dimension_semantics=("arbitrary",), vmem_limit_bytes=VMEM_BYTES
        ),
        name="turn",
    )(hidden, own, other, gain, cotangent, weight, mixer, gate, head_gain, reach)


def back_project_kernel(extra, inputs, d_raw, d_extra, d_gate, query_w, gate_w, *refs):
    weights, (out, gain_out) = refs[:-2], refs[-2:]
    at = query_w.shape[1]
    total = times_transposed(d_raw[:, :at], query_w[...])
    for k, weight in enumerate(weights):
        size = weight.shape[1] - (extra if k == len(weights) - 1 else 0)
        total += times_transposed(d_raw[:, at : at + size], weight[:, :size])
        at += size
    total += times_transposed(d_extra[...], weights[-1][:, -extra:])
    total += times_transposed(d_gate[...], gate_w[...])
    total = low(total)
    out[...] = total

    @pl.when(pl.program_id(0) == 0)
    def _():
        gain_out[...] = jnp.zeros(gain_out.shape, F32)

    values = inputs[...].astype(F32)
    gain_out[...] += jnp.sum(
        total.astype(F32) * (values * row_scale_of(values)), axis=0, keepdims=True
    )


def run_back_project(inputs, d_raw, d_extra, d_gate, weights):
    count, features = inputs.shape
    tile = min(TILE, count)
    tokens = lambda cols: pl.BlockSpec((tile, cols), lambda c: (c, 0))
    return pl.pallas_call(
        functools.partial(back_project_kernel, d_extra.shape[1]),
        grid=(count // tile,),
        in_specs=[tokens(array.shape[1]) for array in (inputs, d_raw, d_extra, d_gate)]
        + [once(weight.shape) for weight in weights],
        out_specs=[tokens(features), whole_spec(1, features)],
        out_shape=[
            jax.ShapeDtypeStruct((count, features), BF16),
            jax.ShapeDtypeStruct((1, features), F32),
        ],
        compiler_params=pltpu.CompilerParams(
            dimension_semantics=("arbitrary",), vmem_limit_bytes=VMEM_BYTES
        ),
        name="back_project",
    )(inputs, d_raw, d_extra, d_gate, *weights)


def mend_kernel(d_raw_in, tail, returned, same_after, taps, d_raw):
    row = lax.broadcasted_iota(jnp.int32, (8, 1), 0)
    spread = tail[...]
    for offset in range(1, taps.shape[0]):
        masked = returned[...] * same_after[:, offset : offset + 1] * taps[offset : offset + 1]
        moved = pltpu.roll(masked, 8 - offset, 0)
        spread = spread + jnp.where(row >= 8 - offset, moved, 0.0)
    d_raw[...] = low(jnp.concatenate([d_raw_in[...].astype(F32)[: HALO - 8], spread], 0))


def mend(d_raw, tail, returned, same_after, taps):
    count, columns = d_raw.shape
    last = count // HALO - 1
    rows = pl.BlockSpec((HALO, columns), lambda c: (last, 0))
    return pl.pallas_call(
        mend_kernel,
        grid=(1,),
        in_specs=[rows, whole_spec(8, columns), whole_spec(8, columns)]
        + [whole_spec(*same_after.shape), whole_spec(*taps.shape)],
        out_specs=rows,
        out_shape=jax.ShapeDtypeStruct(d_raw.shape, BF16),
        input_output_aliases={0: 0},
        compiler_params=pltpu.CompilerParams(dimension_semantics=("arbitrary",)),
        name="mend",
    )(d_raw, tail, returned, same_after, taps)


def shift_seq(array, by):
    count = lax.axis_size("seq")
    return lax.ppermute(
        array, "seq", [(i, i + by) for i in range(count) if 0 <= i + by < count]
    )


def swap_seq(array, distance):
    return lax.ppermute(array, "seq", [(i, i ^ distance) for i in range(lax.axis_size("seq"))])


def swap_head(array):
    return lax.ppermute(array, "head", [(0, 1), (1, 0)])


def head_sum(array):
    return array + swap_head(array)


def fine_low(form, former, latter):
    high, rest = split(former)
    return form(high, latter) + form(rest, latter)


def fine_first(form, former, latter):
    high, rest = split(latter)
    return form(former, high) + form(former, rest)


def join_kernel(final, shift_next, upper, group, other, before, group_out, low_out, before_out):
    heads, width, _ = group.shape

    @pl.when(upper[0] == 1)
    def _():
        lefts = [before] if final else [before, group]
        stacked = []
        for head in range(heads):
            pieces = []
            for left in lefts:
                pieces += list(split(left[head, :, :width]))
            stacked.append(product(jnp.concatenate(pieces, 0), other[head]))
        for head in range(heads):
            if final:
                before_out[head, :, :width] = before[head, :, :width]
                before_out[head, :, width:] = before[head, :, width:] + (
                    stacked[head][:width] + stacked[head][width:]
                )
                continue
            for at, (left, out) in enumerate(zip(lefts, (before_out, group_out))):
                start = 2 * at * width
                both = stacked[head][start : start + width]
                both = both + stacked[head][start + width : start + 2 * width]
                out[head, :, :width] = both[:, :width]
                out[head, :, width:] = both[:, width:] + left[head, :, width:]

    @pl.when(upper[0] == 0)
    def _():
        before_out[...] = before[...]
        if not final:
            for head in range(heads):
                theirs = other[head]
                mine = fine_first(product, theirs[:, :width], group[head])
                group_out[head, :, :width] = mine[:, :width]
                group_out[head, :, width:] = mine[:, width:] + theirs[:, width:].astype(F32)

    if final:
        low_out[...] = low(before_out[:, :, width:])
    else:
        low_out[...] = low(group_out[:, :, width:] if shift_next else group_out[...])


def join_groups(final, shift_next, upper, group, other, before):
    whole = pl.BlockSpec(memory_space=pltpu.VMEM)
    full = jax.ShapeDtypeStruct(group.shape, F32)
    sent = group.shape[1] if final or shift_next else group.shape[2]
    return pl.pallas_call(
        functools.partial(join_kernel, final, shift_next),
        in_specs=[pl.BlockSpec(memory_space=pltpu.SMEM), whole, whole, whole],
        out_specs=[whole, whole, whole],
        out_shape=[full, jax.ShapeDtypeStruct(group.shape[:2] + (sent,), BF16), full],
        compiler_params=pltpu.CompilerParams(vmem_limit_bytes=8 * 1024 * 1024),
        name="join_groups",
    )(upper, group, other, before)


def back_kernel(final, upper, group, other, after, group_map, other_map, after_map, *outs):
    group_out, low_out, after_out, after_map_out = outs
    heads, width, _ = group.shape
    after_out[...] = after[...]
    after_map_out[...] = after_map[...]
    if final:
        group_out[...] = group[...]

    @pl.when(upper[0] == 1)
    def _():
        if not final:
            for head in range(heads):
                theirs = other_map[head, :, :width]
                group_out[head] = other[head].astype(F32) + fine_first(
                    inner_rows, theirs, group[head]
                )

    @pl.when(upper[0] == 0)
    def _():
        stacked = []
        for head in range(heads):
            pieces = list(split(after_map[head]))
            if not final:
                pieces += list(split(group_map[head, :, :width]))
            stacked.append(inner_rows(jnp.concatenate(pieces, 1), other[head]))
        for head in range(heads):
            quarter = lambda k: stacked[head][k * width : (k + 1) * width]
            after_out[head] += quarter(0) + quarter(1)
            if not final:
                group_out[head] = group[head] + (quarter(2) + quarter(3))
                after_map_out[head] = fine_first(
                    product, other_map[head, :, :width], after_map[head]
                )

    low_out[...] = low(group_out[...])


def join_back(final, upper, group, other, after, group_map, other_map, after_map):
    whole = pl.BlockSpec(memory_space=pltpu.VMEM)
    full = jax.ShapeDtypeStruct(group.shape, F32)
    return pl.pallas_call(
        functools.partial(back_kernel, final),
        in_specs=[pl.BlockSpec(memory_space=pltpu.SMEM)] + [whole] * 6,
        out_specs=[whole] * 4,
        out_shape=[full, jax.ShapeDtypeStruct(group.shape, BF16), full, full],
        compiler_params=pltpu.CompilerParams(vmem_limit_bytes=8 * 1024 * 1024),
        name="join_back",
    )(upper, group, other, after, group_map, other_map, after_map)


def states_before(group, eye, beside):
    count, mine = lax.axis_size("seq"), lax.axis_index("seq")
    before = jnp.concatenate([eye, jnp.zeros_like(eye)], 2)
    group_low = low(group)
    kept = []
    distance = 1
    while distance < count:
        other = swap_seq(group_low, distance)
        if distance in beside:
            other, _ = tied(other, beside[distance]())
        upper = ((mine // distance) % 2).astype(jnp.int32).reshape(1)
        kept.append((group, other, upper))
        final = 2 * distance >= count
        group, group_low, before = join_groups(
            final, 4 * distance >= count, upper, group, other, before
        )
        distance *= 2
    return group_low, kept


def adjoints_after(own, kept, eye):
    group, group_low = own, low(own)
    after, after_map = jnp.zeros_like(own), eye
    distance = 1
    for group_map, other_map, upper in kept:
        other = swap_seq(group_low, distance)
        final = 2 * distance >= lax.axis_size("seq")
        group, group_low, after, after_map = join_back(
            final, upper, group, other, after, group_map, other_map, after_map
        )
        distance *= 2
    return after


def bit_orders(count):
    distances = [1 << k for k in range(count.bit_length() - 1)]
    near, far = distances[:3], distances[3:]
    return [near[k:] + near[:k] for k in range(len(near))], far


def scatter_view(array):
    count = lax.axis_size("seq")
    bits = count.bit_length() - 1
    return array.reshape((2,) * bits + (array.shape[0] // count, array.shape[1]))


def swap_all(arrays, distances):
    return [swap_seq(array, distance) for array, distance in zip(arrays, distances)]


def halve_all(terms, distances):
    keeps, sends = [], []
    for arrays, distance in zip(terms, distances):
        axis = arrays[0].ndim - 2 - distance.bit_length()
        own = (lax.axis_index("seq") // distance) % 2
        cut = lambda array, at: lax.dynamic_slice_in_dim(array, at, 1, axis).astype(F32)
        keeps.append(low(functools.reduce(jnp.add, [cut(array, own) for array in arrays])))
        sends.append(low(functools.reduce(jnp.add, [cut(array, 1 - own) for array in arrays])))
    return keeps, sends


def block_at(me, q, have, free, flipped):
    index, left = 0, len(free)
    for distance in have:
        if distance in free:
            left -= 1
            digit = (q // (1 << left)) % 2
        else:
            digit = (me // distance) % 2
            digit = 1 - digit if distance == flipped else digit
        index = index * 2 + digit
    return index


def halve_kernel(counts, me, *refs):
    ins, outs = refs[: 2 * sum(counts)], refs[2 * sum(counts) :]
    for part, count in enumerate(counts):
        for side in range(2):
            total = ins[0][...].astype(F32)
            for ref in ins[1:count]:
                total = total + ref[...].astype(F32)
            outs[2 * part + side][...] = low(total)
            ins = ins[count:]


def halve_parts(terms, haves, distances):
    rows = terms[0][0].shape[-2]
    arrays, specs, out_specs, shapes = [], [], [], []
    blocks = 1 << (min(len(have) for have in haves[0]) - 1)
    for part, part_haves, distance in zip(terms, haves, distances):
        free = [d for d in min(part_haves, key=len) if d != distance]
        columns = part[0].shape[-1]
        for flipped in (None, distance):
            for array, have in zip(part, part_haves):
                arrays.append(array.reshape(-1, columns))
                specs.append(
                    pl.BlockSpec(
                        (rows, columns),
                        lambda q, me, have=have, free=free, flipped=flipped: (
                            block_at(me[0], q, have, free, flipped), 0
                        ),
                    )
                )
            out_specs.append(pl.BlockSpec((rows, columns), lambda q, me: (q, 0)))
            shapes.append(jax.ShapeDtypeStruct((blocks * rows, columns), BF16))
    outs = pl.pallas_call(
        functools.partial(halve_kernel, [len(part) for part in terms]),
        grid_spec=pltpu.PrefetchScalarGridSpec(
            num_scalar_prefetch=1, grid=(blocks,), in_specs=specs, out_specs=out_specs
        ),
        out_shape=shapes,
        compiler_params=pltpu.CompilerParams(
            dimension_semantics=("arbitrary",), vmem_limit_bytes=VMEM_BYTES
        ),
        name="halve",
    )(lax.axis_index("seq").astype(jnp.int32).reshape(1), *arrays)
    return outs[0::2], outs[1::2]


def far_steps(terms, distances):
    for distance in distances:
        keeps, sends = halve_all(terms, [distance] * len(terms))
        merged = swap_seq(jnp.concatenate(sends, -1), distance)
        others, start = [], 0
        for send in sends:
            wide = send.shape[-1]
            others.append(lax.slice_in_dim(merged, start, start + wide, axis=merged.ndim - 1))
            start += wide
        terms = list(zip(keeps, others))
    return [
        functools.reduce(jnp.add, [a.astype(F32) for a in arrays]).reshape(arrays[0].shape[-2:])
        for arrays in terms
    ]


def gather_join(view, other, distance):
    axis = view.ndim - 2 - distance.bit_length()
    upper = (lax.axis_index("seq") // distance) % 2 == 1
    return jnp.concatenate(
        [jnp.where(upper, other, view), jnp.where(upper, view, other)], axis
    )


def lay_kernel(distances, me, *refs):
    parts = len(distances)
    for k, distance in enumerate(distances):
        upper = (me[0] // distance) % 2 == 1
        view, other, out = refs[2 * k], refs[2 * k + 1], refs[2 * parts + k]
        out[:, 0] = jnp.where(upper, other[...], view[...])
        out[:, 1] = jnp.where(upper, view[...], other[...])


def gather_lay(views, others, distances):
    rows = views[0].shape[-2]
    if rows < HALO:
        return [gather_join(*part) for part in zip(views, others, distances)]
    arrays, specs, out_specs, shapes, full = [], [], [], [], []
    for view, other, distance in zip(views, others, distances):
        axis = view.ndim - 2 - distance.bit_length()
        before, after = view.shape[:axis], view.shape[axis + 1 :]
        high = functools.reduce(lambda a, b: a * b, before, 1)
        short = functools.reduce(lambda a, b: a * b, after[:-2], 1)
        columns = view.shape[-1]
        group = max(1, high * short // 4)
        near_rows, far_rows = min(short, group), max(1, group // short)
        steps = short // near_rows
        place = lambda q, me, steps=steps: (q // steps, q % steps, 0, 0)
        specs += [pl.BlockSpec((far_rows, near_rows, rows, columns), place)] * 2
        out_specs.append(
            pl.BlockSpec(
                (far_rows, 2, near_rows, rows, columns),
                lambda q, me, steps=steps: (q // steps, 0, q % steps, 0, 0),
            )
        )
        arrays += [array.reshape(high, short, rows, columns) for array in (view, other)]
        shapes.append(jax.ShapeDtypeStruct((high, 2, short, rows, columns), BF16))
        full.append(before + (2,) + after)
        blocks = high * short // group
    outs = pl.pallas_call(
        functools.partial(lay_kernel, distances),
        grid_spec=pltpu.PrefetchScalarGridSpec(
            num_scalar_prefetch=1, grid=(blocks,), in_specs=specs, out_specs=out_specs
        ),
        out_shape=shapes,
        compiler_params=pltpu.CompilerParams(
            dimension_semantics=("arbitrary",), vmem_limit_bytes=VMEM_BYTES
        ),
        name="lay",
    )(lax.axis_index("seq").astype(jnp.int32).reshape(1), *arrays)
    return [out.reshape(shape) for out, shape in zip(outs, full)]


def gather_far(pack, distances):
    bits = lax.axis_size("seq").bit_length() - 1
    view = pack.reshape((1,) * bits + pack.shape)
    for distance in distances[::-1]:
        view = gather_join(view, swap_seq(view, distance), distance)
    return view


def gather_cut(view, widths):
    parts, at = [], 0
    for wide in widths:
        parts.append(lax.slice_in_dim(view, at, at + wide, axis=view.ndim - 1))
        at += wide
    return parts


def gather_end(views):
    return [view.reshape(-1, view.shape[-1]) for view in views]


def tied(*values):
    return lax.optimization_barrier(values)


def per_device(
    activations,
    log_decay,
    doc_starts,
    query_weight,
    key_weight,
    value_weight,
    beta_weight,
    gate_weight,
    out_weight,
    query_taps,
    key_taps,
    value_taps,
    mixer_gain,
    head_gain,
    feed_gain,
    feed_gate,
    feed_up,
    feed_down,
    cotangent,
):
    count, features = activations.shape
    tap_count = query_taps.shape[0]
    width = head_gain.shape[0]
    query_cols = query_weight.shape[1]
    key_cols = key_weight.shape[1]
    conv_cols = query_cols + 2 * key_cols
    hidden_cols = feed_gate.shape[1]
    head_count = query_cols // width
    beta_cols = beta_weight.shape[1]
    substeps = beta_cols // head_count
    device_rank = lax.axis_index("seq")
    head_rank = lax.axis_index("head")
    extra = 128
    shard_rows = query_weight.shape[0]
    orders, far = bit_orders(lax.axis_size("seq"))
    at_step = lambda k: [order[k] for order in orders]
    gather_at = lambda k: [order[2 - k] for order in orders]
    pad = jnp.zeros((shard_rows, extra - beta_cols - 2), BF16)
    kv_pack = jnp.concatenate(
        [key_weight, value_weight, beta_weight, mixer_gain[:, None], feed_gain[:, None], pad], 1
    )
    side_pack = jnp.concatenate([query_weight, gate_weight, out_weight.T], 1)
    feed_pack = jnp.concatenate([feed_gate, feed_up, feed_down.T], 1)
    third = -(-kv_pack.shape[1] // (3 * width)) * width
    input_edge = shift_seq(activations[count - HALO :], 1)
    kv_view = gather_far(kv_pack, far)
    kv_view, side_pack = tied(kv_view, side_pack)
    kv_parts = gather_cut(kv_view, [third, third, kv_pack.shape[1] - 2 * third])
    side_view = gather_far(side_pack, far)
    for k in range(3):
        others = swap_all(kv_parts, gather_at(k))
        kv_parts = [gather_join(v, o, d) for v, o, d in zip(kv_parts, others, gather_at(k))]
    side_parts = gather_cut(side_view, [query_cols] * 3)
    weights_kv = gather_end(kv_parts)
    weights_kv, side_parts, feed_pack, input_edge = tied(
        weights_kv, side_parts, feed_pack, input_edge
    )
    gains = weights_kv[2][:, -extra + beta_cols : -extra + beta_cols + 2].T.astype(F32)
    gain_one, gain_two = gains[0:1], gains[1:2]

    token_position = device_rank * count + jnp.arange(count, dtype=jnp.int32)
    is_start = jnp.any(token_position[:, None] == doc_starts[None, :], axis=1)

    def same_docs(position):
        doc = lambda p: jnp.sum((p[:, None] >= doc_starts[None, :]).astype(jnp.int32), axis=1)
        own = doc(position)
        return jnp.stack(
            [
                ((doc(position - offset) == own) & (position >= offset)).astype(F32)
                for offset in range(tap_count)
            ],
            1,
        )

    same = same_docs(token_position)
    log_gate = log_decay - RESET * is_start.astype(F32)[:, None]
    chunks = count // BLOCK
    cumulative = jnp.cumsum(log_gate.reshape(chunks, BLOCK, head_count), axis=1)
    cum_col = cumulative.reshape(count, head_count)
    cum_row = jnp.concatenate([jnp.swapaxes(cumulative, 1, 2)] * substeps, 2)
    taps_all = jnp.concatenate([query_taps, key_taps, value_taps], 1).astype(F32)

    side_others = swap_all(side_parts, gather_at(0))
    feed_view = gather_far(feed_pack, far)
    normed, edge_normed, raw_kv, edge_kv, sigmas = run_project(
        activations, input_edge, gain_one, weights_kv, 2 * key_cols, extra
    )
    beta_gate = sigmas
    eye = jnp.broadcast_to(jnp.eye(width, dtype=F32), (head_count, width, width))
    chain = jnp.concatenate([eye, jnp.zeros_like(eye)], 2)
    passed = ()
    feed_parts = None
    side_at, feed_at = 1, 0
    sides = [gather_join(v, o, d) for v, o, d in zip(side_parts, side_others, gather_at(0))]
    marks = [(chunks * k) // (AHEAD_CALLS * PAIR) * PAIR for k in range(AHEAD_CALLS + 1)]
    sends, distances = sides, gather_at(1)
    for call in range(AHEAD_CALLS):
        chain, sends = tied(chain, sends)
        others = swap_all(sends, distances)
        *passed, chain = run_forward(
            marks[call], marks[call + 1], raw_kv, edge_kv, taps_all, same, beta_gate, cum_col,
            cum_row, chain, tuple(passed), head_count, substeps, width,
        )
        if call == 0:
            chain, others, feed_view = tied(chain, others, feed_view)
        else:
            chain, others = tied(chain, others)
        sided = 3 if call < 2 else 0
        joined = [
            gather_join(v, o, d)
            for v, o, d in zip(sends[:sided], others[:sided], distances[:sided])
        ]
        if call > 0:
            joined += gather_lay(sends[sided:], others[sided:], distances[sided:])
        if call == 0:
            feed_parts = gather_cut(feed_view, [hidden_cols] * 3)
            sends, distances = joined + feed_parts, gather_at(2) + gather_at(0)
        elif call == 1:
            sides, sends, distances = joined[:3], joined[3:], gather_at(1)
        else:
            feed_parts = joined
    t_part, p_part, s_part, key_rows, solved = passed
    weight_query, weight_gate, weight_out = gather_end(sides)

    held = {}

    def first():
        held["side"] = run_project_side(normed, edge_normed, weight_query, weight_gate)
        return held["side"]

    state_low, kept = states_before(chain, eye, {2: first})
    raw_query, edge_query, gate_view = held["side"]
    state_low, feed_parts = tied(state_low, feed_parts)
    others = swap_all(feed_parts, gather_at(2))
    q_reach, local_out = run_query(
        raw_query, edge_query, taps_all, same, cum_col, cum_row, key_rows, solved,
        p_part, s_part, head_count, substeps, width,
    )
    head_gain_row = head_gain.astype(F32)[None]
    mixer_out, heads_out, branch_own, branch_low = run_heads(
        local_out, q_reach, state_low, gate_view, head_gain_row, weight_out, head_count, width
    )
    branch_low, others = tied(branch_low, others)
    (
        hidden, normed_ffn, activation, d_gate, d_up, branch_two, d_normed_own, d_normed_low,
    ) = run_feed(
        activations, branch_own, swap_head(branch_low), gain_two, cotangent,
        feed_parts, others, gather_at(2),
    )
    half = features // lax.axis_size("head")
    own_half = lambda array: lax.dynamic_slice_in_dim(array, head_rank * half, half, 1)
    other_half = lambda array: lax.dynamic_slice_in_dim(array, (1 - head_rank) * half, half, 1)
    output = low(
        own_half(hidden)
        + own_half(branch_two).astype(F32)
        + swap_head(other_half(branch_two)).astype(F32)
    )

    near = orders[0]
    grad_orders = [
        [near[1], near[2], near[0]],
        [near[0], near[1], near[2]],
        [near[2], near[0], near[1]],
        [near[2], near[0], near[1]],
        [near[2], near[1], near[0]],
    ]
    down_grad = scatter_view(low(inner_rows(cotangent, activation)))
    _, down_send = halve_all([(down_grad,)], [grad_orders[2][0]])
    d_normed_other, down_send = tied(swap_head(d_normed_low), down_send)
    down_other = swap_all(down_send, [grad_orders[2][0]])[0]
    (
        d_hidden, grad_mixer, d_gate_logit, d_mixer_low, own_part, grad_feed_gain, head_gain_part,
    ) = run_turn(
        hidden, d_normed_own, d_normed_other, gain_two, cotangent, weight_out,
        mixer_out, gate_view, head_gain_row, q_reach, head_count, width,
    )
    grad_feed_gain, head_gain_part = grad_feed_gain[0], head_gain_part[0]
    adjoint = adjoints_after(own_part, kept, eye)
    terms = [
        (scatter_view(low(inner_rows(normed_ffn, d_gate))),),
        (scatter_view(low(inner_rows(normed_ffn, d_up))),),
        (scatter_view(low(inner_rows(grad_mixer, heads_out))),),
        (scatter_view(low(inner_rows(normed, d_gate_logit))),),
    ]
    down_other, adjoint = tied(down_other, adjoint)
    marks = [chunks, (3 * chunks // 8) // PAIR * PAIR, (chunks // 8) // PAIR * PAIR, 0]
    carried = jnp.zeros((8, conv_cols), F32)
    tap_grads = jnp.zeros((tap_count, conv_cols), F32)
    passed = ()
    every = [1 << k for k in range(lax.axis_size("seq").bit_length() - 1)][::-1]
    left = [every] * 5
    haves = [[every]] * 5
    down_terms = (down_grad, down_other)
    bits = len(every)
    for call in range(3):
        distances = [order[call] for order in grad_orders]
        if call == 0:
            kinds = [0, 1, 3, 4]
            sends = halve_all(terms, [distances[k] for k in kinds])[1]
            keeps = [part[0] for part in terms]
            distances = [distances[k] for k in kinds]
        elif shard_rows < HALO:
            views = [
                (
                    [array.reshape((2,) * len(have) + array.shape[-2:]) for array, have in zip(*p)],
                    p[1],
                )
                for p in zip(terms, haves)
            ]
            sums = []
            for part, part_haves in views:
                small_have = min(part_haves, key=len)
                total = None
                for array, have in zip(part, part_haves):
                    for axis, d in reversed(list(enumerate(have))):
                        if d not in small_have:
                            array = lax.dynamic_index_in_dim(
                                array, (lax.axis_index("seq") // d) % 2, axis, keepdims=False
                            )
                    array = array.astype(F32)
                    total = array if total is None else total + array
                sums.append((total, small_have))
            keeps, sends = [], []
            for (total, have), d in zip(sums, distances):
                own = (lax.axis_index("seq") // d) % 2
                columns = total.shape[-1]
                pick = lambda at: low(
                    lax.dynamic_index_in_dim(total, at, have.index(d), keepdims=False)
                ).reshape(-1, columns)
                keeps.append(pick(own))
                sends.append(pick(1 - own))
        else:
            keeps, sends = halve_parts(terms, haves, distances)
        adjoint, sends, keeps = tied(adjoint, sends, keeps)
        others = swap_all(sends, distances)
        d_raw, d_beta_logit, new_tail, adjoint, carried, tap_grads = run_backward(
            marks[call + 1], marks[call],
            raw_query, edge_query, raw_kv, edge_kv, taps_all, same, beta_gate, cum_col, cum_row,
            t_part, p_part, s_part, state_low, d_mixer_low, adjoint, carried, tap_grads, passed,
            head_count, substeps, width,
        )
        if call == 0:
            tail = new_tail
        adjoint, carried, others = tied(adjoint, carried, others)
        passed = (d_raw, d_beta_logit)
        terms = [
            (k.reshape(-1, k.shape[-1]), o.reshape(-1, o.shape[-1])) for k, o in zip(keeps, others)
        ]
        if call == 0:
            down = tuple(array.reshape(-1, array.shape[-1]) for array in down_terms)
            terms = terms[:2] + [down] + terms[2:]
        left = [[d for d in l if d != order[call]] for l, order in zip(left, grad_orders)]
        haves = [[every if call == 0 else l, l] for l in left]
        cube = lambda a: a.reshape(-1, shard_rows, a.shape[-1])
        terms = [tuple(cube(a) for a in part) for part in terms]
    ones = (1,) * (bits - len(far))
    terms = [
        tuple(a.reshape((2,) * len(far) + ones + (shard_rows, a.shape[-1])) for a in part)
        for part in terms
    ]
    first_rows = carried
    zh_keeps, zh_sends = halve_all(terms, [far[0]] * len(terms))
    zh_other = swap_seq(jnp.concatenate(zh_sends, -1), far[0])
    returned = shift_seq(first_rows, -1)
    same_after = same_docs(token_position[-1] + 1 + jnp.arange(8, dtype=jnp.int32))
    d_raw = mend(d_raw, tail, returned, same_after, taps_all)
    d_beta_low = d_beta_logit
    fifth = -(-conv_cols // (5 * width)) * width
    conv_marks = [0, 2 * fifth, 4 * fifth, conv_cols]
    keeps, sends = halve_all(
        [
            (scatter_view(low(inner_rows(normed, d_raw[:, a:b]))),)
            for a, b in zip(conv_marks[:-1], conv_marks[1:])
        ],
        at_step(0),
    )
    d_raw, d_beta_low, sends = tied(d_raw, d_beta_low, sends)
    others = swap_all(sends, at_step(0))
    d_extra = d_beta_low
    d_low, gain_part = run_back_project(
        activations, d_raw, d_extra, d_gate_logit, [weight_query, weight_gate, *weights_kv]
    )
    d_low, gain_part, others, zh_other = tied(d_low, gain_part, others, zh_other)
    start, feed_sums = 0, []
    for keep in zh_keeps:
        wide = keep.shape[-1]
        other = lax.slice_in_dim(zh_other, start, start + wide, axis=zh_other.ndim - 1)
        feed_sums.append((keep, other))
        start += wide
    feed_sums = far_steps(feed_sums, far[1:])
    both_heads = jnp.concatenate([gain_part[0], head_gain_part])
    both_heads = both_heads + swap_head(both_heads)
    d_other = swap_head(d_low)
    small = jnp.concatenate(
        [
            inner_rows(d_beta_low, normed)[:beta_cols].reshape(-1),
            both_heads[:features],
            grad_feed_gain,
            tap_grads.reshape(-1),
            both_heads[features:],
        ]
    )
    small = jnp.pad(small, (0, -small.shape[0] % 1024)).reshape(-1, 128)
    for at in (1, 2):
        keeps, sends = halve_all(list(zip(keeps, others)), at_step(at))
        small, sends, keeps = tied(small, sends, keeps)
        others = swap_all(sends, at_step(at))
        small = small + swap_seq(small, near[at - 1])
        if at == 1:
            d_normed = d_low.astype(F32) + d_other.astype(F32)
            d_input_norm, _ = norm_back(activations.astype(F32), gain_one, d_normed)
            grad_input = own_half(d_hidden + d_input_norm)
            grad_input, small, others = tied(grad_input, small, others)
        else:
            small, others = tied(small, others)
    conv_sum = jnp.concatenate(far_steps(list(zip(keeps, others)), far), 1)
    for distance in near[2:] + far:
        small = small + swap_seq(small, distance)
    small = small.reshape(-1)
    ends, at = [], 0
    for size in (beta_cols * features, features, features, tap_count * conv_cols, width):
        ends.append(small[at : at + size])
        at += size
    own_rows = lambda vector: lax.dynamic_slice_in_dim(
        vector, device_rank * shard_rows, shard_rows, vector.ndim - 1
    )
    tap_total = ends[3].reshape(tap_count, conv_cols)
    cut = lambda array, start, size: array[:, start : start + size]
    return (
        output,
        grad_input,
        cut(conv_sum, 0, query_cols),
        cut(conv_sum, query_cols, key_cols),
        cut(conv_sum, query_cols + key_cols, key_cols),
        own_rows(ends[0].reshape(beta_cols, features)).T,
        feed_sums[4],
        feed_sums[3].T,
        cut(tap_total, 0, query_cols),
        cut(tap_total, query_cols, key_cols),
        cut(tap_total, query_cols + key_cols, key_cols),
        own_rows(ends[1]),
        ends[4],
        own_rows(ends[2]),
        feed_sums[0],
        feed_sums[1],
        feed_sums[2].T,
    )


def solution(mesh):
    in_specs = (
        P("seq", None),
        P("seq", "head"),
        P(),
        P("seq", "head"),
        P("seq", "head"),
        P("seq", "head"),
        P("seq", "head"),
        P("seq", "head"),
        P("head", "seq"),
        P(None, "head"),
        P(None, "head"),
        P(None, "head"),
        P("seq"),
        P(),
        P("seq"),
        P("seq", "head"),
        P("seq", "head"),
        P("head", "seq"),
        P("seq", None),
    )
    out_specs = (
        P("seq", "head"),
        P("seq", "head"),
        P("seq", "head"),
        P("seq", "head"),
        P("seq", "head"),
        P("seq", "head"),
        P("seq", "head"),
        P("head", "seq"),
        P(None, "head"),
        P(None, "head"),
        P(None, "head"),
        P("seq"),
        P(),
        P("seq"),
        P("seq", "head"),
        P("seq", "head"),
        P("head", "seq"),
    )
    return jax.shard_map(
        per_device, mesh=mesh, in_specs=in_specs, out_specs=out_specs, check_vma=False
    )
```
